32 devices in a mesh: gx: 8 (over z, x), gy: 4 (over y, core).
Axes of the slice: x: 2, y: 2, z: 4, core: 2. Of those that a mesh axis runs over, the one named last changes fastest.
Arguments:
- old_states: float32 [8192, 12, 512], P(('gx', 'gy')), may hold values from -6 to 6
- new_place: int32 [8192], P(('gx', 'gy')), may hold values from -1 to 4095, as said below
- vectors_x: float32 [10, 10], replicated, may hold values from -2 to 2
- vectors_s: float32 [10, 10], replicated, may hold values from -2 to 2
- vectors_w: float32 [16, 10, 10], replicated, may hold values from -2 to 2
- values_x: float32 [10], replicated, may hold values from 0.2 to 5
- values_s: float32 [10], replicated, may hold values from 0.2 to 5
- values_w: float32 [16, 10], replicated, may hold values from 0.2 to 5
Outputs:
- new_states: float32 [32, 8, 16, 12, 512], P('gx', 'gy')
- correction: float32 [256, 64, 128], P('gx', 'gy')
The draws below stay inside these ranges and needn't reach their ends.
Inputs may be any that keep to these rules, and one draw needn't show every extreme that they name: `new_place`: every element number appears in exactly one slot; the other slots hold -1. One device's slots send at most 8 elements to any one device, and some pairs reach 8; some devices have all 256 slots filled.
All inputs are finite; a program needn't handle non-finite values.
Results may differ from the reference program's by a relative error of at most 0.00007.
Values sent between devices are 32-bit elements; how exact they have to be, the bound alone decides.
No kernel may reach another device: no remote copies, remote signals or barrier semaphores. Data moves between devices by JAX's collectives and lax.ppermute only.
A program may use at most 128 MiB of HBM per device.

```python
import math
import jax
import jax.numpy as jnp
from jax import lax

NP = 8
EXT = 10
FIELDS = 12
BX = 4
BS = 2
EW = 16
E_DEV = 128
SLOTS = 256
NEX = 32
NES = 8
N_GX = 8
N_GY = 4


def shuffled(key_one, length):
    return jax.random.permutation(key_one, length)


def draw_new_place(key, part):
    devices = N_GX * N_GY
    heavy_n = devices // 4
    light_n = devices - heavy_n
    heavy_cap = 2 * E_DEV // devices
    light_cap = E_DEV // devices
    half_items = E_DEV // 2
    key_order = jax.random.fold_in(key, 11)
    key_local = jax.random.fold_in(key, 23)
    key_slots = jax.random.fold_in(key, 37)
    order = jax.random.permutation(key_order, devices).astype(jnp.int32)
    heavy_set = order[:heavy_n]
    light_set = order[heavy_n:]
    dest = jnp.arange(devices, dtype=jnp.int32)[:, None]
    item = jnp.arange(E_DEV, dtype=jnp.int32)[None, :]
    heavy_src = heavy_set[jnp.minimum(item, half_items - 1) // heavy_cap]
    light_pick = (dest + jnp.maximum(item - half_items, 0) // light_cap) % light_n
    light_src = light_set[light_pick]
    source = jnp.where(item < half_items, jnp.broadcast_to(heavy_src, (devices, E_DEV)), light_src)
    local_perm = jax.vmap(lambda one: shuffled(one, E_DEV))(jax.random.split(key_local, devices)).astype(jnp.int32)
    local_x = local_perm // (BS * EW)
    local_s = local_perm // EW % BS
    local_w = local_perm % EW
    dest_x = dest // N_GY
    dest_y = dest % N_GY
    global_id = ((dest_x * BX + local_x) * (BS * N_GY) + dest_y * BS + local_s) * EW + local_w
    source_flat = source.reshape(-1).astype(jnp.int32)
    global_flat = global_id.reshape(-1).astype(jnp.int32)
    item_total = devices * E_DEV
    sort_order = jnp.argsort(source_flat, stable=True)
    sorted_src = source_flat[sort_order]
    counts = jax.ops.segment_sum(jnp.ones((item_total,), jnp.int32), source_flat, devices)
    starts = jnp.cumsum(counts) - counts
    rank_sorted = jnp.arange(item_total, dtype=jnp.int32) - starts[sorted_src]
    bucket_rank = jnp.zeros((item_total,), jnp.int32).at[sort_order].set(rank_sorted)
    slot_perm = jax.vmap(lambda one: shuffled(one, SLOTS))(jax.random.split(key_slots, devices)).astype(jnp.int32)
    slot_of = slot_perm[source_flat, bucket_rank]
    placed = jnp.full((devices * SLOTS,), -1, jnp.int32).at[source_flat * SLOTS + slot_of].set(global_flat)
    return placed.astype(jnp.int32)


def steps_of(rng, shape, cuts, least, high):
    loudness = 1.0
    for position, shards_of in cuts:
        steps = jax.random.uniform(jax.random.fold_in(jax.random.fold_in(rng, 6), position), (shards_of,), jnp.float32, least / len(cuts), high / len(cuts))
        loudness = loudness * jnp.repeat(jnp.exp(steps), shape[position] // shards_of).reshape((-1,) + (1,) * (len(shape) - 1 - position))
    return loudness


def gaussian(key, shape, deviation, limit, shards=(), held_as=jnp.bfloat16):
    level = steps_of(key, shape, shards, -0.22, 0.18) if shards else 1.0
    values = jax.random.normal(key, shape, jnp.float32) * deviation * level
    return jnp.minimum(jnp.maximum(values, -limit), limit).astype(held_as)


def setup_inputs(seed: int = 0) -> dict:
    key_list = jax.random.split(jax.random.key(seed), 9)
    old_states = gaussian(key_list[0], (SLOTS * N_GX * N_GY, FIELDS, NP**3), 1.0, 6.0, ((0, 32),), jnp.float32)
    new_place = draw_new_place(jax.random.fold_in(key_list[8], 71), 0)
    vectors_x = gaussian(key_list[2], (EXT, EXT), EXT ** -0.5, 2.0, (), jnp.float32)
    vectors_s = gaussian(key_list[3], (EXT, EXT), EXT ** -0.5, 2.0, (), jnp.float32)
    vectors_w = gaussian(key_list[4], (EW, EXT, EXT), EXT ** -0.5, 2.0, (), jnp.float32)
    values_x = jnp.clip(jnp.exp(jax.random.uniform(key_list[5], (EXT,), jnp.float32, math.log(0.2), math.log(5.0))), 0.2, 5.0)
    values_s = jnp.clip(jnp.exp(jax.random.uniform(key_list[6], (EXT,), jnp.float32, math.log(0.2), math.log(5.0))), 0.2, 5.0)
    values_w = jnp.clip(jnp.exp(jax.random.uniform(key_list[7], (EW, EXT), jnp.float32, math.log(0.2), math.log(5.0))), 0.2, 5.0)
    return {"old_states": old_states, "new_place": new_place, "vectors_x": vectors_x, "vectors_s": vectors_s, "vectors_w": vectors_w, "values_x": values_x, "values_s": values_s, "values_w": values_w}


def windows(field, num_blocks, per_side):
    left_face = field[0:num_blocks * per_side:per_side]
    right_face = field[per_side + 1::per_side]
    core_cells = field[1:num_blocks * per_side + 1].reshape((num_blocks, per_side) + field.shape[1:])
    return jnp.concatenate([left_face[:, None], core_cells, right_face[:, None]], axis=1)


def unwindows(windowed, num_blocks, per_side):
    trailing = windowed.shape[2:]
    core_cells = windowed[:, 1:per_side + 1].reshape((num_blocks * per_side,) + trailing)
    result = jnp.zeros((num_blocks * per_side + 2,) + trailing, jnp.float32)
    result = result.at[1:num_blocks * per_side + 1].set(core_cells)
    result = result.at[0:num_blocks * per_side:per_side].add(windowed[:, 0])
    result = result.at[per_side + 1::per_side].add(windowed[:, per_side + 1])
    return result


def extend(padded, blocks, per_side):
    result = padded
    for which in range(3):
        turned = jnp.moveaxis(result, 2 * which, 0)
        turned = windows(turned, blocks[which], per_side)
        result = jnp.moveaxis(turned, (0, 1), (2 * which, 2 * which + 1))
    extent = per_side + 2
    result = jnp.transpose(result, (1, 3, 5, 0, 2, 4))
    return result.reshape(extent, extent, extent, blocks[0] * blocks[1] * blocks[2])


def retract(boxes, blocks, per_side):
    extent = per_side + 2
    result = boxes.reshape(extent, extent, extent, blocks[0], blocks[1], blocks[2])
    result = jnp.transpose(result, (3, 0, 4, 1, 5, 2))
    for which in (2, 1, 0):
        turned = jnp.moveaxis(result, (2 * which, 2 * which + 1), (0, 1))
        turned = unwindows(turned, blocks[which], per_side)
        result = jnp.moveaxis(turned, 0, 2 * which)
    return result


def rim_mask(extent):
    offset = jnp.arange(extent)
    on_rim = ((offset == 0) | (offset == extent - 1)).astype(jnp.int32)
    rim_count = on_rim[:, None, None] + on_rim[None, :, None] + on_rim[None, None, :]
    return (rim_count <= 1).astype(jnp.float32)[..., None]


def diag_solve(extended, vectors_x, vectors_s, stacked_w, values_x, values_s, stacked_values):
    highest = lax.Precision.HIGHEST
    section = jnp.einsum('ui,uvwn->ivwn', vectors_x, extended, precision=highest)
    section = jnp.einsum('vj,ivwn->ijwn', vectors_s, section, precision=highest)
    section = jnp.einsum('wkn,ijwn->ijkn', stacked_w, section, precision=highest)
    denom = values_x[:, None, None, None] + values_s[None, :, None, None] + stacked_values[None, None, :, :]
    modal = section / denom
    section = jnp.einsum('ui,ijkn->ujkn', vectors_x, modal, precision=highest)
    section = jnp.einsum('vj,ujkn->uvkn', vectors_s, section, precision=highest)
    return jnp.einsum('wkn,uvkn->uvwn', stacked_w, section, precision=highest)


def reference(old_states, new_place, vectors_x, vectors_s, vectors_w, values_x, values_s, values_w):
    element_total = NEX * NES * EW
    target_row = jnp.where(new_place < 0, element_total, new_place).astype(jnp.int32)
    new_flat = jnp.zeros((element_total, FIELDS, NP ** 3), jnp.float32).at[target_row].set(old_states, mode='drop')
    new_states = new_flat.reshape(NEX, NES, EW, FIELDS, NP ** 3)
    pressure = 3.0 * new_flat[:, 0] - 3.0 * new_flat[:, 1] + new_flat[:, 2]
    cell_field = pressure.reshape(NEX, NES, EW, NP, NP, NP).transpose(0, 3, 1, 4, 2, 5).reshape(NEX * NP, NES * NP, EW * NP)
    padded = jnp.pad(cell_field, ((1, 1), (1, 1), (0, 0)), mode='wrap')
    padded = jnp.pad(padded, ((0, 0), (0, 0), (1, 1)))
    blocks = (NEX, NES, EW)
    box_mask = rim_mask(NP + 2)
    extended = extend(padded, blocks, NP) * box_mask
    repeat = NEX * NES
    stacked_w = jnp.transpose(jnp.tile(vectors_w, (repeat, 1, 1)), (1, 2, 0))
    stacked_values = jnp.tile(values_w, (repeat, 1)).T
    local_fix = diag_solve(extended, vectors_x, vectors_s, stacked_w, values_x, values_s, stacked_values) * box_mask
    returned = retract(local_fix, blocks, NP)
    returned = returned.at[1].add(returned[-1]).at[-2].add(returned[0])
    returned = returned.at[:, 1].add(returned[:, -1]).at[:, -2].add(returned[:, 0])
    correction = returned[1:-1, 1:-1, 1:-1]
    return new_states, correction
```

```python
import functools

import jax
import jax.numpy as jnp
import numpy as np
from jax import lax
from jax.experimental import pallas as pl
from jax.experimental.pallas import tpu as pltpu
from jax.sharding import PartitionSpec as P

BX = 4
BS = 2
FACE = 8
VMEM_LIMIT = 40 * 1024 * 1024
PARAMS = pltpu.CompilerParams(vmem_limit_bytes=VMEM_LIMIT)
HIGHEST = lax.Precision.HIGHEST
F32 = jnp.float32
BF16 = jnp.bfloat16


class Plan:
    def __init__(self, n_x, n_y, slots, fields, points, layers, extent):
        self.n_x, self.n_y = n_x, n_y
        self.devices = n_x * n_y
        self.lines = n_x // 2
        self.plane = self.devices // self.lines
        self.slots, self.fields, self.points = slots, fields, points
        self.layers, self.extent, self.side = layers, extent, extent - 2
        self.per_dev = BX * BS * layers
        self.cap = 2 * self.per_dev // self.devices
        self.msg_rows = self.lines * self.cap
        self.rows = self.plane * self.msg_rows
        full = self.plane * self.cap
        self.kept = [full] * self.lines
        self.offset = [sum(self.kept[:m]) for m in range(self.lines)]
        self.relay_rows = sum(self.kept) - full
        self.groups = [(0, 3), (3, 4), (7, 5)]


def halves(value, count):
    if count & (count - 1) == 0:
        return lax.shift_right_logical(value, int(count).bit_length() - 1)
    return value // count


def rest(value, count):
    if count & (count - 1) == 0:
        return value & (count - 1)
    return value % count


def three_terms(value):
    high = value.astype(BF16)
    left = value - high.astype(F32)
    middle = left.astype(BF16)
    low = (left - middle.astype(F32)).astype(BF16)
    return high, middle, low


def pick(chooser, value, contract=((1,), (0,))):
    high, middle, low = three_terms(value)
    dims = (contract, ((), ()))
    product = functools.partial(lax.dot_general, dimension_numbers=dims, preferred_element_type=F32)
    return (product(chooser, high) + product(chooser, middle)) + product(chooser, low)


def iota(shape, dim):
    return lax.broadcasted_iota(jnp.int32, shape, dim)


def before(count):
    return (iota((count, count), 0) < iota((count, count), 1)).astype(BF16)


def pack_kernel(plan, fields, marked, me_ref, place_ref, states_ref, *refs):
    outs, chooser_ref = refs[: plan.plane], refs[plan.plane]
    field = pl.program_id(0)
    rows = plan.msg_rows

    @pl.when(field == 0)
    def _():
        me = me_ref[0]
        new_place = place_ref[...]
        live = new_place >= 0
        placed = jnp.maximum(new_place, 0)
        column = halves(placed, plan.layers)
        layer_pos = rest(placed, plan.layers)
        span = BS * plan.n_y
        elem_x = halves(column, span)
        elem_s = rest(column, span)
        target = halves(elem_x, BX) * plan.n_y + halves(elem_s, BS)
        local_row = (rest(elem_x, BX) * BS + rest(elem_s, BS)) * plan.layers + layer_pos
        target = jnp.where(live, target, -1)
        hot = iota((plan.devices, plan.slots), 0) == target
        earlier = jnp.dot(hot.astype(BF16), before(plan.slots), preferred_element_type=F32)
        rank = jnp.sum(jnp.where(hot, earlier, 0.0), axis=0, keepdims=True).astype(jnp.int32)
        across = target ^ me
        row = rest(across, plan.plane) * rows + halves(across, plan.plane) * plan.cap + rank
        row = jnp.where(live, row, -1)
        chooser = (iota((plan.rows, plan.slots), 0) == row).astype(F32)
        chooser_ref[...] = chooser.astype(BF16)
        if marked:
            marks = lax.dot_general(
                jnp.broadcast_to((local_row + 1).astype(F32), (8, plan.slots)),
                chooser,
                (((1,), (1,)), ((), ())),
                precision=HIGHEST,
                preferred_element_type=F32,
            )
            for out in outs:
                out[fields * rows : fields * rows + 8, :] = jnp.zeros((8, plan.points), F32)
                out[fields * rows : fields * rows + 8, : plan.rows] = marks

    moved = pick(chooser_ref[...], states_ref[0])
    start = pl.multiple_of(field * rows, rows)
    for j, out in enumerate(outs):
        out[pl.ds(start, rows), :] = moved[j * rows : (j + 1) * rows]


def whole(shape):
    return pl.BlockSpec(shape, lambda *_: (0,) * len(shape))


def pack(plan, group, me, place_row, states, marked):
    first, fields = group
    shape = (fields * plan.msg_rows + (8 if marked else 0), plan.points)
    return pl.pallas_call(
        functools.partial(pack_kernel, plan, fields, marked),
        grid=(fields,),
        in_specs=[
            pl.BlockSpec(memory_space=pltpu.SMEM),
            whole((1, plan.slots)),
            pl.BlockSpec((1, plan.slots, plan.points), lambda f: (first + f, 0, 0)),
        ],
        out_specs=[whole(shape)] * plan.plane,
        out_shape=[jax.ShapeDtypeStruct(shape, F32)] * plan.plane,
        scratch_shapes=[pltpu.VMEM((plan.rows, plan.slots), BF16)],
        compiler_params=PARAMS,
    )(me, place_row, states)


def route_rows(plan, marks):
    lane = iota((1, plan.rows), 1)
    step = rest(halves(lane, plan.cap), plan.lines)
    filled = marks[:1] > 0.0
    valid = (iota((plan.lines, plan.rows), 0) == step) & filled
    earlier = jnp.dot(valid.astype(BF16), before(plan.rows), preferred_element_type=F32)
    earlier = earlier.astype(jnp.int32)
    row = halves(lane, plan.msg_rows) * plan.cap + rest(lane, plan.cap)
    for m in range(1, plan.lines):
        place = jnp.where(earlier[m : m + 1] < plan.kept[m], earlier[m : m + 1] + plan.offset[m], -1)
        row = jnp.where(step == m, place, row)
    return jnp.where(filled, row, -1)


def gather_marks(plan, fields, messages):
    lane = iota((8, plan.rows), 1)
    marks = jnp.zeros((8, plan.rows), F32)
    base = fields * plan.msg_rows
    for j, message in enumerate(messages):
        part = message[base : base + 8, : plan.rows]
        marks = jnp.where(halves(lane, plan.msg_rows) == j, part, marks)
    return marks


def relay_kernel(plan, fields, marked, *refs):
    messages = refs[: plan.plane]
    refs = refs[plan.plane :]
    if not marked:
        marks_ref, refs = refs[0], refs[1:]
    outs, refs = refs[: plan.lines - 1], refs[plan.lines - 1 :]
    if marked:
        marks = gather_marks(plan, fields, messages)
        marks_out, own_out = refs[:2]
        refs = refs[2:]
        marks_out[...] = marks
    else:
        marks = marks_ref[...]
    (held,) = refs
    row = route_rows(plan, marks)
    spread = (iota((plan.rows, plan.rows), 0) == row).astype(F32)
    if marked:
        landed = lax.dot_general(
            marks, spread, (((1,), (1,)), ((), ())), precision=HIGHEST, preferred_element_type=F32
        )
        own_out[...] = landed
        for m, out in enumerate(outs, 1):
            base = fields * plan.kept[m]
            out[base : base + 8, :] = jnp.zeros((8, plan.points), F32)
            out[base : base + 8, : plan.rows] = landed
    first = plan.offset[1]
    chooser = spread[first : first + plan.relay_rows].astype(BF16)
    for field in range(fields):
        for j, message in enumerate(messages):
            held[j * plan.msg_rows : (j + 1) * plan.msg_rows, :] = message[
                field * plan.msg_rows : (field + 1) * plan.msg_rows, :
            ]
        moved = pick(chooser, held[...])
        for m, out in enumerate(outs, 1):
            at = plan.offset[m] - first
            out[field * plan.kept[m] : (field + 1) * plan.kept[m], :] = moved[at : at + plan.kept[m]]


def relay(plan, group, messages, marks):
    _, fields = group
    marked = marks is None
    extra = 8 if marked else 0
    out_shape = [
        jax.ShapeDtypeStruct((fields * plan.kept[m] + extra, plan.points), F32) for m in range(1, plan.lines)
    ]
    if marked:
        out_shape += [jax.ShapeDtypeStruct((8, plan.rows), F32)] * 2
    operands = list(messages) + ([] if marked else [marks])
    result = pl.pallas_call(
        functools.partial(relay_kernel, plan, fields, marked),
        in_specs=[pl.BlockSpec(memory_space=pltpu.VMEM)] * len(operands),
        out_specs=[pl.BlockSpec(memory_space=pltpu.VMEM)] * len(out_shape),
        out_shape=out_shape,
        scratch_shapes=[pltpu.VMEM((plan.rows, plan.points), F32)],
        compiler_params=PARAMS,
    )(*operands)
    return result[: plan.lines - 1], result[plan.lines - 1 :]


def settle_kernel(plan, fields, marked, *refs):
    messages, refs = refs[: plan.plane], refs[plan.plane :]
    relays, refs = refs[: plan.lines - 1], refs[plan.lines - 1 :]
    if marked:
        own_ref, order_ref = refs[:2]
        out, marks_out, cells_out = refs[2:5]
        refs = refs[5:]
    else:
        marks_ref = refs[0]
        out = refs[2]
        refs = refs[3:]
    chooser_ref, held = refs[:2]
    field = pl.program_id(0)
    full = plan.kept[0]

    @pl.when(field == 0)
    def _():
        if marked:
            lane = iota((8, plan.rows), 1)
            marks = jnp.where(lane < full, own_ref[...], 0.0)
            for m in range(1, plan.lines):
                base = fields * plan.kept[m]
                part = relays[m - 1][base : base + 8, : plan.rows]
                inside = (lane >= plan.offset[m]) & (lane < plan.offset[m] + plan.kept[m])
                marks = jnp.where(inside, part, marks)
            marks_out[...] = marks
        else:
            marks = marks_ref[...]
        element = iota((plan.per_dev, plan.rows), 0).astype(F32) + 1.0
        chooser_ref[...] = (element == marks[:1]).astype(F32).astype(BF16)
        used = plan.offset[-1] + plan.kept[-1]
        if used < plan.rows:
            held[used:, :] = jnp.zeros((plan.rows - used, plan.points), F32)

    start = field * plan.msg_rows
    for j, message in enumerate(messages):
        held[j * plan.cap : (j + 1) * plan.cap, :] = message[pl.ds(start, plan.msg_rows), :][: plan.cap]
    for m, part in enumerate(relays, 1):
        kept = plan.kept[m]
        held[plan.offset[m] : plan.offset[m] + kept, :] = part[pl.ds(pl.multiple_of(field * kept, 8), kept), :]
    placed = pick(chooser_ref[...], held[...])
    out[...] = placed.reshape(out.shape)

    if marked:
        pressure_ref = refs[2]

        @pl.when(field == 0)
        def _():
            pressure_ref[...] = 3.0 * placed

        @pl.when(field == 1)
        def _():
            pressure_ref[...] = pressure_ref[...] - 3.0 * placed

        @pl.when(field == 2)
        def _():
            cells_out[...] = pick(order_ref[...], pressure_ref[...] + placed, ((1,), (1,)))


def cell_order(side):
    rows = []
    for k in range(side):
        rows += [(i * side + j) * side + k for i in range(side) for j in range(side)]
        rows += [(i * side + side - 1) * side + k for i in range(side)]
        rows += [(i * side) * side + k for i in range(side)]
    order = np.zeros((len(rows), side**3), np.float32)
    order[np.arange(len(rows)), rows] = 1.0
    return order


def settle(plan, group, messages, relays, marks, buffer, own, order):
    first, fields = group
    marked = marks is None
    columns = BX * BS
    states_shape = (columns, plan.fields, plan.layers, plan.points)
    out_specs = [pl.BlockSpec((columns, 1, plan.layers, plan.points), lambda f: (0, first + f, 0, 0))]
    out_shape = [jax.ShapeDtypeStruct(states_shape, F32)]
    scratch = [pltpu.VMEM((plan.per_dev, plan.rows), BF16), pltpu.VMEM((plan.rows, plan.points), F32)]
    operands = list(messages) + list(relays)
    aliases = {}
    if marked:
        operands += [own, order]
        cells = (order.shape[0], plan.per_dev)
        out_specs += [whole((8, plan.rows)), whole(cells)]
        out_shape += [jax.ShapeDtypeStruct((8, plan.rows), F32), jax.ShapeDtypeStruct(cells, F32)]
        scratch += [pltpu.VMEM((plan.per_dev, plan.points), F32)]
        in_specs = [whole(o.shape) for o in operands]
    else:
        operands += [marks, buffer]
        in_specs = [whole(o.shape) for o in operands[:-1]] + [pl.BlockSpec(memory_space=pl.ANY)]
        aliases = {len(operands) - 1: 0}
    return pl.pallas_call(
        functools.partial(settle_kernel, plan, fields, marked),
        grid=(fields,),
        in_specs=in_specs,
        out_specs=out_specs,
        out_shape=out_shape,
        scratch_shapes=scratch,
        input_output_aliases=aliases,
        compiler_params=PARAMS,
    )(*operands)


def lane_steps(plan):
    lane = iota((FACE, plan.per_dev), 1)
    layer = rest(lane, plan.layers)
    row_s = rest(halves(lane, plan.layers), BS)
    row_x = halves(lane, plan.layers * BS)
    return layer, row_s, row_x


def roll(value, steps):
    return pltpu.roll(value, steps % value.shape[1], 1)


def solve_kernel(plan, cells, from_xlow, from_xup, from_slow, from_sup, mix, mix_t, weights, sum_xs, values_w, *refs):
    total, out_xlow, out_xup, out_slow, out_sup, box, section, modal = refs
    side, extent = plan.side, plan.extent
    layer, row_s, row_x = lane_steps(plan)
    points = side * side
    stride = points + 2 * FACE
    width = plan.layers
    wide = width * BS
    box_rows = points + 4 * FACE

    def cell(k, start):
        return cells[k * stride + start : k * stride + start + FACE, :]

    def piece(ref, k):
        return ref[k * FACE : (k + 1) * FACE, :]

    for k in range(side):
        w = k + 1
        for i in range(side):
            box[w * box_rows + i * FACE : w * box_rows + (i + 1) * FACE, :] = cell(k, i * FACE)
        at = w * box_rows + points
        low = jnp.where(row_x == 0, roll(piece(from_xlow, k), wide), roll(cell(k, points - FACE), wide))
        up = jnp.where(row_x == BX - 1, roll(piece(from_xup, k), -wide), roll(cell(k, 0), -wide))
        box[at : at + FACE, :] = low
        box[at + FACE : at + 2 * FACE, :] = up
        top, bottom = cell(k, points), cell(k, points + FACE)
        back = (BS - 1) * width
        low = jnp.where(row_s == 0, roll(piece(from_slow, k), -back), roll(top, width))
        up = jnp.where(row_s == BS - 1, roll(piece(from_sup, k), back), roll(bottom, -width))
        box[at + 2 * FACE : at + 3 * FACE, :] = low
        box[at + 3 * FACE : at + 4 * FACE, :] = up
    last = (extent - 1) * box_rows
    for i in range(side):
        below = jnp.where(layer == 0, 0.0, roll(cell(side - 1, i * FACE), 1))
        above = jnp.where(layer == width - 1, 0.0, roll(cell(0, i * FACE), -1))
        box[i * FACE : (i + 1) * FACE, :] = below
        box[last + i * FACE : last + (i + 1) * FACE, :] = above

    modal_rows = mix.shape[0]
    lanes = plan.per_dev
    for w in range(extent):
        rows = points if w in (0, extent - 1) else box_rows
        section[w] = jnp.dot(
            mix[:, :rows], box[w * box_rows : w * box_rows + rows, :], precision=HIGHEST, preferred_element_type=F32
        )
    for block in range(0, modal_rows, FACE):
        held = [section[w, block : block + FACE, :] for w in range(extent)]
        out = [None] * extent
        base = jnp.broadcast_to(sum_xs[block : block + FACE, :], (FACE, lanes))
        for k in range(extent):
            value = None
            for w in range(extent):
                term = weights[w, k : k + 1, :] * held[w]
                value = term if value is None else value + term
            value = value / (base + values_w[k : k + 1, :])
            for w in range(extent):
                term = weights[w, k : k + 1, :] * value
                out[w] = term if out[w] is None else out[w] + term
        for w in range(extent):
            modal[w, block : block + FACE, :] = out[w]
    for w in range(extent):
        rows = points if w in (0, extent - 1) else box_rows
        box[w * box_rows : w * box_rows + rows, :] = jnp.dot(
            mix_t[:rows, :], modal[w], precision=HIGHEST, preferred_element_type=F32
        )

    for k in range(side):
        at = (k + 1) * box_rows
        total[k * points : (k + 1) * points, :] = box[at : at + points, :]
        for out, shift in ((out_xlow, 0), (out_xup, 1), (out_slow, 2), (out_sup, 3)):
            start = at + points + shift * FACE
            out[k * FACE : (k + 1) * FACE, :] = box[start : start + FACE, :]
    for i in range(side):
        below = jnp.where(layer == width - 1, 0.0, roll(box[i * FACE : (i + 1) * FACE, :], -1))
        above = jnp.where(layer == 0, 0.0, roll(box[last + i * FACE : last + (i + 1) * FACE, :], 1))
        top = (side - 1) * points + i * FACE
        total[top : top + FACE, :] += below
        total[i * FACE : (i + 1) * FACE, :] += above


def finish_kernel(plan, total, xlow, xup, slow, sup, from_x_up, from_x_low, from_s_up, from_s_low, out, held):
    side = plan.side
    points = side * side
    layer, row_s, row_x = lane_steps(plan)
    width = plan.layers
    wide = width * BS
    back = (BS - 1) * width
    sub = iota((FACE, plan.per_dev), 0)
    for k in range(side):
        part = slice(k * FACE, (k + 1) * FACE)
        rows = [total[k * points + i * FACE : k * points + (i + 1) * FACE, :] for i in range(side)]
        rows[side - 1] = rows[side - 1] + jnp.where(
            row_x == BX - 1, roll(from_x_up[part, :], -wide), roll(xlow[part, :], -wide)
        )
        rows[0] = rows[0] + jnp.where(row_x == 0, roll(from_x_low[part, :], wide), roll(xup[part, :], wide))
        to_last = jnp.where(row_s == BS - 1, roll(from_s_up[part, :], back), roll(slow[part, :], -width))
        to_first = jnp.where(row_s == 0, roll(from_s_low[part, :], -back), roll(sup[part, :], width))
        for i in range(side):
            last = jnp.broadcast_to(to_last[i : i + 1, :], sub.shape)
            first = jnp.broadcast_to(to_first[i : i + 1, :], sub.shape)
            value = rows[i] + jnp.where(sub == side - 1, last, 0.0) + jnp.where(sub == 0, first, 0.0)
            held[k * points + i * FACE : k * points + (i + 1) * FACE, :] = value
    lanes = plan.layers * side
    source = iota((plan.per_dev, lanes), 0)
    lane = iota((plan.per_dev, lanes), 1)
    terms = three_terms(held[...])
    kept = rest(iota((points, lanes), 1), side)
    for column in range(BX * BS):
        chooser = (source == halves(lane, side) + column * plan.layers).astype(F32).astype(BF16)
        high, middle, low = [jnp.dot(t, chooser, preferred_element_type=F32) for t in terms]
        spread = (high + middle) + low
        value = jnp.zeros((points, lanes), F32)
        for k in range(side):
            value = jnp.where(kept == k, spread[k * points : (k + 1) * points], value)
        b, s = column // BS, column % BS
        for i in range(side):
            out[b * side + i, s * side : (s + 1) * side, :] = value[i * side : (i + 1) * side]


def simple_call(kernel, operands, out_shape, scratch):
    return pl.pallas_call(
        kernel,
        in_specs=[pl.BlockSpec(memory_space=pltpu.VMEM)] * len(operands),
        out_specs=[pl.BlockSpec(memory_space=pltpu.VMEM)] * len(out_shape),
        out_shape=out_shape,
        scratch_shapes=scratch,
        compiler_params=PARAMS,
    )(*operands)


def box_tables(plan, vectors_x, vectors_s, vectors_w, values_x, values_s, values_w):
    extent = plan.extent
    rim = [0, extent - 1]
    inside = slice(1, extent - 1)

    def kron(left, right):
        return (left[:, None, :, None] * right[None, :, None, :]).reshape(
            left.shape[0] * right.shape[0], extent * extent
        )

    ends_x = jnp.stack([vectors_x[r] for r in rim])
    ends_s = jnp.stack([vectors_s[r] for r in rim])
    mix_t = jnp.concatenate(
        [
            kron(vectors_x[inside], vectors_s[inside]),
            kron(ends_x, vectors_s[inside]),
            kron(ends_s, vectors_x[inside]).reshape(-1, extent, extent).swapaxes(1, 2).reshape(-1, extent * extent),
        ]
    )
    modal_rows = -(-extent * extent // FACE) * FACE
    more = modal_rows - extent * extent
    mix_t = jnp.pad(mix_t, ((0, 0), (0, more)))
    sum_xs = (values_x[:, None] + values_s[None, :]).reshape(-1, 1)
    sum_xs = jnp.pad(sum_xs, ((0, more), (0, 0)), constant_values=1.0)
    columns = BX * BS
    weights = jnp.tile(jnp.transpose(vectors_w, (1, 2, 0)), (1, 1, columns))
    lane_values = jnp.tile(values_w.T, (1, columns))
    return mix_t.T, mix_t, weights, sum_xs, lane_values


def shards(old_states, new_place, vectors_x, vectors_s, vectors_w, values_x, values_s, values_w):
    n_x, n_y = lax.axis_size("gx"), lax.axis_size("gy")
    slots, fields, points = old_states.shape
    plan = Plan(n_x, n_y, slots, fields, points, vectors_w.shape[0], vectors_x.shape[0])
    place = lax.axis_index("gx") * n_y + lax.axis_index("gy")
    me = place.astype(jnp.int32).reshape(1)
    states = jnp.transpose(old_states, (1, 0, 2))
    place_row = new_place.reshape(1, slots)
    both = ("gx", "gy")

    def across(value, flip):
        return lax.ppermute(value, both, [(d, d ^ flip) for d in range(plan.devices)])

    def shifted(value, axis, steps):
        count = lax.axis_size(axis)
        return lax.ppermute(value, axis, [(s, (s + steps) % count) for s in range(count)])

    order = jnp.asarray(cell_order(plan.side), BF16)
    tables = box_tables(plan, vectors_x, vectors_s, vectors_w, values_x, values_s, values_w)

    packed = [pack(plan, group, me, place_row, states, g == 0) for g, group in enumerate(plan.groups)]
    marks = None
    held = []
    for group, sent in zip(plan.groups, packed):
        messages = [sent[0]] + [across(sent[j], j) for j in range(1, plan.plane)]
        relays, more = relay(plan, group, messages, marks)
        if marks is None:
            marks, own = more
        arrived = [across(relays[m - 1], m * plan.plane) for m in range(1, plan.lines)]
        held.append((messages, arrived))

    buffer, row_marks, cells = settle(plan, plan.groups[0], *held[0], None, None, own, order)
    side = plan.side
    face = jax.ShapeDtypeStruct((side * FACE, plan.per_dev), F32)
    layered = cells.reshape(side, side * side + 2 * FACE, plan.per_dev)

    def rows(start):
        return layered[:, start : start + FACE].reshape(side * FACE, plan.per_dev)

    inner = side * side
    halo = [
        shifted(rows(inner - FACE), "gx", 1),
        shifted(rows(0), "gx", -1),
        shifted(rows(inner), "gy", 1),
        shifted(rows(inner + FACE), "gy", -1),
    ]
    modal_rows = tables[0].shape[0]
    total, xlow, xup, slow, sup = simple_call(
        functools.partial(solve_kernel, plan),
        [cells, *halo, *tables],
        [jax.ShapeDtypeStruct((side * inner, plan.per_dev), F32)] + [face] * 4,
        [pltpu.VMEM((plan.extent * (inner + 4 * FACE), plan.per_dev), F32)]
        + [pltpu.VMEM((plan.extent, modal_rows, plan.per_dev), F32)] * 2,
    )
    returned = [shifted(xlow, "gx", -1), shifted(xup, "gx", 1), shifted(slow, "gy", -1), shifted(sup, "gy", 1)]
    (correction,) = simple_call(
        functools.partial(finish_kernel, plan),
        [total, xlow, xup, slow, sup, *returned],
        [jax.ShapeDtypeStruct((BX * side, BS * side, plan.layers * side), F32)],
        [pltpu.VMEM((side * inner, plan.per_dev), F32)],
    )
    for group, (messages, arrived) in zip(plan.groups[1:], held[1:]):
        (buffer,) = settle(plan, group, messages, arrived, row_marks, buffer, None, None)
    new_states = buffer.reshape(BX, BS, fields, plan.layers, points).transpose(0, 1, 3, 2, 4)
    return new_states, correction


def solution(mesh):
    placed = (P(("gx", "gy"), None, None), P(("gx", "gy")), P(), P(), P(), P(), P(), P())
    return jax.shard_map(
        shards,
        mesh=mesh,
        in_specs=placed,
        out_specs=(P("gx", "gy", None, None, None), P("gx", "gy", None)),
        check_vma=False,
    )
```

```python
import functools

import jax
import jax.numpy as jnp
import numpy as np
from jax import lax
from jax.experimental import pallas as pl
from jax.experimental.pallas import tpu as pltpu
from jax.sharding import PartitionSpec as P

BX = 4
BS = 2
FACE = 8
MERGE_FLOPS = 40_000_000_000
VMEM_LIMIT = 12 * 1024 * 1024
PARAMS = pltpu.CompilerParams(vmem_limit_bytes=VMEM_LIMIT)
HIGHEST = lax.Precision.HIGHEST
F32 = jnp.float32
BF16 = jnp.bfloat16


class Plan:
    def __init__(self, n_x, n_y, slots, fields, points, layers, extent):
        self.n_x, self.n_y = n_x, n_y
        self.devices = n_x * n_y
        self.lines = n_x // 2
        self.plane = self.devices // self.lines
        self.slots, self.fields, self.points = slots, fields, points
        self.layers, self.extent, self.side = layers, extent, extent - 2
        self.per_dev = BX * BS * layers
        self.cap = 2 * self.per_dev // self.devices
        self.msg_rows = self.lines * self.cap
        self.pairs = self.plane // 2
        self.pair_rows = 2 * self.msg_rows
        self.rows = self.plane * self.msg_rows
        full = self.plane * self.cap
        self.kept = [full] * self.lines
        self.offset = [sum(self.kept[:m]) for m in range(self.lines)]
        self.relay_rows = sum(self.kept) - full
        self.groups = [(0, 3), (3, 4), (7, 5)]


def halves(value, count):
    if count & (count - 1) == 0:
        return lax.shift_right_logical(value, int(count).bit_length() - 1)
    return value // count


def rest(value, count):
    if count & (count - 1) == 0:
        return value & (count - 1)
    return value % count


def three_terms(value):
    high = value.astype(BF16)
    left = value - high.astype(F32)
    middle = left.astype(BF16)
    low = (left - middle.astype(F32)).astype(BF16)
    return high, middle, low


def pick(chooser, value, contract=((1,), (0,))):
    high, middle, low = three_terms(value)
    dims = (contract, ((), ()))
    product = functools.partial(lax.dot_general, dimension_numbers=dims, preferred_element_type=F32)
    return (product(chooser, high) + product(chooser, middle)) + product(chooser, low)


def iota(shape, dim):
    return lax.broadcasted_iota(jnp.int32, shape, dim)


def before(count):
    return (iota((count, count), 0) < iota((count, count), 1)).astype(BF16)


def pack_kernel(plan, fields, marked, me_ref, place_ref, states_ref, *refs):
    outs, chooser_ref = refs[:-1], refs[-1]
    field = pl.program_id(0)
    rows = plan.msg_rows

    @pl.when(field == 0)
    def _():
        me = me_ref[0]
        new_place = place_ref[...]
        live = new_place >= 0
        placed = jnp.maximum(new_place, 0)
        column = halves(placed, plan.layers)
        layer_pos = rest(placed, plan.layers)
        span = BS * plan.n_y
        elem_x = halves(column, span)
        elem_s = rest(column, span)
        target = halves(elem_x, BX) * plan.n_y + halves(elem_s, BS)
        local_row = (rest(elem_x, BX) * BS + rest(elem_s, BS)) * plan.layers + layer_pos
        target = jnp.where(live, target, -1)
        hot = iota((plan.devices, plan.slots), 0) == target
        earlier = jnp.dot(hot.astype(BF16), before(plan.slots), preferred_element_type=F32)
        rank = jnp.sum(jnp.where(hot, earlier, 0.0), axis=0, keepdims=True).astype(jnp.int32)
        across = target ^ me
        row = rest(across, plan.plane) * rows + halves(across, plan.plane) * plan.cap + rank
        row = jnp.where(live, row, -1)
        chooser = (iota((plan.rows, plan.slots), 0) == row).astype(F32)
        chooser_ref[...] = chooser.astype(BF16)
        if marked:
            marks = lax.dot_general(
                jnp.broadcast_to((local_row + 1).astype(F32), (8, plan.slots)),
                chooser,
                (((1,), (1,)), ((), ())),
                precision=HIGHEST,
                preferred_element_type=F32,
            )
            for out, held in zip(outs, [rows] * (len(outs) - 1) + [rows * plan.pairs]):
                out[fields * held : fields * held + 8, :] = jnp.zeros((8, plan.points), F32)
                out[fields * held : fields * held + 8, : plan.rows] = marks

    moved = pick(chooser_ref[...], states_ref[0])
    start = pl.multiple_of(field * rows, rows)
    aside = pl.multiple_of(field * rows * plan.pairs, rows)
    for b in range(plan.pairs):
        outs[b][pl.ds(start, rows), :] = moved[2 * b * rows : (2 * b + 1) * rows]
        outs[-1][pl.ds(aside + b * rows, rows), :] = moved[(2 * b + 1) * rows : (2 * b + 2) * rows]


def whole(shape):
    return pl.BlockSpec(shape, lambda *_: (0,) * len(shape))


def pack(plan, group, me, place_row, states, marked):
    first, fields = group
    extra = 8 if marked else 0
    shapes = [(fields * plan.msg_rows + extra, plan.points)] * plan.pairs
    shapes.append((fields * plan.msg_rows * plan.pairs + extra, plan.points))
    return pl.pallas_call(
        functools.partial(pack_kernel, plan, fields, marked),
        grid=(fields,),
        in_specs=[
            pl.BlockSpec(memory_space=pltpu.SMEM),
            whole((1, plan.slots)),
            pl.BlockSpec((1, plan.slots, plan.points), lambda f: (first + f, 0, 0)),
        ],
        out_specs=[pl.BlockSpec(memory_space=pltpu.VMEM)] * len(shapes),
        out_shape=[jax.ShapeDtypeStruct(shape, F32) for shape in shapes],
        scratch_shapes=[pltpu.VMEM((plan.rows, plan.slots), BF16)],
        compiler_params=PARAMS,
    )(me, place_row, states)


def merge_kernel(plan, fields, marked, *refs):
    near, refs = refs[: plan.pairs], refs[plan.pairs :]
    aside, outs = refs[0], refs[1:]
    rows = plan.msg_rows
    for b, out in enumerate(outs):
        for field in range(fields):
            start = field * plan.pair_rows
            other = (field * plan.pairs + b) * rows
            out[start : start + rows, :] = near[b][field * rows : (field + 1) * rows, :]
            out[start + rows : start + 2 * rows, :] = aside[other : other + rows, :]
        if marked:
            lane = iota((8, plan.rows), 1)
            mine = near[0][fields * rows : fields * rows + 8, : plan.rows]
            base = fields * rows * plan.pairs
            other = aside[base : base + 8, : plan.rows]
            marks = jnp.where(rest(halves(lane, rows), 2) == 0, mine, other)
            base = fields * plan.pair_rows
            out[base : base + 8, :] = jnp.zeros((8, plan.points), F32)
            out[base : base + 8, : plan.rows] = marks


def merge(plan, group, near, aside, marked, cost):
    _, fields = group
    shape = (fields * plan.pair_rows + (8 if marked else 0), plan.points)
    return simple_call(
        functools.partial(merge_kernel, plan, fields, marked),
        [*near, aside],
        [jax.ShapeDtypeStruct(shape, F32)] * plan.pairs,
        [],
        cost,
    )


def route_rows(plan, marks):
    lane = iota((1, plan.rows), 1)
    step = rest(halves(lane, plan.cap), plan.lines)
    filled = marks[:1] > 0.0
    valid = (iota((plan.lines, plan.rows), 0) == step) & filled
    earlier = jnp.dot(valid.astype(BF16), before(plan.rows), preferred_element_type=F32)
    earlier = earlier.astype(jnp.int32)
    row = halves(lane, plan.msg_rows) * plan.cap + rest(lane, plan.cap)
    for m in range(1, plan.lines):
        place = jnp.where(earlier[m : m + 1] < plan.kept[m], earlier[m : m + 1] + plan.offset[m], -1)
        row = jnp.where(step == m, place, row)
    return jnp.where(filled, row, -1)


def gather_marks(plan, fields, messages):
    lane = iota((8, plan.rows), 1)
    marks = jnp.zeros((8, plan.rows), F32)
    base = fields * plan.pair_rows
    for b, message in enumerate(messages):
        part = message[base : base + 8, : plan.rows]
        marks = jnp.where(halves(lane, plan.pair_rows) == b, part, marks)
    return marks


def relay_kernel(plan, fields, marked, *refs):
    messages, refs = refs[: plan.pairs], refs[plan.pairs :]
    if not marked:
        marks_ref, refs = refs[0], refs[1:]
    outs, refs = refs[: plan.lines - 1], refs[plan.lines - 1 :]
    if marked:
        marks = gather_marks(plan, fields, messages)
        marks_out, own_out = refs[:2]
        refs = refs[2:]
        marks_out[...] = marks
    else:
        marks = marks_ref[...]
    (held,) = refs
    row = route_rows(plan, marks)
    spread = (iota((plan.rows, plan.rows), 0) == row).astype(F32)
    if marked:
        landed = lax.dot_general(
            marks, spread, (((1,), (1,)), ((), ())), precision=HIGHEST, preferred_element_type=F32
        )
        own_out[...] = landed
        for m, out in enumerate(outs, 1):
            base = fields * plan.kept[m]
            out[base : base + 8, :] = jnp.zeros((8, plan.points), F32)
            out[base : base + 8, : plan.rows] = landed
    first = plan.offset[1]
    chooser = spread[first : first + plan.relay_rows].astype(BF16)
    for field in range(fields):
        for b, message in enumerate(messages):
            held[b * plan.pair_rows : (b + 1) * plan.pair_rows, :] = message[
                field * plan.pair_rows : (field + 1) * plan.pair_rows, :
            ]
        moved = pick(chooser, held[...])
        for m, out in enumerate(outs, 1):
            at = plan.offset[m] - first
            out[field * plan.kept[m] : (field + 1) * plan.kept[m], :] = moved[at : at + plan.kept[m]]


def relay(plan, group, messages, marks):
    _, fields = group
    marked = marks is None
    extra = 8 if marked else 0
    out_shape = [
        jax.ShapeDtypeStruct((fields * plan.kept[m] + extra, plan.points), F32) for m in range(1, plan.lines)
    ]
    if marked:
        out_shape += [jax.ShapeDtypeStruct((8, plan.rows), F32)] * 2
    operands = list(messages) + ([] if marked else [marks])
    result = pl.pallas_call(
        functools.partial(relay_kernel, plan, fields, marked),
        in_specs=[pl.BlockSpec(memory_space=pltpu.VMEM)] * len(operands),
        out_specs=[pl.BlockSpec(memory_space=pltpu.VMEM)] * len(out_shape),
        out_shape=out_shape,
        scratch_shapes=[pltpu.VMEM((plan.rows, plan.points), F32)],
        compiler_params=PARAMS,
    )(*operands)
    return result[: plan.lines - 1], result[plan.lines - 1 :]


def settle_kernel(plan, fields, marked, *refs):
    messages, refs = refs[: plan.pairs], refs[plan.pairs :]
    relays, refs = refs[: plan.lines - 1], refs[plan.lines - 1 :]
    if marked:
        own_ref, order_ref = refs[:2]
        out, marks_out, cells_out = refs[2:5]
        refs = refs[5:]
    else:
        marks_ref = refs[0]
        out = refs[2]
        refs = refs[3:]
    chooser_ref, held = refs[:2]
    field = pl.program_id(0)
    full = plan.kept[0]

    @pl.when(field == 0)
    def _():
        if marked:
            lane = iota((8, plan.rows), 1)
            marks = jnp.where(lane < full, own_ref[...], 0.0)
            for m in range(1, plan.lines):
                base = fields * plan.kept[m]
                part = relays[m - 1][base : base + 8, : plan.rows]
                inside = (lane >= plan.offset[m]) & (lane < plan.offset[m] + plan.kept[m])
                marks = jnp.where(inside, part, marks)
            marks_out[...] = marks
        else:
            marks = marks_ref[...]
        element = iota((plan.per_dev, plan.rows), 0).astype(F32) + 1.0
        chooser_ref[...] = (element == marks[:1]).astype(F32).astype(BF16)
        used = plan.offset[-1] + plan.kept[-1]
        if used < plan.rows:
            held[used:, :] = jnp.zeros((plan.rows - used, plan.points), F32)

    for j in range(plan.plane):
        start = pl.multiple_of((field * 2 + j % 2) * plan.msg_rows, plan.msg_rows)
        part = messages[j // 2][pl.ds(start, plan.msg_rows), :]
        held[j * plan.cap : (j + 1) * plan.cap, :] = part[: plan.cap]
    for m, part in enumerate(relays, 1):
        kept = plan.kept[m]
        held[plan.offset[m] : plan.offset[m] + kept, :] = part[pl.ds(pl.multiple_of(field * kept, 8), kept), :]
    placed = pick(chooser_ref[...], held[...])
    out[...] = placed.reshape(out.shape)

    if marked:
        pressure_ref = refs[2]

        @pl.when(field == 0)
        def _():
            pressure_ref[...] = 3.0 * placed

        @pl.when(field == 1)
        def _():
            pressure_ref[...] = pressure_ref[...] - 3.0 * placed

        @pl.when(field == 2)
        def _():
            cells_out[...] = pick(order_ref[...], pressure_ref[...] + placed, ((1,), (1,)))


def cell_order(side):
    rows = []
    for k in range(side):
        rows += [(i * side + j) * side + k for i in range(side) for j in range(side)]
        rows += [(i * side + side - 1) * side + k for i in range(side)]
        rows += [(i * side) * side + k for i in range(side)]
    order = np.zeros((len(rows), side**3), np.float32)
    order[np.arange(len(rows)), rows] = 1.0
    return order


def settle(plan, group, messages, relays, marks, buffer, own, order):
    first, fields = group
    marked = marks is None
    columns = BX * BS
    states_shape = (columns, plan.fields, plan.layers, plan.points)
    out_specs = [pl.BlockSpec((columns, 1, plan.layers, plan.points), lambda f: (0, first + f, 0, 0))]
    out_shape = [jax.ShapeDtypeStruct(states_shape, F32)]
    scratch = [pltpu.VMEM((plan.per_dev, plan.rows), BF16), pltpu.VMEM((plan.rows, plan.points), F32)]
    operands = list(messages) + list(relays)
    aliases = {}
    if marked:
        operands += [own, order]
        cells = (order.shape[0], plan.per_dev)
        out_specs += [pl.BlockSpec(memory_space=pltpu.VMEM)] * 2
        out_shape += [jax.ShapeDtypeStruct((8, plan.rows), F32), jax.ShapeDtypeStruct(cells, F32)]
        scratch += [pltpu.VMEM((plan.per_dev, plan.points), F32)]
        in_specs = [pl.BlockSpec(memory_space=pltpu.VMEM)] * len(operands)
    else:
        operands += [marks, buffer]
        in_specs = [pl.BlockSpec(memory_space=pltpu.VMEM)] * (len(operands) - 1) + [pl.BlockSpec(memory_space=pl.ANY)]
        aliases = {len(operands) - 1: 0}
    return pl.pallas_call(
        functools.partial(settle_kernel, plan, fields, marked),
        grid=(fields,),
        in_specs=in_specs,
        out_specs=out_specs,
        out_shape=out_shape,
        scratch_shapes=scratch,
        input_output_aliases=aliases,
        compiler_params=PARAMS,
    )(*operands)


def lane_steps(plan):
    lane = iota((FACE, plan.per_dev), 1)
    layer = rest(lane, plan.layers)
    row_s = rest(halves(lane, plan.layers), BS)
    row_x = halves(lane, plan.layers * BS)
    return layer, row_s, row_x


def roll(value, steps):
    return pltpu.roll(value, steps % value.shape[1], 1)


def solve_kernel(plan, cells, from_xlow, from_xup, from_slow, from_sup, mix, mix_t, weights, sum_xs, values_w, *refs):
    total, out_xlow, out_xup, out_slow, out_sup, box, section, modal = refs
    side, extent = plan.side, plan.extent
    layer, row_s, row_x = lane_steps(plan)
    points = side * side
    stride = points + 2 * FACE
    width = plan.layers
    wide = width * BS
    box_rows = points + 4 * FACE

    def cell(k, start):
        return cells[k * stride + start : k * stride + start + FACE, :]

    def piece(ref, k):
        return ref[k * FACE : (k + 1) * FACE, :]

    for k in range(side):
        w = k + 1
        for i in range(side):
            box[w * box_rows + i * FACE : w * box_rows + (i + 1) * FACE, :] = cell(k, i * FACE)
        at = w * box_rows + points
        low = jnp.where(row_x == 0, roll(piece(from_xlow, k), wide), roll(cell(k, points - FACE), wide))
        up = jnp.where(row_x == BX - 1, roll(piece(from_xup, k), -wide), roll(cell(k, 0), -wide))
        box[at : at + FACE, :] = low
        box[at + FACE : at + 2 * FACE, :] = up
        top, bottom = cell(k, points), cell(k, points + FACE)
        back = (BS - 1) * width
        low = jnp.where(row_s == 0, roll(piece(from_slow, k), -back), roll(top, width))
        up = jnp.where(row_s == BS - 1, roll(piece(from_sup, k), back), roll(bottom, -width))
        box[at + 2 * FACE : at + 3 * FACE, :] = low
        box[at + 3 * FACE : at + 4 * FACE, :] = up
    last = (extent - 1) * box_rows
    for i in range(side):
        below = jnp.where(layer == 0, 0.0, roll(cell(side - 1, i * FACE), 1))
        above = jnp.where(layer == width - 1, 0.0, roll(cell(0, i * FACE), -1))
        box[i * FACE : (i + 1) * FACE, :] = below
        box[last + i * FACE : last + (i + 1) * FACE, :] = above

    modal_rows = mix.shape[0]
    lanes = plan.per_dev
    for w in range(extent):
        rows = points if w in (0, extent - 1) else box_rows
        section[w] = jnp.dot(
            mix[:, :rows], box[w * box_rows : w * box_rows + rows, :], precision=HIGHEST, preferred_element_type=F32
        )
    for block in range(0, modal_rows, FACE):
        held = [section[w, block : block + FACE, :] for w in range(extent)]
        out = [None] * extent
        base = jnp.broadcast_to(sum_xs[block : block + FACE, :], (FACE, lanes))
        for k in range(extent):
            value = None
            for w in range(extent):
                term = weights[w, k : k + 1, :] * held[w]
                value = term if value is None else value + term
            value = value / (base + values_w[k : k + 1, :])
            for w in range(extent):
                term = weights[w, k : k + 1, :] * value
                out[w] = term if out[w] is None else out[w] + term
        for w in range(extent):
            modal[w, block : block + FACE, :] = out[w]
    for w in range(extent):
        rows = points if w in (0, extent - 1) else box_rows
        box[w * box_rows : w * box_rows + rows, :] = jnp.dot(
            mix_t[:rows, :], modal[w], precision=HIGHEST, preferred_element_type=F32
        )

    for k in range(side):
        at = (k + 1) * box_rows
        total[k * points : (k + 1) * points, :] = box[at : at + points, :]
        for out, shift in ((out_xlow, 0), (out_xup, 1), (out_slow, 2), (out_sup, 3)):
            start = at + points + shift * FACE
            out[k * FACE : (k + 1) * FACE, :] = box[start : start + FACE, :]
    for i in range(side):
        below = jnp.where(layer == width - 1, 0.0, roll(box[i * FACE : (i + 1) * FACE, :], -1))
        above = jnp.where(layer == 0, 0.0, roll(box[last + i * FACE : last + (i + 1) * FACE, :], 1))
        top = (side - 1) * points + i * FACE
        total[top : top + FACE, :] += below
        total[i * FACE : (i + 1) * FACE, :] += above


def finish_kernel(plan, total, xlow, xup, slow, sup, from_x_up, from_x_low, from_s_up, from_s_low, out, held):
    side = plan.side
    points = side * side
    layer, row_s, row_x = lane_steps(plan)
    width = plan.layers
    wide = width * BS
    back = (BS - 1) * width
    sub = iota((FACE, plan.per_dev), 0)
    for k in range(side):
        part = slice(k * FACE, (k + 1) * FACE)
        rows = [total[k * points + i * FACE : k * points + (i + 1) * FACE, :] for i in range(side)]
        rows[side - 1] = rows[side - 1] + jnp.where(
            row_x == BX - 1, roll(from_x_up[part, :], -wide), roll(xlow[part, :], -wide)
        )
        rows[0] = rows[0] + jnp.where(row_x == 0, roll(from_x_low[part, :], wide), roll(xup[part, :], wide))
        to_last = jnp.where(row_s == BS - 1, roll(from_s_up[part, :], back), roll(slow[part, :], -width))
        to_first = jnp.where(row_s == 0, roll(from_s_low[part, :], -back), roll(sup[part, :], width))
        for i in range(side):
            last = jnp.broadcast_to(to_last[i : i + 1, :], sub.shape)
            first = jnp.broadcast_to(to_first[i : i + 1, :], sub.shape)
            value = rows[i] + jnp.where(sub == side - 1, last, 0.0) + jnp.where(sub == 0, first, 0.0)
            held[k * points + i * FACE : k * points + (i + 1) * FACE, :] = value
    lanes = plan.layers * side
    source = iota((plan.per_dev, lanes), 0)
    lane = iota((plan.per_dev, lanes), 1)
    terms = three_terms(held[...])
    kept = rest(iota((points, lanes), 1), side)
    for column in range(BX * BS):
        chooser = (source == halves(lane, side) + column * plan.layers).astype(F32).astype(BF16)
        high, middle, low = [jnp.dot(t, chooser, preferred_element_type=F32) for t in terms]
        spread = (high + middle) + low
        value = jnp.zeros((points, lanes), F32)
        for k in range(side):
            value = jnp.where(kept == k, spread[k * points : (k + 1) * points], value)
        b, s = column // BS, column % BS
        for i in range(side):
            out[b * side + i, s * side : (s + 1) * side, :] = value[i * side : (i + 1) * side]


def simple_call(kernel, operands, out_shape, scratch, cost=None):
    return pl.pallas_call(
        kernel,
        in_specs=[pl.BlockSpec(memory_space=pltpu.VMEM)] * len(operands),
        out_specs=[pl.BlockSpec(memory_space=pltpu.VMEM)] * len(out_shape),
        out_shape=out_shape,
        scratch_shapes=scratch,
        compiler_params=PARAMS,
        cost_estimate=cost,
    )(*operands)


def box_tables(plan, vectors_x, vectors_s, vectors_w, values_x, values_s, values_w):
    extent = plan.extent
    rim = [0, extent - 1]
    inside = slice(1, extent - 1)

    def kron(left, right):
        return (left[:, None, :, None] * right[None, :, None, :]).reshape(
            left.shape[0] * right.shape[0], extent * extent
        )

    ends_x = jnp.stack([vectors_x[r] for r in rim])
    ends_s = jnp.stack([vectors_s[r] for r in rim])
    mix_t = jnp.concatenate(
        [
            kron(vectors_x[inside], vectors_s[inside]),
            kron(ends_x, vectors_s[inside]),
            kron(ends_s, vectors_x[inside]).reshape(-1, extent, extent).swapaxes(1, 2).reshape(-1, extent * extent),
        ]
    )
    modal_rows = -(-extent * extent // FACE) * FACE
    more = modal_rows - extent * extent
    mix_t = jnp.pad(mix_t, ((0, 0), (0, more)))
    sum_xs = (values_x[:, None] + values_s[None, :]).reshape(-1, 1)
    sum_xs = jnp.pad(sum_xs, ((0, more), (0, 0)), constant_values=1.0)
    columns = BX * BS
    weights = jnp.tile(jnp.transpose(vectors_w, (1, 2, 0)), (1, 1, columns))
    lane_values = jnp.tile(values_w.T, (1, columns))
    return mix_t.T, mix_t, weights, sum_xs, lane_values


def after(value, earlier):
    return lax.optimization_barrier((value, earlier))[0]


def shards(old_states, new_place, vectors_x, vectors_s, vectors_w, values_x, values_s, values_w):
    n_x, n_y = lax.axis_size("gx"), lax.axis_size("gy")
    slots, fields, points = old_states.shape
    plan = Plan(n_x, n_y, slots, fields, points, vectors_w.shape[0], vectors_x.shape[0])
    place = lax.axis_index("gx") * n_y + lax.axis_index("gy")
    me = place.astype(jnp.int32).reshape(1)
    states = jnp.transpose(old_states, (1, 0, 2))
    place_row = new_place.reshape(1, slots)
    both = ("gx", "gy")

    def across(value, flip):
        return lax.ppermute(value, both, [(d, d ^ flip) for d in range(plan.devices)])

    def shifted(value, axis, steps):
        count = lax.axis_size(axis)
        return lax.ppermute(value, axis, [(s, (s + steps) % count) for s in range(count)])

    order = jnp.asarray(cell_order(plan.side), BF16)
    tables = box_tables(plan, vectors_x, vectors_s, vectors_w, values_x, values_s, values_w)

    merged = []
    for g, group in enumerate(plan.groups):
        *near, aside = pack(plan, group, me, place_row, states, g == 0)
        cost = pl.CostEstimate(flops=MERGE_FLOPS if g else 0, bytes_accessed=0, transcendentals=0)
        merged.append(functools.partial(merge, plan, group, near, across(aside, 1), g == 0, cost))
    marks = None
    held = []
    gate = None
    arrived = [None] * (plan.lines - 1)
    for g, group in enumerate(plan.groups):
        if g:
            near = merged[g].args[2]
            merged[g] = functools.partial(
                merge, plan, group, [after(near[0], gate)] + near[1:], *merged[g].args[3:]
            )
        sent = merged[g]()
        messages = [sent[0]] + [across(sent[b], 2 * b) for b in range(1, plan.pairs)]
        relays, more = relay(plan, group, messages, marks)
        if marks is None:
            marks, own = more
        gate = relays[0]
        for m in reversed(range(1, plan.lines)):
            ready = relays[m - 1]
            if g:
                ready = after(ready, arrived[m - 1])
            arrived[m - 1] = across(ready, m * plan.plane)
        held.append((messages, list(arrived)))

    buffer, row_marks, cells = settle(plan, plan.groups[0], *held[0], None, None, own, order)
    side = plan.side
    face = jax.ShapeDtypeStruct((side * FACE, plan.per_dev), F32)
    layered = cells.reshape(side, side * side + 2 * FACE, plan.per_dev)

    def rows(start):
        return layered[:, start : start + FACE].reshape(side * FACE, plan.per_dev)

    inner = side * side
    halo = [
        shifted(rows(inner - FACE), "gx", 1),
        shifted(rows(0), "gx", -1),
        shifted(rows(inner), "gy", 1),
        shifted(rows(inner + FACE), "gy", -1),
    ]
    modal_rows = tables[0].shape[0]
    total, xlow, xup, slow, sup = simple_call(
        functools.partial(solve_kernel, plan),
        [cells, *halo, *tables],
        [jax.ShapeDtypeStruct((side * inner, plan.per_dev), F32)] + [face] * 4,
        [pltpu.VMEM((plan.extent * (inner + 4 * FACE), plan.per_dev), F32)]
        + [pltpu.VMEM((plan.extent, modal_rows, plan.per_dev), F32)] * 2,
    )
    returned = [shifted(xlow, "gx", -1), shifted(xup, "gx", 1), shifted(slow, "gy", -1), shifted(sup, "gy", 1)]
    (correction,) = simple_call(
        functools.partial(finish_kernel, plan),
        [total, xlow, xup, slow, sup, *returned],
        [jax.ShapeDtypeStruct((BX * side, BS * side, plan.layers * side), F32)],
        [pltpu.VMEM((side * inner, plan.per_dev), F32)],
    )
    for group, (messages, arrived) in zip(plan.groups[1:], held[1:]):
        (buffer,) = settle(plan, group, messages, arrived, row_marks, buffer, None, None)
    new_states = buffer.reshape(BX, BS, fields, plan.layers, points).transpose(0, 1, 3, 2, 4)
    return new_states, correction


def solution(mesh):
    placed = (P(("gx", "gy"), None, None), P(("gx", "gy")), P(), P(), P(), P(), P(), P())
    return jax.shard_map(
        shards,
        mesh=mesh,
        in_specs=placed,
        out_specs=(P("gx", "gy", None, None, None), P("gx", "gy", None)),
        check_vma=False,
    )
```

```python
import functools

import jax
import jax.numpy as jnp
import numpy as np
from jax import lax
from jax.experimental import pallas as pl
from jax.experimental.pallas import tpu as pltpu
from jax.sharding import PartitionSpec as P

BX = 4
BS = 2
FACE = 8
MERGE_FLOPS = 40_000_000_000
VMEM_LIMIT = 12 * 1024 * 1024
PARAMS = pltpu.CompilerParams(vmem_limit_bytes=VMEM_LIMIT)
HIGHEST = lax.Precision.HIGHEST
F32 = jnp.float32
BF16 = jnp.bfloat16


class Plan:
    def __init__(self, n_x, n_y, slots, fields, points, layers, extent):
        self.n_x, self.n_y = n_x, n_y
        self.devices = n_x * n_y
        self.lines = n_x // 2
        self.plane = self.devices // self.lines
        self.slots, self.fields, self.points = slots, fields, points
        self.layers, self.extent, self.side = layers, extent, extent - 2
        self.per_dev = BX * BS * layers
        self.cap = 2 * self.per_dev // self.devices
        self.msg_rows = self.lines * self.cap
        self.pairs = self.plane // 2
        self.pair_rows = 2 * self.msg_rows
        self.rows = self.plane * self.msg_rows
        self.full = self.plane * self.cap
        self.kept = [self.full] * 2 + [self.full * 3 // 4] * (self.lines - 2)
        self.spill = [m for m in range(self.lines) if self.kept[m] < self.full]
        second = (fields - 3) * 4 // 9
        self.groups = [(0, 3), (3, second), (3 + second, fields - 3 - second)]


def halves(value, count):
    if count & (count - 1) == 0:
        return lax.shift_right_logical(value, int(count).bit_length() - 1)
    return value // count


def rest(value, count):
    if count & (count - 1) == 0:
        return value & (count - 1)
    return value % count


def three_terms(value):
    high = value.astype(BF16)
    left = value - high.astype(F32)
    middle = left.astype(BF16)
    low = (left - middle.astype(F32)).astype(BF16)
    return high, middle, low


def pick(chooser, value, contract=((1,), (0,))):
    high, middle, low = three_terms(value)
    dims = (contract, ((), ()))
    product = functools.partial(lax.dot_general, dimension_numbers=dims, preferred_element_type=F32)
    return (product(chooser, high) + product(chooser, middle)) + product(chooser, low)


def iota(shape, dim):
    return lax.broadcasted_iota(jnp.int32, shape, dim)


def before(count):
    return (iota((count, count), 0) < iota((count, count), 1)).astype(BF16)


def pack_kernel(plan, fields, marked, me_ref, place_ref, states_ref, *refs):
    outs, chooser_ref = refs[:-1], refs[-1]
    field = pl.program_id(0)
    rows = plan.msg_rows

    @pl.when(field == 0)
    def _():
        me = me_ref[0]
        new_place = place_ref[...]
        live = new_place >= 0
        placed = jnp.maximum(new_place, 0)
        column = halves(placed, plan.layers)
        layer_pos = rest(placed, plan.layers)
        span = BS * plan.n_y
        elem_x = halves(column, span)
        elem_s = rest(column, span)
        target = halves(elem_x, BX) * plan.n_y + halves(elem_s, BS)
        local_row = (rest(elem_x, BX) * BS + rest(elem_s, BS)) * plan.layers + layer_pos
        target = jnp.where(live, target, -1)
        hot = iota((plan.devices, plan.slots), 0) == target
        earlier = jnp.dot(hot.astype(BF16), before(plan.slots), preferred_element_type=F32)
        rank = jnp.sum(jnp.where(hot, earlier, 0.0), axis=0, keepdims=True).astype(jnp.int32)
        across = target ^ me
        row = rest(across, plan.plane) * rows + halves(across, plan.plane) * plan.cap + rank
        row = jnp.where(live, row, -1)
        chooser = (iota((plan.rows, plan.slots), 0) == row).astype(F32)
        chooser_ref[...] = chooser.astype(BF16)
        if marked:
            marks = lax.dot_general(
                jnp.broadcast_to((local_row + 1).astype(F32), (8, plan.slots)),
                chooser,
                (((1,), (1,)), ((), ())),
                precision=HIGHEST,
                preferred_element_type=F32,
            )
            for out, held in zip(outs, [rows] * (len(outs) - 1) + [rows * plan.pairs]):
                out[fields * held : fields * held + 8, :] = jnp.zeros((8, plan.points), F32)
                out[fields * held : fields * held + 8, : plan.rows] = marks

    moved = pick(chooser_ref[...], states_ref[0])
    start = pl.multiple_of(field * rows, rows)
    aside = pl.multiple_of(field * rows * plan.pairs, rows)
    for b in range(plan.pairs):
        outs[b][pl.ds(start, rows), :] = moved[2 * b * rows : (2 * b + 1) * rows]
        outs[-1][pl.ds(aside + b * rows, rows), :] = moved[(2 * b + 1) * rows : (2 * b + 2) * rows]


def whole(shape):
    return pl.BlockSpec(shape, lambda *_: (0,) * len(shape))


def pack(plan, group, me, place_row, states, marked):
    first, fields = group
    extra = 8 if marked else 0
    shapes = [(fields * plan.msg_rows + extra, plan.points)] * plan.pairs
    shapes.append((fields * plan.msg_rows * plan.pairs + extra, plan.points))
    return pl.pallas_call(
        functools.partial(pack_kernel, plan, fields, marked),
        grid=(fields,),
        in_specs=[
            pl.BlockSpec(memory_space=pltpu.SMEM),
            whole((1, plan.slots)),
            pl.BlockSpec((1, plan.slots, plan.points), lambda f: (first + f, 0, 0)),
        ],
        out_specs=[pl.BlockSpec(memory_space=pltpu.VMEM)] * len(shapes),
        out_shape=[jax.ShapeDtypeStruct(shape, F32) for shape in shapes],
        scratch_shapes=[pltpu.VMEM((plan.rows, plan.slots), BF16)],
        compiler_params=PARAMS,
    )(me, place_row, states)


def merge_kernel(plan, fields, marked, flagged, *refs):
    near, refs = refs[: plan.pairs], refs[plan.pairs :]
    aside, outs = refs[0], refs[-plan.pairs :]
    rows = plan.msg_rows
    for b, out in enumerate(outs):
        for field in range(fields):
            start = field * plan.pair_rows
            other = (field * plan.pairs + b) * rows
            out[start : start + rows, :] = near[b][field * rows : (field + 1) * rows, :]
            out[start + rows : start + 2 * rows, :] = aside[other : other + rows, :]
        if marked:
            lane = iota((8, plan.rows), 1)
            mine = near[0][fields * rows : fields * rows + 8, : plan.rows]
            base = fields * rows * plan.pairs
            other = aside[base : base + 8, : plan.rows]
            marks = jnp.where(rest(halves(lane, rows), 2) == 0, mine, other)
            base = fields * plan.pair_rows
            out[base : base + 8, :] = jnp.zeros((8, plan.points), F32)
            out[base : base + 8, : plan.rows] = marks
        if flagged:
            base = fields * plan.pair_rows
            out[base : base + 8, :] = jnp.zeros((8, plan.points), F32)
            out[base : base + 8, : plan.rows] = jnp.maximum(refs[1][...], refs[2][...])


def merge(plan, group, near, aside, marked, flags, cost):
    _, fields = group
    shape = (fields * plan.pair_rows + (8 if marked or flags else 0), plan.points)
    return simple_call(
        functools.partial(merge_kernel, plan, fields, marked, bool(flags)),
        [*near, aside, *flags],
        [jax.ShapeDtypeStruct(shape, F32)] * plan.pairs,
        [],
        cost,
    )


def route_rows(plan, marks):
    lane = iota((1, plan.rows), 1)
    step = rest(halves(lane, plan.cap), plan.lines)
    filled = marks[:1] > 0.0
    valid = (iota((plan.lines, plan.rows), 0) == step) & filled
    earlier = jnp.dot(valid.astype(BF16), before(plan.rows), preferred_element_type=F32)
    earlier = earlier.astype(jnp.int32)
    row = halves(lane, plan.msg_rows) * plan.cap + rest(lane, plan.cap)
    over = jnp.zeros((1, plan.rows), F32)
    for m in range(1, plan.lines):
        number = earlier[m : m + 1]
        row = jnp.where(step == m, number + m * plan.full, row)
        over = jnp.maximum(over, jnp.where((step == m) & filled & (number >= plan.kept[m]), 1.0, 0.0))
    return jnp.where(filled, row, -1), jnp.max(over, axis=1, keepdims=True)


def gather_marks(plan, fields, messages):
    lane = iota((8, plan.rows), 1)
    marks = jnp.zeros((8, plan.rows), F32)
    base = fields * plan.pair_rows
    for b, message in enumerate(messages):
        part = message[base : base + 8, : plan.rows]
        marks = jnp.where(halves(lane, plan.pair_rows) == b, part, marks)
    return marks


def put_tail(plan, out, value):
    base = out.shape[0] - 8
    out[base:, :] = jnp.zeros((8, plan.points), F32)
    out[base:, : plan.rows] = value


def relay_kernel(plan, fields, marked, flagged, *refs):
    messages, refs = refs[: plan.pairs], refs[plan.pairs :]
    if not marked:
        marks_ref, refs = refs[0], refs[1:]
    outs, refs = refs[: plan.lines - 1], refs[plan.lines - 1 :]
    late, refs = refs[: len(plan.spill)], refs[len(plan.spill) :]
    held = refs[-1]
    marks = gather_marks(plan, fields, messages) if marked else marks_ref[...]
    row, over = route_rows(plan, marks)
    spread = (iota((plan.rows, plan.rows), 0) == row).astype(F32)
    if marked:
        marks_out, own_out, flag_out = refs[:3]
        landed = lax.dot_general(
            marks, spread, (((1,), (1,)), ((), ())), precision=HIGHEST, preferred_element_type=F32
        )
        marks_out[...] = marks
        own_out[...] = landed
        flag_out[...] = jnp.broadcast_to(over, (8, plan.rows))
        for out in outs:
            put_tail(plan, out, landed)
    if flagged:
        flag = messages[0][fields * plan.pair_rows :, : plan.rows]
        for message in messages[1:]:
            flag = jnp.maximum(flag, message[fields * plan.pair_rows :, : plan.rows])
        refs[0][...] = flag
        for out in outs:
            put_tail(plan, out, flag)
    chooser = spread[plan.full :].astype(BF16)
    for field in range(fields):
        for b, message in enumerate(messages):
            held[b * plan.pair_rows : (b + 1) * plan.pair_rows, :] = message[
                field * plan.pair_rows : (field + 1) * plan.pair_rows, :
            ]
        moved = pick(chooser, held[...])
        for m, out in enumerate(outs, 1):
            at, kept = (m - 1) * plan.full, plan.kept[m]
            out[field * kept : (field + 1) * kept, :] = moved[at : at + kept]
        for m, out in zip(plan.spill, late):
            at, kept = (m - 1) * plan.full, plan.kept[m]
            left = plan.full - kept
            out[field * left : (field + 1) * left, :] = moved[at + kept : at + plan.full]


def relay(plan, group, messages, marks, flagged):
    _, fields = group
    marked = marks is None
    extra = 8 if marked or flagged else 0
    shapes = [(fields * kept + extra, plan.points) for kept in plan.kept[1:]]
    shapes += [(fields * (plan.full - plan.kept[m]), plan.points) for m in plan.spill]
    shapes += [(8, plan.rows)] * (3 if marked else 1 if flagged else 0)
    result = simple_call(
        functools.partial(relay_kernel, plan, fields, marked, flagged),
        list(messages) + ([] if marked else [marks]),
        [jax.ShapeDtypeStruct(shape, F32) for shape in shapes],
        [pltpu.VMEM((plan.rows, plan.points), F32)],
    )
    split = plan.lines - 1
    return result[:split], result[split : split + len(plan.spill)], result[split + len(plan.spill) :]


def element_chooser(plan, marks):
    element = iota((plan.per_dev, plan.rows), 0).astype(F32) + 1.0
    return (element == marks[:1]).astype(F32).astype(BF16)


def settle_kernel(plan, fields, marked, flagged, *refs):
    messages, refs = refs[: plan.pairs], refs[plan.pairs :]
    relays, refs = refs[: plan.lines - 1], refs[plan.lines - 1 :]
    if marked or flagged:
        tails, refs = refs[: plan.lines - 1], refs[plan.lines - 1 :]
    if marked:
        own_ref, order_ref, out, marks_out, cells_out, chooser_ref, held, pressure_ref = refs
    elif flagged:
        marks_ref, flag_ref, _, out, flag_out, chooser_ref, held = refs
    else:
        marks_ref, _, out, chooser_ref, held = refs
    field = pl.program_id(0)

    @pl.when(field == 0)
    def _():
        if marked:
            lane = iota((8, plan.rows), 1)
            marks = own_ref[...]
            for m in range(1, plan.lines):
                marks = jnp.where(halves(lane, plan.full) == m, tails[m - 1][:, : plan.rows], marks)
            marks_out[...] = marks
        else:
            marks = marks_ref[...]
        if flagged:
            flag = flag_ref[...]
            for tail in tails:
                flag = jnp.maximum(flag, tail[:, : plan.rows])
            flag_out[...] = flag
        chooser_ref[...] = element_chooser(plan, marks)
        for m in plan.spill:
            start = m * plan.full + plan.kept[m]
            held[start : (m + 1) * plan.full, :] = jnp.zeros((plan.full - plan.kept[m], plan.points), F32)

    for j in range(plan.plane):
        start = j % 2 * plan.msg_rows
        held[j * plan.cap : (j + 1) * plan.cap, :] = messages[j // 2][start : start + plan.cap, :]
    for m, part in enumerate(relays, 1):
        held[m * plan.full : m * plan.full + plan.kept[m], :] = part[...]
    placed = pick(chooser_ref[...], held[...])
    out[...] = placed.reshape(out.shape)

    if marked:

        @pl.when(field == 0)
        def _():
            pressure_ref[...] = 3.0 * placed

        @pl.when(field == 1)
        def _():
            pressure_ref[...] = pressure_ref[...] - 3.0 * placed

        @pl.when(field == 2)
        def _():
            cells_out[...] = pick(order_ref[...], pressure_ref[...] + placed, ((1,), (1,)))


def cell_order(side):
    rows = []
    for k in range(side):
        rows += [(i * side + j) * side + k for i in range(side) for j in range(side)]
        rows += [(i * side + side - 1) * side + k for i in range(side)]
        rows += [(i * side) * side + k for i in range(side)]
    order = np.zeros((len(rows), side**3), np.float32)
    order[np.arange(len(rows)), rows] = 1.0
    return order


def states_block(plan, first):
    columns = BX * BS
    block = pl.BlockSpec((columns, 1, plan.layers, plan.points), lambda f: (0, first + f, 0, 0))
    return block, jax.ShapeDtypeStruct((columns, plan.fields, plan.layers, plan.points), F32)


def settle(plan, group, messages, relays, marks, buffer, own, order, flag):
    first, fields = group
    marked, flagged = marks is None, flag is not None
    in_vmem = pl.BlockSpec(memory_space=pltpu.VMEM)
    block, states = states_block(plan, first)
    out_specs, out_shape = [block], [states]
    scratch = [pltpu.VMEM((plan.per_dev, plan.rows), BF16), pltpu.VMEM((plan.rows, plan.points), F32)]
    operands = list(messages) + list(relays)
    in_specs = [pl.BlockSpec((plan.pair_rows, plan.points), lambda f: (f, 0))] * plan.pairs
    in_specs += [pl.BlockSpec((kept, plan.points), lambda f: (f, 0)) for kept in plan.kept[1:]]
    if marked or flagged:
        operands += list(relays)
        in_specs += [
            pl.BlockSpec((8, plan.points), lambda f, at=fields * kept // 8: (at, 0)) for kept in plan.kept[1:]
        ]
    known = [own, order] if marked else [marks, flag] if flagged else [marks]
    operands += known
    in_specs += [in_vmem] * len(known)
    aliases = {}
    row = jax.ShapeDtypeStruct((8, plan.rows), F32)
    if marked:
        out_shape += [row, jax.ShapeDtypeStruct((order.shape[0], plan.per_dev), F32)]
        out_specs += [in_vmem] * 2
        scratch += [pltpu.VMEM((plan.per_dev, plan.points), F32)]
    else:
        aliases = {len(operands): 0}
        operands += [buffer]
        in_specs += [pl.BlockSpec(memory_space=pl.ANY)]
        if flagged:
            out_shape += [row]
            out_specs += [in_vmem]
    return pl.pallas_call(
        functools.partial(settle_kernel, plan, fields, marked, flagged),
        grid=(fields,),
        in_specs=in_specs,
        out_specs=out_specs,
        out_shape=out_shape,
        scratch_shapes=scratch,
        input_output_aliases=aliases,
        compiler_params=PARAMS,
    )(*operands)


def add_late_kernel(plan, *refs):
    parts, (marks_ref, states_ref, out, held) = refs[: len(plan.spill)], refs[len(plan.spill) :]
    held[...] = jnp.zeros(held.shape, F32)
    for m, part in zip(plan.spill, parts):
        held[m * plan.full + plan.kept[m] : (m + 1) * plan.full, :] = part[...]
    placed = pick(element_chooser(plan, marks_ref[...]), held[...])
    out[...] = states_ref[...] + placed.reshape(out.shape)


def add_late(plan, group, parts, marks, buffer):
    first, fields = group
    block, states = states_block(plan, first)
    return pl.pallas_call(
        functools.partial(add_late_kernel, plan),
        grid=(fields,),
        in_specs=[pl.BlockSpec((plan.full - plan.kept[m], plan.points), lambda f: (f, 0)) for m in plan.spill]
        + [pl.BlockSpec(memory_space=pltpu.VMEM), block],
        out_specs=block,
        out_shape=states,
        scratch_shapes=[pltpu.VMEM((plan.rows, plan.points), F32)],
        input_output_aliases={len(parts) + 1: 0},
        compiler_params=PARAMS,
    )(*parts, marks, buffer)


def cells_kernel(plan, states_ref, order_ref, out):
    held = states_ref[...]
    pressure = 3.0 * held[:, 0] - 3.0 * held[:, 1] + held[:, 2]
    out[...] = pick(order_ref[...], pressure.reshape(plan.per_dev, plan.points), ((1,), (1,)))


def cells_of(plan, buffer, order):
    return pl.pallas_call(
        functools.partial(cells_kernel, plan),
        grid=(1,),
        in_specs=[
            pl.BlockSpec((BX * BS, 3, plan.layers, plan.points), lambda f: (0, 0, 0, 0)),
            whole(order.shape),
        ],
        out_specs=whole((order.shape[0], plan.per_dev)),
        out_shape=jax.ShapeDtypeStruct((order.shape[0], plan.per_dev), F32),
        compiler_params=PARAMS,
    )(buffer, order)


def lane_steps(plan):
    lane = iota((FACE, plan.per_dev), 1)
    layer = rest(lane, plan.layers)
    row_s = rest(halves(lane, plan.layers), BS)
    row_x = halves(lane, plan.layers * BS)
    return layer, row_s, row_x


def roll(value, steps):
    return pltpu.roll(value, steps % value.shape[1], 1)


def solve_kernel(plan, cells, from_xlow, from_xup, from_slow, from_sup, mix, mix_t, weights, sum_xs, values_w, *refs):
    total, out_xlow, out_xup, out_slow, out_sup, box, section, modal = refs
    side, extent = plan.side, plan.extent
    layer, row_s, row_x = lane_steps(plan)
    points = side * side
    stride = points + 2 * FACE
    width = plan.layers
    wide = width * BS
    box_rows = points + 4 * FACE

    def cell(k, start):
        return cells[k * stride + start : k * stride + start + FACE, :]

    def piece(ref, k):
        return ref[k * FACE : (k + 1) * FACE, :]

    for k in range(side):
        w = k + 1
        for i in range(side):
            box[w * box_rows + i * FACE : w * box_rows + (i + 1) * FACE, :] = cell(k, i * FACE)
        at = w * box_rows + points
        low = jnp.where(row_x == 0, roll(piece(from_xlow, k), wide), roll(cell(k, points - FACE), wide))
        up = jnp.where(row_x == BX - 1, roll(piece(from_xup, k), -wide), roll(cell(k, 0), -wide))
        box[at : at + FACE, :] = low
        box[at + FACE : at + 2 * FACE, :] = up
        top, bottom = cell(k, points), cell(k, points + FACE)
        back = (BS - 1) * width
        low = jnp.where(row_s == 0, roll(piece(from_slow, k), -back), roll(top, width))
        up = jnp.where(row_s == BS - 1, roll(piece(from_sup, k), back), roll(bottom, -width))
        box[at + 2 * FACE : at + 3 * FACE, :] = low
        box[at + 3 * FACE : at + 4 * FACE, :] = up
    last = (extent - 1) * box_rows
    for i in range(side):
        below = jnp.where(layer == 0, 0.0, roll(cell(side - 1, i * FACE), 1))
        above = jnp.where(layer == width - 1, 0.0, roll(cell(0, i * FACE), -1))
        box[i * FACE : (i + 1) * FACE, :] = below
        box[last + i * FACE : last + (i + 1) * FACE, :] = above

    modal_rows = mix.shape[0]
    lanes = plan.per_dev
    for w in range(extent):
        rows = points if w in (0, extent - 1) else box_rows
        section[w] = jnp.dot(
            mix[:, :rows], box[w * box_rows : w * box_rows + rows, :], precision=HIGHEST, preferred_element_type=F32
        )
    for block in range(0, modal_rows, FACE):
        held = [section[w, block : block + FACE, :] for w in range(extent)]
        out = [None] * extent
        base = jnp.broadcast_to(sum_xs[block : block + FACE, :], (FACE, lanes))
        for k in range(extent):
            value = None
            for w in range(extent):
                term = weights[w, k : k + 1, :] * held[w]
                value = term if value is None else value + term
            value = value / (base + values_w[k : k + 1, :])
            for w in range(extent):
                term = weights[w, k : k + 1, :] * value
                out[w] = term if out[w] is None else out[w] + term
        for w in range(extent):
            modal[w, block : block + FACE, :] = out[w]
    for w in range(extent):
        rows = points if w in (0, extent - 1) else box_rows
        box[w * box_rows : w * box_rows + rows, :] = jnp.dot(
            mix_t[:rows, :], modal[w], precision=HIGHEST, preferred_element_type=F32
        )

    for k in range(side):
        at = (k + 1) * box_rows
        total[k * points : (k + 1) * points, :] = box[at : at + points, :]
        for out, shift in ((out_xlow, 0), (out_xup, 1), (out_slow, 2), (out_sup, 3)):
            start = at + points + shift * FACE
            out[k * FACE : (k + 1) * FACE, :] = box[start : start + FACE, :]
    for i in range(side):
        below = jnp.where(layer == width - 1, 0.0, roll(box[i * FACE : (i + 1) * FACE, :], -1))
        above = jnp.where(layer == 0, 0.0, roll(box[last + i * FACE : last + (i + 1) * FACE, :], 1))
        top = (side - 1) * points + i * FACE
        total[top : top + FACE, :] += below
        total[i * FACE : (i + 1) * FACE, :] += above


def finish_kernel(plan, total, xlow, xup, slow, sup, from_x_up, from_x_low, from_s_up, from_s_low, out, held):
    side = plan.side
    points = side * side
    layer, row_s, row_x = lane_steps(plan)
    width = plan.layers
    wide = width * BS
    back = (BS - 1) * width
    sub = iota((FACE, plan.per_dev), 0)
    for k in range(side):
        part = slice(k * FACE, (k + 1) * FACE)
        rows = [total[k * points + i * FACE : k * points + (i + 1) * FACE, :] for i in range(side)]
        rows[side - 1] = rows[side - 1] + jnp.where(
            row_x == BX - 1, roll(from_x_up[part, :], -wide), roll(xlow[part, :], -wide)
        )
        rows[0] = rows[0] + jnp.where(row_x == 0, roll(from_x_low[part, :], wide), roll(xup[part, :], wide))
        to_last = jnp.where(row_s == BS - 1, roll(from_s_up[part, :], back), roll(slow[part, :], -width))
        to_first = jnp.where(row_s == 0, roll(from_s_low[part, :], -back), roll(sup[part, :], width))
        for i in range(side):
            last = jnp.broadcast_to(to_last[i : i + 1, :], sub.shape)
            first = jnp.broadcast_to(to_first[i : i + 1, :], sub.shape)
            value = rows[i] + jnp.where(sub == side - 1, last, 0.0) + jnp.where(sub == 0, first, 0.0)
            held[k * points + i * FACE : k * points + (i + 1) * FACE, :] = value
    lanes = plan.layers * side
    source = iota((plan.per_dev, lanes), 0)
    lane = iota((plan.per_dev, lanes), 1)
    terms = three_terms(held[...])
    kept = rest(iota((points, lanes), 1), side)
    for column in range(BX * BS):
        chooser = (source == halves(lane, side) + column * plan.layers).astype(F32).astype(BF16)
        high, middle, low = [jnp.dot(t, chooser, preferred_element_type=F32) for t in terms]
        spread = (high + middle) + low
        value = jnp.zeros((points, lanes), F32)
        for k in range(side):
            value = jnp.where(kept == k, spread[k * points : (k + 1) * points], value)
        b, s = column // BS, column % BS
        for i in range(side):
            out[b * side + i, s * side : (s + 1) * side, :] = value[i * side : (i + 1) * side]


def simple_call(kernel, operands, out_shape, scratch, cost=None):
    return pl.pallas_call(
        kernel,
        in_specs=[pl.BlockSpec(memory_space=pltpu.VMEM)] * len(operands),
        out_specs=[pl.BlockSpec(memory_space=pltpu.VMEM)] * len(out_shape),
        out_shape=out_shape,
        scratch_shapes=scratch,
        compiler_params=PARAMS,
        cost_estimate=cost,
    )(*operands)


def box_tables(plan, vectors_x, vectors_s, vectors_w, values_x, values_s, values_w):
    extent = plan.extent
    rim = [0, extent - 1]
    inside = slice(1, extent - 1)

    def kron(left, right):
        return (left[:, None, :, None] * right[None, :, None, :]).reshape(
            left.shape[0] * right.shape[0], extent * extent
        )

    ends_x = jnp.stack([vectors_x[r] for r in rim])
    ends_s = jnp.stack([vectors_s[r] for r in rim])
    mix_t = jnp.concatenate(
        [
            kron(vectors_x[inside], vectors_s[inside]),
            kron(ends_x, vectors_s[inside]),
            kron(ends_s, vectors_x[inside]).reshape(-1, extent, extent).swapaxes(1, 2).reshape(-1, extent * extent),
        ]
    )
    modal_rows = -(-extent * extent // FACE) * FACE
    more = modal_rows - extent * extent
    mix_t = jnp.pad(mix_t, ((0, 0), (0, more)))
    sum_xs = (values_x[:, None] + values_s[None, :]).reshape(-1, 1)
    sum_xs = jnp.pad(sum_xs, ((0, more), (0, 0)), constant_values=1.0)
    columns = BX * BS
    weights = jnp.tile(jnp.transpose(vectors_w, (1, 2, 0)), (1, 1, columns))
    lane_values = jnp.tile(values_w.T, (1, columns))
    return mix_t.T, mix_t, weights, sum_xs, lane_values


def after(value, earlier):
    return lax.optimization_barrier((value, earlier))[0]


def shards(old_states, new_place, vectors_x, vectors_s, vectors_w, values_x, values_s, values_w):
    n_x, n_y = lax.axis_size("gx"), lax.axis_size("gy")
    slots, fields, points = old_states.shape
    plan = Plan(n_x, n_y, slots, fields, points, vectors_w.shape[0], vectors_x.shape[0])
    place = lax.axis_index("gx") * n_y + lax.axis_index("gy")
    me = place.astype(jnp.int32).reshape(1)
    states = jnp.transpose(old_states, (1, 0, 2))
    place_row = new_place.reshape(1, slots)
    both = ("gx", "gy")

    def across(value, flip):
        return lax.ppermute(value, both, [(d, d ^ flip) for d in range(plan.devices)])

    def shifted(value, axis, steps):
        count = lax.axis_size(axis)
        return lax.ppermute(value, axis, [(s, (s + steps) % count) for s in range(count)])

    order = jnp.asarray(cell_order(plan.side), BF16)
    tables = box_tables(plan, vectors_x, vectors_s, vectors_w, values_x, values_s, values_w)

    side = plan.side
    inner = side * side

    def solve(cells, earlier):
        layered = cells.reshape(side, inner + 2 * FACE, plan.per_dev)

        def rows(start):
            return layered[:, start : start + FACE].reshape(side * FACE, plan.per_dev)

        halo = [
            shifted(rows(inner - FACE), "gx", 1),
            shifted(rows(0), "gx", -1),
            shifted(rows(inner), "gy", 1),
            shifted(rows(inner + FACE), "gy", -1),
        ]
        if earlier is not None:
            cells = after(cells, earlier)
        face = jax.ShapeDtypeStruct((side * FACE, plan.per_dev), F32)
        sections = (plan.extent, tables[0].shape[0], plan.per_dev)
        total, xlow, xup, slow, sup = simple_call(
            functools.partial(solve_kernel, plan),
            [cells, *halo, *tables],
            [jax.ShapeDtypeStruct((side * inner, plan.per_dev), F32)] + [face] * 4,
            [pltpu.VMEM((plan.extent * (inner + 4 * FACE), plan.per_dev), F32)] + [pltpu.VMEM(sections, F32)] * 2,
        )
        returned = [shifted(xlow, "gx", -1), shifted(xup, "gx", 1), shifted(slow, "gy", -1), shifted(sup, "gy", 1)]
        (correction,) = simple_call(
            functools.partial(finish_kernel, plan),
            [total, xlow, xup, slow, sup, *returned],
            [jax.ShapeDtypeStruct((BX * side, BS * side, plan.layers * side), F32)],
            [pltpu.VMEM((side * inner, plan.per_dev), F32)],
        )
        return correction

    packed = []
    for g, group in enumerate(plan.groups):
        *near, aside = pack(plan, group, me, place_row, states, g == 0)
        packed.append((near, across(aside, 1)))

    marks = gate = None
    flags, arrived, held = [], [], []
    for g, (group, (near, aside)) in enumerate(zip(plan.groups, packed)):
        first, flagged = g == 0, g == 1
        if not first:
            near[0] = after(near[0], gate)
        cost = pl.CostEstimate(flops=0 if first else MERGE_FLOPS, bytes_accessed=0, transcendentals=0)
        sent = merge(plan, group, near, aside, first, flags if flagged else [], cost)
        messages = [sent[0]] + [across(sent[b], 2 * b) for b in range(1, plan.pairs)]
        if not first:
            messages[0] = after(messages[0], arrived[1:])
        relays, late, more = relay(plan, group, messages, marks, flagged)
        if first:
            marks, own, over = more
            flags = [over, across(over, 1)]
        if flagged:
            (flag,) = more
        gate = relays[0]
        ready = list(relays)
        ready[0] = after(ready[0], messages[1:] if first else [messages[1], arrived[0]])
        arrived = [across(r, m * plan.plane) for m, r in enumerate(ready, 1)]
        held.append((messages, arrived, late))

    buffer, row_marks, cells = settle(plan, plan.groups[0], *held[0][:2], None, None, own, order, None)
    buffer, flag = settle(plan, plan.groups[1], *held[1][:2], row_marks, buffer, None, None, flag)
    correction = solve(after(cells, gate), buffer)
    for group, (messages, arrived, _) in zip(plan.groups[2:], held[2:]):
        (buffer,) = settle(plan, group, messages, arrived, row_marks, buffer, None, None, None)

    def send_rest(buffer, correction, late):
        for group, parts in zip(plan.groups, late):
            parts = [across(part, m * plan.plane) for m, part in zip(plan.spill, parts)]
            buffer = add_late(plan, group, parts, row_marks, buffer)
        return buffer, solve(cells_of(plan, buffer, order), None)

    def keep(buffer, correction, late):
        return buffer, correction

    late = [rows_left for _, _, rows_left in held]
    if plan.spill:
        buffer, correction = lax.cond(flag[0, 0] > 0.0, send_rest, keep, buffer, correction, late)
    new_states = buffer.reshape(BX, BS, fields, plan.layers, points).transpose(0, 1, 3, 2, 4)
    return new_states, correction


def solution(mesh):
    placed = (P(("gx", "gy"), None, None), P(("gx", "gy")), P(), P(), P(), P(), P(), P())
    return jax.shard_map(
        shards,
        mesh=mesh,
        in_specs=placed,
        out_specs=(P("gx", "gy", None, None, None), P("gx", "gy", None)),
        check_vma=False,
    )
```

```python
import functools

import jax
import jax.numpy as jnp
import numpy as np
from jax import lax
from jax.experimental import pallas as pl
from jax.experimental.pallas import tpu as pltpu
from jax.sharding import PartitionSpec as P

BX = 4
BS = 2
FACE = 8
MERGE_FLOPS = 40_000_000_000
VMEM_LIMIT = 12 * 1024 * 1024
PARAMS = pltpu.CompilerParams(vmem_limit_bytes=VMEM_LIMIT)
HIGHEST = lax.Precision.HIGHEST
F32 = jnp.float32
BF16 = jnp.bfloat16


class Plan:
    def __init__(self, n_x, n_y, slots, fields, points, layers, extent):
        self.n_x, self.n_y = n_x, n_y
        self.devices = n_x * n_y
        self.lines = n_x // 2
        self.plane = self.devices // self.lines
        self.slots, self.fields, self.points = slots, fields, points
        self.layers, self.extent, self.side = layers, extent, extent - 2
        self.per_dev = BX * BS * layers
        self.cap = 2 * self.per_dev // self.devices
        self.msg_rows = self.lines * self.cap
        self.pairs = self.plane // 2
        self.pair_rows = 2 * self.msg_rows
        self.rows = self.plane * self.msg_rows
        self.full = self.plane * self.cap
        self.kept = [self.full] * 2 + [self.full * 3 // 4] * (self.lines - 2)
        self.spill = [m for m in range(self.lines) if self.kept[m] < self.full]
        second = (fields - 3) * 4 // 9
        self.groups = [(0, 3), (3, second), (3 + second, fields - 3 - second)]


def halves(value, count):
    if count & (count - 1) == 0:
        return lax.shift_right_logical(value, int(count).bit_length() - 1)
    return value // count


def rest(value, count):
    if count & (count - 1) == 0:
        return value & (count - 1)
    return value % count


def three_terms(value):
    high = value.astype(BF16)
    left = value - high.astype(F32)
    middle = left.astype(BF16)
    low = (left - middle.astype(F32)).astype(BF16)
    return high, middle, low


def pick(chooser, value, contract=((1,), (0,))):
    high, middle, low = three_terms(value)
    dims = (contract, ((), ()))
    product = functools.partial(lax.dot_general, dimension_numbers=dims, preferred_element_type=F32)
    return (product(chooser, high) + product(chooser, middle)) + product(chooser, low)


def iota(shape, dim):
    return lax.broadcasted_iota(jnp.int32, shape, dim)


def before(count):
    return (iota((count, count), 0) < iota((count, count), 1)).astype(BF16)


def pack_kernel(plan, fields, marked, me_ref, place_ref, states_ref, *refs):
    outs, chooser_ref = refs[:-1], refs[-1]
    field = pl.program_id(0)
    rows = plan.msg_rows

    @pl.when(field == 0)
    def _():
        me = me_ref[0]
        new_place = place_ref[...]
        live = new_place >= 0
        placed = jnp.maximum(new_place, 0)
        column = halves(placed, plan.layers)
        layer_pos = rest(placed, plan.layers)
        span = BS * plan.n_y
        elem_x = halves(column, span)
        elem_s = rest(column, span)
        target = halves(elem_x, BX) * plan.n_y + halves(elem_s, BS)
        local_row = (rest(elem_x, BX) * BS + rest(elem_s, BS)) * plan.layers + layer_pos
        target = jnp.where(live, target, -1)
        hot = iota((plan.devices, plan.slots), 0) == target
        earlier = jnp.dot(hot.astype(BF16), before(plan.slots), preferred_element_type=F32)
        rank = jnp.sum(jnp.where(hot, earlier, 0.0), axis=0, keepdims=True).astype(jnp.int32)
        across = target ^ me
        row = rest(across, plan.plane) * rows + halves(across, plan.plane) * plan.cap + rank
        row = jnp.where(live, row, -1)
        chooser = (iota((plan.rows, plan.slots), 0) == row).astype(F32)
        chooser_ref[...] = chooser.astype(BF16)
        if marked:
            marks = lax.dot_general(
                jnp.broadcast_to((local_row + 1).astype(F32), (8, plan.slots)),
                chooser,
                (((1,), (1,)), ((), ())),
                precision=HIGHEST,
                preferred_element_type=F32,
            )
            for out, held in zip(outs, [rows] * (len(outs) - 1) + [rows * plan.pairs]):
                out[fields * held : fields * held + 8, :] = jnp.zeros((8, plan.points), F32)
                out[fields * held : fields * held + 8, : plan.rows] = marks

    moved = pick(chooser_ref[...], states_ref[0])
    start = pl.multiple_of(field * rows, rows)
    aside = pl.multiple_of(field * rows * plan.pairs, rows)
    for b in range(plan.pairs):
        outs[b][pl.ds(start, rows), :] = moved[2 * b * rows : (2 * b + 1) * rows]
        outs[-1][pl.ds(aside + b * rows, rows), :] = moved[(2 * b + 1) * rows : (2 * b + 2) * rows]


def whole(shape):
    return pl.BlockSpec(shape, lambda *_: (0,) * len(shape))


def pack(plan, group, me, place_row, states, marked):
    first, fields = group
    extra = 8 if marked else 0
    shapes = [(fields * plan.msg_rows + extra, plan.points)] * plan.pairs
    shapes.append((fields * plan.msg_rows * plan.pairs + extra, plan.points))
    return pl.pallas_call(
        functools.partial(pack_kernel, plan, fields, marked),
        grid=(fields,),
        in_specs=[
            pl.BlockSpec(memory_space=pltpu.SMEM),
            whole((1, plan.slots)),
            pl.BlockSpec((1, plan.slots, plan.points), lambda f: (first + f, 0, 0)),
        ],
        out_specs=[pl.BlockSpec(memory_space=pltpu.VMEM)] * len(shapes),
        out_shape=[jax.ShapeDtypeStruct(shape, F32) for shape in shapes],
        scratch_shapes=[pltpu.VMEM((plan.rows, plan.slots), BF16)],
        compiler_params=PARAMS,
    )(me, place_row, states)


def merge_kernel(plan, fields, marked, flagged, *refs):
    near, refs = refs[: plan.pairs], refs[plan.pairs :]
    aside, outs = refs[0], refs[-plan.pairs :]
    rows = plan.msg_rows
    for b, out in enumerate(outs):
        for field in range(fields):
            start = field * plan.pair_rows
            other = (field * plan.pairs + b) * rows
            out[start : start + rows, :] = near[b][field * rows : (field + 1) * rows, :]
            out[start + rows : start + 2 * rows, :] = aside[other : other + rows, :]
        if marked:
            lane = iota((8, plan.rows), 1)
            mine = near[0][fields * rows : fields * rows + 8, : plan.rows]
            base = fields * rows * plan.pairs
            other = aside[base : base + 8, : plan.rows]
            marks = jnp.where(rest(halves(lane, rows), 2) == 0, mine, other)
            base = fields * plan.pair_rows
            out[base : base + 8, :] = jnp.zeros((8, plan.points), F32)
            out[base : base + 8, : plan.rows] = marks
        if flagged:
            base = fields * plan.pair_rows
            out[base : base + 8, :] = jnp.zeros((8, plan.points), F32)
            out[base : base + 8, : plan.rows] = refs[1][...]


def merge(plan, group, near, aside, marked, flags, cost):
    _, fields = group
    shape = (fields * plan.pair_rows + (8 if marked or flags else 0), plan.points)
    return simple_call(
        functools.partial(merge_kernel, plan, fields, marked, bool(flags)),
        [*near, aside, *flags],
        [jax.ShapeDtypeStruct(shape, F32)] * plan.pairs,
        [],
        cost,
    )


def route_rows(plan, marks):
    lane = iota((1, plan.rows), 1)
    step = rest(halves(lane, plan.cap), plan.lines)
    filled = marks[:1] > 0.0
    valid = (iota((plan.lines, plan.rows), 0) == step) & filled
    earlier = jnp.dot(valid.astype(BF16), before(plan.rows), preferred_element_type=F32)
    earlier = earlier.astype(jnp.int32)
    row = halves(lane, plan.msg_rows) * plan.cap + rest(lane, plan.cap)
    over = jnp.zeros((1, plan.rows), F32)
    for m in range(1, plan.lines):
        number = earlier[m : m + 1]
        row = jnp.where(step == m, number + m * plan.full, row)
        over = jnp.maximum(over, jnp.where((step == m) & filled & (number >= plan.kept[m]), 1.0, 0.0))
    return jnp.where(filled, row, -1), jnp.max(over, axis=1, keepdims=True)


def gather_marks(plan, fields, messages):
    lane = iota((8, plan.rows), 1)
    marks = jnp.zeros((8, plan.rows), F32)
    base = fields * plan.pair_rows
    for b, message in enumerate(messages):
        part = message[base : base + 8, : plan.rows]
        marks = jnp.where(halves(lane, plan.pair_rows) == b, part, marks)
    return marks


def put_tail(plan, out, value):
    base = out.shape[0] - 8
    out[base:, :] = jnp.zeros((8, plan.points), F32)
    out[base:, : plan.rows] = value


def relay_kernel(plan, fields, marked, flagged, *refs):
    messages, refs = refs[: plan.pairs], refs[plan.pairs :]
    if not marked:
        marks_ref, refs = refs[0], refs[1:]
    outs, refs = refs[: plan.lines - 1], refs[plan.lines - 1 :]
    late, refs = refs[: len(plan.spill)], refs[len(plan.spill) :]
    held = refs[-1]
    marks = gather_marks(plan, fields, messages) if marked else marks_ref[...]
    row, over = route_rows(plan, marks)
    spread = (iota((plan.rows, plan.rows), 0) == row).astype(F32)
    if marked:
        marks_out, own_out, flag_out = refs[:3]
        landed = lax.dot_general(
            marks, spread, (((1,), (1,)), ((), ())), precision=HIGHEST, preferred_element_type=F32
        )
        marks_out[...] = marks
        own_out[...] = landed
        flag_out[...] = jnp.broadcast_to(over, (8, plan.rows))
        for out in outs:
            put_tail(plan, out, landed)
    if flagged:
        flag = messages[0][fields * plan.pair_rows :, : plan.rows]
        for message in messages[1:]:
            flag = jnp.maximum(flag, message[fields * plan.pair_rows :, : plan.rows])
        refs[0][...] = flag
        for out in outs:
            put_tail(plan, out, flag)
    chooser = spread[plan.full :].astype(BF16)
    for field in range(fields):
        for b, message in enumerate(messages):
            held[b * plan.pair_rows : (b + 1) * plan.pair_rows, :] = message[
                field * plan.pair_rows : (field + 1) * plan.pair_rows, :
            ]
        moved = pick(chooser, held[...])
        for m, out in enumerate(outs, 1):
            at, kept = (m - 1) * plan.full, plan.kept[m]
            out[field * kept : (field + 1) * kept, :] = moved[at : at + kept]
        for m, out in zip(plan.spill, late):
            at, kept = (m - 1) * plan.full, plan.kept[m]
            left = plan.full - kept
            out[field * left : (field + 1) * left, :] = moved[at + kept : at + plan.full]


def relay(plan, group, messages, marks, flagged):
    _, fields = group
    marked = marks is None
    extra = 8 if marked or flagged else 0
    shapes = [(fields * kept + extra, plan.points) for kept in plan.kept[1:]]
    shapes += [(fields * (plan.full - plan.kept[m]), plan.points) for m in plan.spill]
    shapes += [(8, plan.rows)] * (3 if marked else 1 if flagged else 0)
    result = simple_call(
        functools.partial(relay_kernel, plan, fields, marked, flagged),
        list(messages) + ([] if marked else [marks]),
        [jax.ShapeDtypeStruct(shape, F32) for shape in shapes],
        [pltpu.VMEM((plan.rows, plan.points), F32)],
    )
    split = plan.lines - 1
    return result[:split], result[split : split + len(plan.spill)], result[split + len(plan.spill) :]


def element_chooser(plan, marks):
    element = iota((plan.per_dev, plan.rows), 0).astype(F32) + 1.0
    return (element == marks[:1]).astype(F32).astype(BF16)


def settle_kernel(plan, fields, marked, flagged, *refs):
    messages, refs = refs[: plan.pairs], refs[plan.pairs :]
    relays, refs = refs[: plan.lines - 1], refs[plan.lines - 1 :]
    if marked or flagged:
        tails, refs = refs[: plan.lines - 1], refs[plan.lines - 1 :]
    if marked:
        own_ref, order_ref, out, marks_out, cells_out, chooser_ref, held, pressure_ref = refs
    elif flagged:
        marks_ref, flag_ref, _, out, flag_out, chooser_ref, held = refs
    else:
        marks_ref, _, out, chooser_ref, held = refs
    field = pl.program_id(0)

    @pl.when(field == 0)
    def _():
        if marked:
            lane = iota((8, plan.rows), 1)
            marks = own_ref[...]
            for m in range(1, plan.lines):
                marks = jnp.where(halves(lane, plan.full) == m, tails[m - 1][:, : plan.rows], marks)
            marks_out[...] = marks
        else:
            marks = marks_ref[...]
        if flagged:
            flag = flag_ref[...]
            for tail in tails:
                flag = jnp.maximum(flag, tail[:, : plan.rows])
            flag_out[...] = flag
        chooser_ref[...] = element_chooser(plan, marks)
        for m in plan.spill:
            start = m * plan.full + plan.kept[m]
            held[start : (m + 1) * plan.full, :] = jnp.zeros((plan.full - plan.kept[m], plan.points), F32)

    for j in range(plan.plane):
        start = j % 2 * plan.msg_rows
        held[j * plan.cap : (j + 1) * plan.cap, :] = messages[j // 2][start : start + plan.cap, :]
    for m, part in enumerate(relays, 1):
        held[m * plan.full : m * plan.full + plan.kept[m], :] = part[...]
    placed = pick(chooser_ref[...], held[...])
    out[...] = placed.reshape(out.shape)

    if marked:

        @pl.when(field == 0)
        def _():
            pressure_ref[...] = 3.0 * placed

        @pl.when(field == 1)
        def _():
            pressure_ref[...] = pressure_ref[...] - 3.0 * placed

        @pl.when(field == 2)
        def _():
            cells_out[...] = pick(order_ref[...], pressure_ref[...] + placed, ((1,), (1,)))


def cell_order(side):
    rows = []
    for k in range(side):
        rows += [(i * side + j) * side + k for i in range(side) for j in range(side)]
        rows += [(i * side + side - 1) * side + k for i in range(side)]
        rows += [(i * side) * side + k for i in range(side)]
    order = np.zeros((len(rows), side**3), np.float32)
    order[np.arange(len(rows)), rows] = 1.0
    return order


def states_block(plan, first):
    columns = BX * BS
    block = pl.BlockSpec((columns, 1, plan.layers, plan.points), lambda f: (0, first + f, 0, 0))
    return block, jax.ShapeDtypeStruct((columns, plan.fields, plan.layers, plan.points), F32)


def settle(plan, group, messages, relays, marks, buffer, own, order, flag):
    first, fields = group
    marked, flagged = marks is None, flag is not None
    in_vmem = pl.BlockSpec(memory_space=pltpu.VMEM)
    block, states = states_block(plan, first)
    out_specs, out_shape = [block], [states]
    scratch = [pltpu.VMEM((plan.per_dev, plan.rows), BF16), pltpu.VMEM((plan.rows, plan.points), F32)]
    operands = list(messages) + list(relays)
    in_specs = [pl.BlockSpec((plan.pair_rows, plan.points), lambda f: (f, 0))] * plan.pairs
    in_specs += [pl.BlockSpec((kept, plan.points), lambda f: (f, 0)) for kept in plan.kept[1:]]
    if marked or flagged:
        operands += list(relays)
        in_specs += [
            pl.BlockSpec((8, plan.points), lambda f, at=fields * kept // 8: (at, 0)) for kept in plan.kept[1:]
        ]
    known = [own, order] if marked else [marks, flag] if flagged else [marks]
    operands += known
    in_specs += [in_vmem] * len(known)
    aliases = {}
    row = jax.ShapeDtypeStruct((8, plan.rows), F32)
    if marked:
        out_shape += [row, jax.ShapeDtypeStruct((order.shape[0], plan.per_dev), F32)]
        out_specs += [in_vmem] * 2
        scratch += [pltpu.VMEM((plan.per_dev, plan.points), F32)]
    else:
        aliases = {len(operands): 0}
        operands += [buffer]
        in_specs += [pl.BlockSpec(memory_space=pl.ANY)]
        if flagged:
            out_shape += [row]
            out_specs += [in_vmem]
    return pl.pallas_call(
        functools.partial(settle_kernel, plan, fields, marked, flagged),
        grid=(fields,),
        in_specs=in_specs,
        out_specs=out_specs,
        out_shape=out_shape,
        scratch_shapes=scratch,
        input_output_aliases=aliases,
        compiler_params=PARAMS,
    )(*operands)


def add_late_kernel(plan, *refs):
    parts, (marks_ref, states_ref, out, held) = refs[: len(plan.spill)], refs[len(plan.spill) :]
    held[...] = jnp.zeros(held.shape, F32)
    for m, part in zip(plan.spill, parts):
        held[m * plan.full + plan.kept[m] : (m + 1) * plan.full, :] = part[...]
    placed = pick(element_chooser(plan, marks_ref[...]), held[...])
    out[...] = states_ref[...] + placed.reshape(out.shape)


def add_late(plan, group, parts, marks, buffer):
    first, fields = group
    block, states = states_block(plan, first)
    return pl.pallas_call(
        functools.partial(add_late_kernel, plan),
        grid=(fields,),
        in_specs=[pl.BlockSpec((plan.full - plan.kept[m], plan.points), lambda f: (f, 0)) for m in plan.spill]
        + [pl.BlockSpec(memory_space=pltpu.VMEM), block],
        out_specs=block,
        out_shape=states,
        scratch_shapes=[pltpu.VMEM((plan.rows, plan.points), F32)],
        input_output_aliases={len(parts) + 1: 0},
        compiler_params=PARAMS,
    )(*parts, marks, buffer)


def cells_kernel(plan, states_ref, order_ref, out):
    held = states_ref[...]
    pressure = 3.0 * held[:, 0] - 3.0 * held[:, 1] + held[:, 2]
    out[...] = pick(order_ref[...], pressure.reshape(plan.per_dev, plan.points), ((1,), (1,)))


def cells_of(plan, buffer, order):
    return pl.pallas_call(
        functools.partial(cells_kernel, plan),
        grid=(1,),
        in_specs=[
            pl.BlockSpec((BX * BS, 3, plan.layers, plan.points), lambda f: (0, 0, 0, 0)),
            whole(order.shape),
        ],
        out_specs=whole((order.shape[0], plan.per_dev)),
        out_shape=jax.ShapeDtypeStruct((order.shape[0], plan.per_dev), F32),
        compiler_params=PARAMS,
    )(buffer, order)


def lane_steps(plan):
    lane = iota((FACE, plan.per_dev), 1)
    layer = rest(lane, plan.layers)
    row_s = rest(halves(lane, plan.layers), BS)
    row_x = halves(lane, plan.layers * BS)
    return layer, row_s, row_x


def roll(value, steps):
    return pltpu.roll(value, steps % value.shape[1], 1)


def solve_kernel(plan, cells, from_xlow, from_xup, from_slow, from_sup, *refs):
    tables, refs = refs[:10], refs[10:]
    total, out_xlow, out_xup, out_slow, out_sup, box, section, modal, weights, values_w = refs
    vectors_x, vectors_s, vectors_w, own_x, own_s, own_w, pick_x, pick_s, spread_x, spread_s = tables
    side, extent = plan.side, plan.extent
    layer, row_s, row_x = lane_steps(plan)
    points = side * side
    stride = points + 2 * FACE
    width = plan.layers
    wide = width * BS
    box_rows = points + 4 * FACE

    def cell(k, start):
        return cells[k * stride + start : k * stride + start + FACE, :]

    def piece(ref, k):
        return ref[k * FACE : (k + 1) * FACE, :]

    for k in range(side):
        w = k + 1
        for i in range(side):
            box[w * box_rows + i * FACE : w * box_rows + (i + 1) * FACE, :] = cell(k, i * FACE)
        at = w * box_rows + points
        low = jnp.where(row_x == 0, roll(piece(from_xlow, k), wide), roll(cell(k, points - FACE), wide))
        up = jnp.where(row_x == BX - 1, roll(piece(from_xup, k), -wide), roll(cell(k, 0), -wide))
        box[at : at + FACE, :] = low
        box[at + FACE : at + 2 * FACE, :] = up
        top, bottom = cell(k, points), cell(k, points + FACE)
        back = (BS - 1) * width
        low = jnp.where(row_s == 0, roll(piece(from_slow, k), -back), roll(top, width))
        up = jnp.where(row_s == BS - 1, roll(piece(from_sup, k), back), roll(bottom, -width))
        box[at + 2 * FACE : at + 3 * FACE, :] = low
        box[at + 3 * FACE : at + 4 * FACE, :] = up
    last = (extent - 1) * box_rows
    for i in range(side):
        below = jnp.where(layer == 0, 0.0, roll(cell(side - 1, i * FACE), 1))
        above = jnp.where(layer == width - 1, 0.0, roll(cell(0, i * FACE), -1))
        box[i * FACE : (i + 1) * FACE, :] = below
        box[last + i * FACE : last + (i + 1) * FACE, :] = above

    def exact(left, right, contract=((1,), (0,))):
        dims = (contract, ((), ()))
        return lax.dot_general(left, right, dims, precision=HIGHEST, preferred_element_type=F32)

    mix_t = exact(exact(pick_x[...], vectors_x[...]), spread_x[...], ((1,), (1,)))
    mix_t = mix_t * exact(exact(pick_s[...], vectors_s[...]), spread_s[...], ((1,), (1,)))
    modal_rows = spread_x.shape[0]
    lanes = plan.per_dev
    held_by = (iota((width, lanes), 0) == rest(iota((width, lanes), 1), width)).astype(F32)
    for w in range(extent):
        weights[w] = exact(vectors_w[w], held_by, ((0,), (0,)))
    values_w[...] = exact(own_w[...], held_by, ((0,), (0,)))
    sum_xs = jnp.sum(spread_x[...] * own_x[...] + spread_s[...] * own_s[...], axis=1, keepdims=True)
    sum_xs = jnp.where(iota(sum_xs.shape, 0) < extent * extent, sum_xs, 1.0)
    for w in range(extent):
        rows = points if w in (0, extent - 1) else box_rows
        section[w] = exact(mix_t[:rows], box[w * box_rows : w * box_rows + rows, :], ((0,), (0,)))
    for block in range(0, modal_rows, FACE):
        held = [section[w, block : block + FACE, :] for w in range(extent)]
        out = [None] * extent
        base = jnp.broadcast_to(sum_xs[block : block + FACE], (FACE, lanes))
        for k in range(extent):
            value = None
            for w in range(extent):
                term = weights[w, k : k + 1, :] * held[w]
                value = term if value is None else value + term
            value = value / (base + values_w[k : k + 1, :])
            for w in range(extent):
                term = weights[w, k : k + 1, :] * value
                out[w] = term if out[w] is None else out[w] + term
        for w in range(extent):
            modal[w, block : block + FACE, :] = out[w]
    for w in range(extent):
        rows = points if w in (0, extent - 1) else box_rows
        box[w * box_rows : w * box_rows + rows, :] = exact(mix_t[:rows], modal[w])

    for k in range(side):
        at = (k + 1) * box_rows
        total[k * points : (k + 1) * points, :] = box[at : at + points, :]
        for out, shift in ((out_xlow, 0), (out_xup, 1), (out_slow, 2), (out_sup, 3)):
            start = at + points + shift * FACE
            out[k * FACE : (k + 1) * FACE, :] = box[start : start + FACE, :]
    for i in range(side):
        below = jnp.where(layer == width - 1, 0.0, roll(box[i * FACE : (i + 1) * FACE, :], -1))
        above = jnp.where(layer == 0, 0.0, roll(box[last + i * FACE : last + (i + 1) * FACE, :], 1))
        top = (side - 1) * points + i * FACE
        total[top : top + FACE, :] += below
        total[i * FACE : (i + 1) * FACE, :] += above


def finish_kernel(plan, total, xlow, xup, slow, sup, from_x_up, from_x_low, from_s_up, from_s_low, out, held):
    side = plan.side
    points = side * side
    layer, row_s, row_x = lane_steps(plan)
    width = plan.layers
    wide = width * BS
    back = (BS - 1) * width
    sub = iota((FACE, plan.per_dev), 0)
    for k in range(side):
        part = slice(k * FACE, (k + 1) * FACE)
        rows = [total[k * points + i * FACE : k * points + (i + 1) * FACE, :] for i in range(side)]
        rows[side - 1] = rows[side - 1] + jnp.where(
            row_x == BX - 1, roll(from_x_up[part, :], -wide), roll(xlow[part, :], -wide)
        )
        rows[0] = rows[0] + jnp.where(row_x == 0, roll(from_x_low[part, :], wide), roll(xup[part, :], wide))
        to_last = jnp.where(row_s == BS - 1, roll(from_s_up[part, :], back), roll(slow[part, :], -width))
        to_first = jnp.where(row_s == 0, roll(from_s_low[part, :], -back), roll(sup[part, :], width))
        for i in range(side):
            last = jnp.broadcast_to(to_last[i : i + 1, :], sub.shape)
            first = jnp.broadcast_to(to_first[i : i + 1, :], sub.shape)
            value = rows[i] + jnp.where(sub == side - 1, last, 0.0) + jnp.where(sub == 0, first, 0.0)
            held[k * points + i * FACE : k * points + (i + 1) * FACE, :] = value
    lanes = plan.layers * side
    source = iota((plan.per_dev, lanes), 0)
    lane = iota((plan.per_dev, lanes), 1)
    terms = three_terms(held[...])
    kept = rest(iota((points, lanes), 1), side)
    for column in range(BX * BS):
        chooser = (source == halves(lane, side) + column * plan.layers).astype(F32).astype(BF16)
        high, middle, low = [jnp.dot(t, chooser, preferred_element_type=F32) for t in terms]
        spread = (high + middle) + low
        value = jnp.zeros((points, lanes), F32)
        for k in range(side):
            value = jnp.where(kept == k, spread[k * points : (k + 1) * points], value)
        b, s = column // BS, column % BS
        for i in range(side):
            out[b * side + i, s * side : (s + 1) * side, :] = value[i * side : (i + 1) * side]


def simple_call(kernel, operands, out_shape, scratch, cost=None):
    return pl.pallas_call(
        kernel,
        in_specs=[pl.BlockSpec(memory_space=pltpu.VMEM)] * len(operands),
        out_specs=[pl.BlockSpec(memory_space=pltpu.VMEM)] * len(out_shape),
        out_shape=out_shape,
        scratch_shapes=scratch,
        compiler_params=PARAMS,
        cost_estimate=cost,
    )(*operands)


def box_rows_of(extent):
    inside = range(1, extent - 1)
    points = [(u, v) for u in inside for v in inside]
    points += [(u, v) for u in (0, extent - 1) for v in inside]
    points += [(u, v) for v in (0, extent - 1) for u in inside]
    modes = [(i, j) for i in range(extent) for j in range(extent)]
    modal_rows = -(-len(modes) // FACE) * FACE

    def hot(rows, values):
        table = np.zeros((rows, extent), np.float32)
        table[np.arange(len(values)), values] = 1.0
        return jnp.asarray(table)

    us, vs = zip(*points)
    i_s, j_s = zip(*modes)
    return hot(len(us), us), hot(len(vs), vs), hot(modal_rows, i_s), hot(modal_rows, j_s)


def after(value, earlier):
    return lax.optimization_barrier((value, earlier))[0]


def shards(old_states, new_place, vectors_x, vectors_s, vectors_w, values_x, values_s, values_w):
    n_x, n_y = lax.axis_size("gx"), lax.axis_size("gy")
    slots, fields, points = old_states.shape
    plan = Plan(n_x, n_y, slots, fields, points, vectors_w.shape[0], vectors_x.shape[0])
    place = lax.axis_index("gx") * n_y + lax.axis_index("gy")
    me = place.astype(jnp.int32).reshape(1)
    states = jnp.transpose(old_states, (1, 0, 2))
    place_row = new_place.reshape(1, slots)
    both = ("gx", "gy")

    def across(value, flip):
        return lax.ppermute(value, both, [(d, d ^ flip) for d in range(plan.devices)])

    def shifted(value, axis, steps):
        count = lax.axis_size(axis)
        return lax.ppermute(value, axis, [(s, (s + steps) % count) for s in range(count)])

    order = jnp.asarray(cell_order(plan.side), BF16)
    tables = [vectors_x, vectors_s, jnp.transpose(vectors_w, (1, 0, 2))]
    tables += [values_x.reshape(1, -1), values_s.reshape(1, -1), values_w, *box_rows_of(plan.extent)]

    side = plan.side
    inner = side * side

    def solve(cells, earlier):
        layered = cells.reshape(side, inner + 2 * FACE, plan.per_dev)

        def rows(start):
            return layered[:, start : start + FACE].reshape(side * FACE, plan.per_dev)

        halo = [
            shifted(rows(inner - FACE), "gx", 1),
            shifted(rows(0), "gx", -1),
            shifted(rows(inner), "gy", 1),
            shifted(rows(inner + FACE), "gy", -1),
        ]
        if earlier is not None:
            cells = after(cells, earlier)
        face = jax.ShapeDtypeStruct((side * FACE, plan.per_dev), F32)
        sections = (plan.extent, tables[-1].shape[0], plan.per_dev)
        total, xlow, xup, slow, sup = simple_call(
            functools.partial(solve_kernel, plan),
            [cells, *halo, *tables],
            [jax.ShapeDtypeStruct((side * inner, plan.per_dev), F32)] + [face] * 4,
            [pltpu.VMEM((plan.extent * (inner + 4 * FACE), plan.per_dev), F32)]
            + [pltpu.VMEM(sections, F32)] * 2
            + [pltpu.VMEM((plan.extent, plan.extent, plan.per_dev), F32)]
            + [pltpu.VMEM((plan.extent, plan.per_dev), F32)],
        )
        returned = [shifted(xlow, "gx", -1), shifted(xup, "gx", 1), shifted(slow, "gy", -1), shifted(sup, "gy", 1)]
        (correction,) = simple_call(
            functools.partial(finish_kernel, plan),
            [total, xlow, xup, slow, sup, *returned],
            [jax.ShapeDtypeStruct((BX * side, BS * side, plan.layers * side), F32)],
            [pltpu.VMEM((side * inner, plan.per_dev), F32)],
        )
        return correction

    packed = []
    for g, group in enumerate(plan.groups):
        *near, aside = pack(plan, group, me, place_row, states, g == 0)
        packed.append((near, across(aside, 1)))

    marks = gate = None
    flags, arrived, held = [], [], []
    for g, (group, (near, aside)) in enumerate(zip(plan.groups, packed)):
        first, flagged = g == 0, g == 1
        if not first:
            near[0] = after(near[0], gate)
        cost = pl.CostEstimate(flops=0 if first else MERGE_FLOPS, bytes_accessed=0, transcendentals=0)
        sent = merge(plan, group, near, aside, first, flags if flagged else [], cost)
        messages = [sent[0]] + [across(sent[b], 2 * b) for b in range(1, plan.pairs)]
        if not first:
            messages[0] = after(messages[0], arrived[1:])
        relays, late, more = relay(plan, group, messages, marks, flagged)
        if first:
            marks, own, over = more
            flags = [over]
        if flagged:
            (flag,) = more
        gate = relays[0]
        ready = list(relays)
        ready[0] = after(ready[0], messages[1:] if first else [messages[1], arrived[0]])
        arrived = [across(r, m * plan.plane) for m, r in enumerate(ready, 1)]
        held.append((messages, arrived, late))

    buffer, row_marks, cells = settle(plan, plan.groups[0], *held[0][:2], None, None, own, order, None)
    buffer, flag = settle(plan, plan.groups[1], *held[1][:2], row_marks, buffer, None, None, flag)
    flag = jnp.maximum(flag[:1, :1], across(flag, 1)[:1, :1])
    correction = solve(after(cells, gate), buffer)
    for group, (messages, arrived, _) in zip(plan.groups[2:], held[2:]):
        (buffer,) = settle(plan, group, messages, arrived, row_marks, buffer, None, None, None)

    def send_rest(buffer, correction, late):
        for group, parts in zip(plan.groups, late):
            parts = [across(part, m * plan.plane) for m, part in zip(plan.spill, parts)]
            buffer = add_late(plan, group, parts, row_marks, buffer)
        return buffer, solve(cells_of(plan, buffer, order), None)

    def keep(buffer, correction, late):
        return buffer, correction

    late = [rows_left for _, _, rows_left in held]
    if plan.spill:
        buffer, correction = lax.cond(flag[0, 0] > 0.0, send_rest, keep, buffer, correction, late)
    new_states = buffer.reshape(BX, BS, fields, plan.layers, points).transpose(0, 1, 3, 2, 4)
    return new_states, correction


def solution(mesh):
    placed = (P(("gx", "gy"), None, None), P(("gx", "gy")), P(), P(), P(), P(), P(), P())
    return jax.shard_map(
        shards,
        mesh=mesh,
        in_specs=placed,
        out_specs=(P("gx", "gy", None, None, None), P("gx", "gy", None)),
        check_vma=False,
    )
```

```python
import functools

import jax
import jax.numpy as jnp
import numpy as np
from jax import lax
from jax.experimental import pallas as pl
from jax.experimental.pallas import tpu as pltpu
from jax.sharding import PartitionSpec as P

BX = 4
BS = 2
FACE = 8
MERGE_FLOPS = 40_000_000_000
VMEM_LIMIT = 12 * 1024 * 1024
PARAMS = pltpu.CompilerParams(vmem_limit_bytes=VMEM_LIMIT)
HIGHEST = lax.Precision.HIGHEST
F32 = jnp.float32
BF16 = jnp.bfloat16


class Plan:
    def __init__(self, n_x, n_y, slots, fields, points, layers, extent):
        self.n_x, self.n_y = n_x, n_y
        self.devices = n_x * n_y
        self.lines = n_x // 2
        self.plane = self.devices // self.lines
        self.slots, self.fields, self.points = slots, fields, points
        self.layers, self.extent, self.side = layers, extent, extent - 2
        self.per_dev = BX * BS * layers
        self.cap = 2 * self.per_dev // self.devices
        self.msg_rows = self.lines * self.cap
        self.pairs = self.plane // 2
        self.pair_rows = 2 * self.msg_rows
        self.rows = self.plane * self.msg_rows
        self.full = self.plane * self.cap
        self.kept = [self.full] * 2 + [self.full * 3 // 4] * (self.lines - 2)
        self.spill = [m for m in range(self.lines) if self.kept[m] < self.full]
        second = (fields - 3) * 4 // 9
        self.groups = [(0, 3), (3, second), (3 + second, fields - 3 - second)]


def halves(value, count):
    if count & (count - 1) == 0:
        return lax.shift_right_logical(value, int(count).bit_length() - 1)
    return value // count


def rest(value, count):
    if count & (count - 1) == 0:
        return value & (count - 1)
    return value % count


def three_terms(value):
    high = value.astype(BF16)
    left = value - high.astype(F32)
    middle = left.astype(BF16)
    low = (left - middle.astype(F32)).astype(BF16)
    return high, middle, low


def pick(chooser, value, contract=((1,), (0,))):
    high, middle, low = three_terms(value)
    dims = (contract, ((), ()))
    product = functools.partial(lax.dot_general, dimension_numbers=dims, preferred_element_type=F32)
    return (product(chooser, high) + product(chooser, middle)) + product(chooser, low)


def iota(shape, dim):
    return lax.broadcasted_iota(jnp.int32, shape, dim)


def before(count):
    return (iota((count, count), 0) < iota((count, count), 1)).astype(BF16)


def pack_kernel(plan, fields, marked, me_ref, place_ref, states_ref, *refs):
    outs, chooser_ref = refs[:-1], refs[-1]
    field = pl.program_id(0)
    rows = plan.msg_rows

    @pl.when(field == 0)
    def _():
        me = me_ref[0]
        new_place = place_ref[...]
        live = new_place >= 0
        placed = jnp.maximum(new_place, 0)
        column = halves(placed, plan.layers)
        layer_pos = rest(placed, plan.layers)
        span = BS * plan.n_y
        elem_x = halves(column, span)
        elem_s = rest(column, span)
        target = halves(elem_x, BX) * plan.n_y + halves(elem_s, BS)
        local_row = (rest(elem_x, BX) * BS + rest(elem_s, BS)) * plan.layers + layer_pos
        target = jnp.where(live, target, -1)
        hot = iota((plan.devices, plan.slots), 0) == target
        earlier = jnp.dot(hot.astype(BF16), before(plan.slots), preferred_element_type=F32)
        rank = jnp.sum(jnp.where(hot, earlier, 0.0), axis=0, keepdims=True).astype(jnp.int32)
        across = target ^ me
        row = rest(across, plan.plane) * rows + halves(across, plan.plane) * plan.cap + rank
        row = jnp.where(live, row, -1)
        chooser = (iota((plan.rows, plan.slots), 0) == row).astype(F32)
        chooser_ref[...] = chooser.astype(BF16)
        if marked:
            marks = lax.dot_general(
                jnp.broadcast_to((local_row + 1).astype(F32), (8, plan.slots)),
                chooser,
                (((1,), (1,)), ((), ())),
                precision=HIGHEST,
                preferred_element_type=F32,
            )
            for out, held in zip(outs, [rows] * (len(outs) - 1) + [rows * plan.pairs]):
                out[fields * held : fields * held + 8, :] = jnp.zeros((8, plan.points), F32)
                out[fields * held : fields * held + 8, : plan.rows] = marks

    moved = pick(chooser_ref[...], states_ref[0])
    start = pl.multiple_of(field * rows, rows)
    aside = pl.multiple_of(field * rows * plan.pairs, rows)
    for b in range(plan.pairs):
        outs[b][pl.ds(start, rows), :] = moved[2 * b * rows : (2 * b + 1) * rows]
        outs[-1][pl.ds(aside + b * rows, rows), :] = moved[(2 * b + 1) * rows : (2 * b + 2) * rows]


def whole(shape):
    return pl.BlockSpec(shape, lambda *_: (0,) * len(shape))


def pack(plan, group, me, place_row, states, marked):
    first, fields = group
    extra = 8 if marked else 0
    shapes = [(fields * plan.msg_rows + extra, plan.points)] * plan.pairs
    shapes.append((fields * plan.msg_rows * plan.pairs + extra, plan.points))
    return pl.pallas_call(
        functools.partial(pack_kernel, plan, fields, marked),
        grid=(fields,),
        in_specs=[
            pl.BlockSpec(memory_space=pltpu.SMEM),
            whole((1, plan.slots)),
            pl.BlockSpec((1, plan.slots, plan.points), lambda f: (first + f, 0, 0)),
        ],
        out_specs=[pl.BlockSpec(memory_space=pltpu.VMEM)] * len(shapes),
        out_shape=[jax.ShapeDtypeStruct(shape, F32) for shape in shapes],
        scratch_shapes=[pltpu.VMEM((plan.rows, plan.slots), BF16)],
        compiler_params=PARAMS,
    )(me, place_row, states)


def merge_kernel(plan, fields, marked, flagged, *refs):
    near, refs = refs[: plan.pairs], refs[plan.pairs :]
    aside, outs = refs[0], refs[-plan.pairs :]
    rows = plan.msg_rows
    for b, out in enumerate(outs):
        for field in range(fields):
            start = field * plan.pair_rows
            other = (field * plan.pairs + b) * rows
            out[start : start + rows, :] = near[b][field * rows : (field + 1) * rows, :]
            out[start + rows : start + 2 * rows, :] = aside[other : other + rows, :]
        if marked:
            lane = iota((8, plan.rows), 1)
            mine = near[0][fields * rows : fields * rows + 8, : plan.rows]
            base = fields * rows * plan.pairs
            other = aside[base : base + 8, : plan.rows]
            marks = jnp.where(rest(halves(lane, rows), 2) == 0, mine, other)
            base = fields * plan.pair_rows
            out[base : base + 8, :] = jnp.zeros((8, plan.points), F32)
            out[base : base + 8, : plan.rows] = marks
        if flagged:
            base = fields * plan.pair_rows
            out[base : base + 8, :] = jnp.zeros((8, plan.points), F32)
            out[base : base + 8, : plan.rows] = refs[1][...]


def merge(plan, group, near, aside, marked, flags, cost):
    _, fields = group
    shape = (fields * plan.pair_rows + (8 if marked or flags else 0), plan.points)
    return simple_call(
        functools.partial(merge_kernel, plan, fields, marked, bool(flags)),
        [*near, aside, *flags],
        [jax.ShapeDtypeStruct(shape, F32)] * plan.pairs,
        [],
        cost,
    )


def route_rows(plan, marks):
    lane = iota((1, plan.rows), 1)
    step = rest(halves(lane, plan.cap), plan.lines)
    filled = marks[:1] > 0.0
    valid = (iota((plan.lines, plan.rows), 0) == step) & filled
    earlier = jnp.dot(valid.astype(BF16), before(plan.rows), preferred_element_type=F32)
    earlier = earlier.astype(jnp.int32)
    row = halves(lane, plan.msg_rows) * plan.cap + rest(lane, plan.cap)
    over = jnp.zeros((1, plan.rows), F32)
    for m in range(1, plan.lines):
        number = earlier[m : m + 1]
        row = jnp.where(step == m, number + m * plan.full, row)
        over = jnp.maximum(over, jnp.where((step == m) & filled & (number >= plan.kept[m]), 1.0, 0.0))
    return jnp.where(filled, row, -1), jnp.max(over, axis=1, keepdims=True)


def gather_marks(plan, fields, messages):
    lane = iota((8, plan.rows), 1)
    marks = jnp.zeros((8, plan.rows), F32)
    base = fields * plan.pair_rows
    for b, message in enumerate(messages):
        part = message[base : base + 8, : plan.rows]
        marks = jnp.where(halves(lane, plan.pair_rows) == b, part, marks)
    return marks


def put_tail(plan, out, value):
    base = out.shape[0] - 8
    out[base:, :] = jnp.zeros((8, plan.points), F32)
    out[base:, : plan.rows] = value


def relay_kernel(plan, fields, marked, flagged, *refs):
    messages, refs = refs[: plan.pairs], refs[plan.pairs :]
    if not marked:
        marks_ref, refs = refs[0], refs[1:]
    outs, refs = refs[: plan.lines - 1], refs[plan.lines - 1 :]
    late, refs = refs[: len(plan.spill)], refs[len(plan.spill) :]
    held = refs[-1]
    marks = gather_marks(plan, fields, messages) if marked else marks_ref[...]
    row, over = route_rows(plan, marks)
    spread = (iota((plan.rows, plan.rows), 0) == row).astype(F32)
    if marked:
        marks_out, own_out, flag_out = refs[:3]
        landed = lax.dot_general(
            marks, spread, (((1,), (1,)), ((), ())), precision=HIGHEST, preferred_element_type=F32
        )
        marks_out[...] = marks
        own_out[...] = landed
        flag_out[...] = jnp.broadcast_to(over, (8, plan.rows))
        for out in outs:
            put_tail(plan, out, landed)
    if flagged:
        flag = messages[0][fields * plan.pair_rows :, : plan.rows]
        for message in messages[1:]:
            flag = jnp.maximum(flag, message[fields * plan.pair_rows :, : plan.rows])
        refs[0][...] = flag
        for out in outs:
            put_tail(plan, out, flag)
    chooser = spread[plan.full :].astype(BF16)
    for field in range(fields):
        for b, message in enumerate(messages):
            held[b * plan.pair_rows : (b + 1) * plan.pair_rows, :] = message[
                field * plan.pair_rows : (field + 1) * plan.pair_rows, :
            ]
        moved = pick(chooser, held[...])
        for m, out in enumerate(outs, 1):
            at, kept = (m - 1) * plan.full, plan.kept[m]
            out[field * kept : (field + 1) * kept, :] = moved[at : at + kept]
        for m, out in zip(plan.spill, late):
            at, kept = (m - 1) * plan.full, plan.kept[m]
            left = plan.full - kept
            out[field * left : (field + 1) * left, :] = moved[at + kept : at + plan.full]


def relay(plan, group, messages, marks, flagged):
    _, fields = group
    marked = marks is None
    extra = 8 if marked or flagged else 0
    shapes = [(fields * kept + extra, plan.points) for kept in plan.kept[1:]]
    shapes += [(fields * (plan.full - plan.kept[m]), plan.points) for m in plan.spill]
    shapes += [(8, plan.rows)] * (3 if marked else 1 if flagged else 0)
    result = simple_call(
        functools.partial(relay_kernel, plan, fields, marked, flagged),
        list(messages) + ([] if marked else [marks]),
        [jax.ShapeDtypeStruct(shape, F32) for shape in shapes],
        [pltpu.VMEM((plan.rows, plan.points), F32)],
    )
    split = plan.lines - 1
    return result[:split], result[split : split + len(plan.spill)], result[split + len(plan.spill) :]


def element_chooser(plan, marks):
    element = iota((plan.per_dev, plan.rows), 0).astype(F32) + 1.0
    return (element == marks[:1]).astype(F32).astype(BF16)


def settle_kernel(plan, fields, marked, flagged, *refs):
    messages, refs = refs[: plan.pairs], refs[plan.pairs :]
    relays, refs = refs[: plan.lines - 1], refs[plan.lines - 1 :]
    if marked or flagged:
        tails, refs = refs[: plan.lines - 1], refs[plan.lines - 1 :]
    if marked:
        own_ref, order_ref, out, marks_out, cells_out, chooser_ref, held, pressure_ref = refs
    elif flagged:
        marks_ref, flag_ref, _, out, flag_out, chooser_ref, held = refs
    else:
        marks_ref, _, out, chooser_ref, held = refs
    field = pl.program_id(0)

    @pl.when(field == 0)
    def _():
        if marked:
            lane = iota((8, plan.rows), 1)
            marks = own_ref[...]
            for m in range(1, plan.lines):
                marks = jnp.where(halves(lane, plan.full) == m, tails[m - 1][:, : plan.rows], marks)
            marks_out[...] = marks
        else:
            marks = marks_ref[...]
        if flagged:
            flag = flag_ref[...]
            for tail in tails:
                flag = jnp.maximum(flag, tail[:, : plan.rows])
            flag_out[...] = flag
        chooser_ref[...] = element_chooser(plan, marks)
        for m in plan.spill:
            start = m * plan.full + plan.kept[m]
            held[start : (m + 1) * plan.full, :] = jnp.zeros((plan.full - plan.kept[m], plan.points), F32)

    for j in range(plan.plane):
        start = j % 2 * plan.msg_rows
        held[j * plan.cap : (j + 1) * plan.cap, :] = messages[j // 2][start : start + plan.cap, :]
    for m, part in enumerate(relays, 1):
        held[m * plan.full : m * plan.full + plan.kept[m], :] = part[...]
    placed = pick(chooser_ref[...], held[...])
    out[...] = placed.reshape(out.shape)

    if marked:

        @pl.when(field == 0)
        def _():
            pressure_ref[...] = 3.0 * placed

        @pl.when(field == 1)
        def _():
            pressure_ref[...] = pressure_ref[...] - 3.0 * placed

        @pl.when(field == 2)
        def _():
            cells_out[...] = pick(order_ref[...], pressure_ref[...] + placed, ((1,), (1,)))


def cell_order(side):
    rows = []
    for k in range(side):
        rows += [(i * side + j) * side + k for i in range(side) for j in range(side)]
        rows += [(i * side + side - 1) * side + k for i in range(side)]
        rows += [(i * side) * side + k for i in range(side)]
    order = np.zeros((len(rows), side**3), np.float32)
    order[np.arange(len(rows)), rows] = 1.0
    return order


def states_block(plan, first):
    columns = BX * BS
    block = pl.BlockSpec((columns, 1, plan.layers, plan.points), lambda f: (0, first + f, 0, 0))
    return block, jax.ShapeDtypeStruct((columns, plan.fields, plan.layers, plan.points), F32)


def settle(plan, group, messages, relays, marks, buffer, own, order, flag):
    first, fields = group
    marked, flagged = marks is None, flag is not None
    in_vmem = pl.BlockSpec(memory_space=pltpu.VMEM)
    block, states = states_block(plan, first)
    out_specs, out_shape = [block], [states]
    scratch = [pltpu.VMEM((plan.per_dev, plan.rows), BF16), pltpu.VMEM((plan.rows, plan.points), F32)]
    operands = list(messages) + list(relays)
    in_specs = [pl.BlockSpec((plan.pair_rows, plan.points), lambda f: (f, 0))] * plan.pairs
    in_specs += [pl.BlockSpec((kept, plan.points), lambda f: (f, 0)) for kept in plan.kept[1:]]
    if marked or flagged:
        operands += list(relays)
        in_specs += [
            pl.BlockSpec((8, plan.points), lambda f, at=fields * kept // 8: (at, 0)) for kept in plan.kept[1:]
        ]
    known = [own, order] if marked else [marks, flag] if flagged else [marks]
    operands += known
    in_specs += [in_vmem] * len(known)
    aliases = {}
    row = jax.ShapeDtypeStruct((8, plan.rows), F32)
    if marked:
        out_shape += [row, jax.ShapeDtypeStruct((order.shape[0], plan.per_dev), F32)]
        out_specs += [in_vmem] * 2
        scratch += [pltpu.VMEM((plan.per_dev, plan.points), F32)]
    else:
        aliases = {len(operands): 0}
        operands += [buffer]
        in_specs += [pl.BlockSpec(memory_space=pl.ANY)]
        if flagged:
            out_shape += [row]
            out_specs += [in_vmem]
    return pl.pallas_call(
        functools.partial(settle_kernel, plan, fields, marked, flagged),
        grid=(fields,),
        in_specs=in_specs,
        out_specs=out_specs,
        out_shape=out_shape,
        scratch_shapes=scratch,
        input_output_aliases=aliases,
        compiler_params=PARAMS,
    )(*operands)


def add_late_kernel(plan, *refs):
    parts, (marks_ref, states_ref, out, held) = refs[: len(plan.spill)], refs[len(plan.spill) :]
    held[...] = jnp.zeros(held.shape, F32)
    for m, part in zip(plan.spill, parts):
        held[m * plan.full + plan.kept[m] : (m + 1) * plan.full, :] = part[...]
    placed = pick(element_chooser(plan, marks_ref[...]), held[...])
    out[...] = states_ref[...] + placed.reshape(out.shape)


def add_late(plan, group, parts, marks, buffer):
    first, fields = group
    block, states = states_block(plan, first)
    return pl.pallas_call(
        functools.partial(add_late_kernel, plan),
        grid=(fields,),
        in_specs=[pl.BlockSpec((plan.full - plan.kept[m], plan.points), lambda f: (f, 0)) for m in plan.spill]
        + [pl.BlockSpec(memory_space=pltpu.VMEM), block],
        out_specs=block,
        out_shape=states,
        scratch_shapes=[pltpu.VMEM((plan.rows, plan.points), F32)],
        input_output_aliases={len(parts) + 1: 0},
        compiler_params=PARAMS,
    )(*parts, marks, buffer)


def cells_kernel(plan, states_ref, order_ref, out):
    held = states_ref[...]
    pressure = 3.0 * held[:, 0] - 3.0 * held[:, 1] + held[:, 2]
    out[...] = pick(order_ref[...], pressure.reshape(plan.per_dev, plan.points), ((1,), (1,)))


def cells_of(plan, buffer, order):
    return pl.pallas_call(
        functools.partial(cells_kernel, plan),
        grid=(1,),
        in_specs=[
            pl.BlockSpec((BX * BS, 3, plan.layers, plan.points), lambda f: (0, 0, 0, 0)),
            whole(order.shape),
        ],
        out_specs=whole((order.shape[0], plan.per_dev)),
        out_shape=jax.ShapeDtypeStruct((order.shape[0], plan.per_dev), F32),
        compiler_params=PARAMS,
    )(buffer, order)


def lane_steps(plan):
    lane = iota((FACE, plan.per_dev), 1)
    layer = rest(lane, plan.layers)
    row_s = rest(halves(lane, plan.layers), BS)
    row_x = halves(lane, plan.layers * BS)
    return layer, row_s, row_x


def roll(value, steps):
    return pltpu.roll(value, steps % value.shape[1], 1)


def solve_kernel(plan, cells, from_xlow, from_xup, from_slow, from_sup, *refs):
    tables, refs = refs[:10], refs[10:]
    total, out_xlow, out_xup, out_slow, out_sup, box, section, modal, weights, values_w, sums = refs
    vectors_x, vectors_s, vectors_w, own_x, own_s, own_w, pick_x, pick_s, spread_x, spread_s = tables
    side, extent = plan.side, plan.extent
    layer, row_s, row_x = lane_steps(plan)
    points = side * side
    stride = points + 2 * FACE
    width = plan.layers
    wide = width * BS
    box_rows = points + 4 * FACE

    def cell(k, start):
        return cells[k * stride + start : k * stride + start + FACE, :]

    def piece(ref, k):
        return ref[k * FACE : (k + 1) * FACE, :]

    for k in range(side):
        w = k + 1
        for i in range(side):
            box[w * box_rows + i * FACE : w * box_rows + (i + 1) * FACE, :] = cell(k, i * FACE)
        at = w * box_rows + points
        low = jnp.where(row_x == 0, roll(piece(from_xlow, k), wide), roll(cell(k, points - FACE), wide))
        up = jnp.where(row_x == BX - 1, roll(piece(from_xup, k), -wide), roll(cell(k, 0), -wide))
        box[at : at + FACE, :] = low
        box[at + FACE : at + 2 * FACE, :] = up
        top, bottom = cell(k, points), cell(k, points + FACE)
        back = (BS - 1) * width
        low = jnp.where(row_s == 0, roll(piece(from_slow, k), -back), roll(top, width))
        up = jnp.where(row_s == BS - 1, roll(piece(from_sup, k), back), roll(bottom, -width))
        box[at + 2 * FACE : at + 3 * FACE, :] = low
        box[at + 3 * FACE : at + 4 * FACE, :] = up
    last = (extent - 1) * box_rows
    for i in range(side):
        below = jnp.where(layer == 0, 0.0, roll(cell(side - 1, i * FACE), 1))
        above = jnp.where(layer == width - 1, 0.0, roll(cell(0, i * FACE), -1))
        box[i * FACE : (i + 1) * FACE, :] = below
        box[last + i * FACE : last + (i + 1) * FACE, :] = above

    def exact(left, right, contract=((1,), (0,))):
        dims = (contract, ((), ()))
        return lax.dot_general(left, right, dims, precision=HIGHEST, preferred_element_type=F32)

    mix_t = exact(exact(pick_x[...], vectors_x[...]), spread_x[...], ((1,), (1,)))
    mix_t = mix_t * exact(exact(pick_s[...], vectors_s[...]), spread_s[...], ((1,), (1,)))
    modal_rows = spread_x.shape[0]
    lanes = plan.per_dev
    held_by = (iota((width, lanes), 0) == rest(iota((width, lanes), 1), width)).astype(F32)
    for w in range(extent):
        weights[w] = exact(vectors_w[w], held_by, ((0,), (0,)))
    values_w[...] = exact(own_w[...], held_by, ((0,), (0,)))
    sum_xs = jnp.sum(spread_x[...] * own_x[...] + spread_s[...] * own_s[...], axis=1, keepdims=True)
    sum_xs = jnp.where(iota(sum_xs.shape, 0) < extent * extent, sum_xs, 1.0)
    for w in range(extent):
        rows = points if w in (0, extent - 1) else box_rows
        section[w] = exact(mix_t[:rows], box[w * box_rows : w * box_rows + rows, :], ((0,), (0,)))
    sums[...] = jnp.broadcast_to(sum_xs, sums.shape)

    @pl.loop(0, modal_rows // FACE)
    def _(block):
        part = pl.ds(pl.multiple_of(block * FACE, FACE), FACE)
        held = [section[w, part, :] for w in range(extent)]
        out = [None] * extent
        base = sums[part, :]
        for k in range(extent):
            value = None
            for w in range(extent):
                term = weights[w, k : k + 1, :] * held[w]
                value = term if value is None else value + term
            value = value / (base + values_w[k : k + 1, :])
            for w in range(extent):
                term = weights[w, k : k + 1, :] * value
                out[w] = term if out[w] is None else out[w] + term
        for w in range(extent):
            modal[w, part, :] = out[w]

    for w in range(extent):
        rows = points if w in (0, extent - 1) else box_rows
        box[w * box_rows : w * box_rows + rows, :] = exact(mix_t[:rows], modal[w])

    for k in range(side):
        at = (k + 1) * box_rows
        total[k * points : (k + 1) * points, :] = box[at : at + points, :]
        for out, shift in ((out_xlow, 0), (out_xup, 1), (out_slow, 2), (out_sup, 3)):
            start = at + points + shift * FACE
            out[k * FACE : (k + 1) * FACE, :] = box[start : start + FACE, :]
    for i in range(side):
        below = jnp.where(layer == width - 1, 0.0, roll(box[i * FACE : (i + 1) * FACE, :], -1))
        above = jnp.where(layer == 0, 0.0, roll(box[last + i * FACE : last + (i + 1) * FACE, :], 1))
        top = (side - 1) * points + i * FACE
        total[top : top + FACE, :] += below
        total[i * FACE : (i + 1) * FACE, :] += above


def finish_kernel(plan, total, xlow, xup, slow, sup, from_x_up, from_x_low, from_s_up, from_s_low, out, held):
    side = plan.side
    points = side * side
    layer, row_s, row_x = lane_steps(plan)
    width = plan.layers
    wide = width * BS
    back = (BS - 1) * width
    sub = iota((FACE, plan.per_dev), 0)
    for k in range(side):
        part = slice(k * FACE, (k + 1) * FACE)
        rows = [total[k * points + i * FACE : k * points + (i + 1) * FACE, :] for i in range(side)]
        rows[side - 1] = rows[side - 1] + jnp.where(
            row_x == BX - 1, roll(from_x_up[part, :], -wide), roll(xlow[part, :], -wide)
        )
        rows[0] = rows[0] + jnp.where(row_x == 0, roll(from_x_low[part, :], wide), roll(xup[part, :], wide))
        to_last = jnp.where(row_s == BS - 1, roll(from_s_up[part, :], back), roll(slow[part, :], -width))
        to_first = jnp.where(row_s == 0, roll(from_s_low[part, :], -back), roll(sup[part, :], width))
        for i in range(side):
            last = jnp.broadcast_to(to_last[i : i + 1, :], sub.shape)
            first = jnp.broadcast_to(to_first[i : i + 1, :], sub.shape)
            value = rows[i] + jnp.where(sub == side - 1, last, 0.0) + jnp.where(sub == 0, first, 0.0)
            held[k * points + i * FACE : k * points + (i + 1) * FACE, :] = value
    lanes = plan.layers * side
    source = iota((plan.per_dev, lanes), 0)
    lane = iota((plan.per_dev, lanes), 1)
    terms = three_terms(held[...])
    kept = rest(iota((points, lanes), 1), side)
    for column in range(BX * BS):
        chooser = (source == halves(lane, side) + column * plan.layers).astype(F32).astype(BF16)
        high, middle, low = [jnp.dot(t, chooser, preferred_element_type=F32) for t in terms]
        spread = (high + middle) + low
        value = jnp.zeros((points, lanes), F32)
        for k in range(side):
            value = jnp.where(kept == k, spread[k * points : (k + 1) * points], value)
        b, s = column // BS, column % BS
        for i in range(side):
            out[b * side + i, s * side : (s + 1) * side, :] = value[i * side : (i + 1) * side]


def simple_call(kernel, operands, out_shape, scratch, cost=None):
    return pl.pallas_call(
        kernel,
        in_specs=[pl.BlockSpec(memory_space=pltpu.VMEM)] * len(operands),
        out_specs=[pl.BlockSpec(memory_space=pltpu.VMEM)] * len(out_shape),
        out_shape=out_shape,
        scratch_shapes=scratch,
        compiler_params=PARAMS,
        cost_estimate=cost,
    )(*operands)


def box_rows_of(extent):
    inside = range(1, extent - 1)
    points = [(u, v) for u in inside for v in inside]
    points += [(u, v) for u in (0, extent - 1) for v in inside]
    points += [(u, v) for v in (0, extent - 1) for u in inside]
    modes = [(i, j) for i in range(extent) for j in range(extent)]
    modal_rows = -(-len(modes) // FACE) * FACE

    def hot(rows, values):
        table = np.zeros((rows, extent), np.float32)
        table[np.arange(len(values)), values] = 1.0
        return jnp.asarray(table)

    us, vs = zip(*points)
    i_s, j_s = zip(*modes)
    return hot(len(us), us), hot(len(vs), vs), hot(modal_rows, i_s), hot(modal_rows, j_s)


def after(value, earlier):
    return lax.optimization_barrier((value, earlier))[0]


def shards(old_states, new_place, vectors_x, vectors_s, vectors_w, values_x, values_s, values_w):
    n_x, n_y = lax.axis_size("gx"), lax.axis_size("gy")
    slots, fields, points = old_states.shape
    plan = Plan(n_x, n_y, slots, fields, points, vectors_w.shape[0], vectors_x.shape[0])
    place = lax.axis_index("gx") * n_y + lax.axis_index("gy")
    me = place.astype(jnp.int32).reshape(1)
    states = jnp.transpose(old_states, (1, 0, 2))
    place_row = new_place.reshape(1, slots)
    both = ("gx", "gy")

    def across(value, flip):
        return lax.ppermute(value, both, [(d, d ^ flip) for d in range(plan.devices)])

    def shifted(value, axis, steps):
        count = lax.axis_size(axis)
        return lax.ppermute(value, axis, [(s, (s + steps) % count) for s in range(count)])

    order = jnp.asarray(cell_order(plan.side), BF16)
    tables = [vectors_x, vectors_s, jnp.transpose(vectors_w, (1, 0, 2))]
    tables += [values_x.reshape(1, -1), values_s.reshape(1, -1), values_w, *box_rows_of(plan.extent)]

    side = plan.side
    inner = side * side

    def faces(cells):
        layered = cells.reshape(side, inner + 2 * FACE, plan.per_dev)

        def rows(start):
            return layered[:, start : start + FACE].reshape(side * FACE, plan.per_dev)

        ends = [rows(inner - FACE), rows(0)]
        side_faces = [shifted(rows(inner), "gy", 1), shifted(rows(inner + FACE), "gy", -1)]
        return [shifted(ends[0], "gx", 1), shifted(ends[1], "gx", -1)] + side_faces

    def solve(cells, halo):
        face = jax.ShapeDtypeStruct((side * FACE, plan.per_dev), F32)
        sections = (plan.extent, tables[-1].shape[0], plan.per_dev)
        total, xlow, xup, slow, sup = simple_call(
            functools.partial(solve_kernel, plan),
            [cells, *halo, *tables],
            [jax.ShapeDtypeStruct((side * inner, plan.per_dev), F32)] + [face] * 4,
            [pltpu.VMEM((plan.extent * (inner + 4 * FACE), plan.per_dev), F32)]
            + [pltpu.VMEM(sections, F32)] * 2
            + [pltpu.VMEM((plan.extent, plan.extent, plan.per_dev), F32)]
            + [pltpu.VMEM((plan.extent, plan.per_dev), F32), pltpu.VMEM(sections[1:], F32)],
        )
        returned = [shifted(xlow, "gx", -1), shifted(xup, "gx", 1), shifted(slow, "gy", -1), shifted(sup, "gy", 1)]
        (correction,) = simple_call(
            functools.partial(finish_kernel, plan),
            [total, xlow, xup, slow, sup, *returned],
            [jax.ShapeDtypeStruct((BX * side, BS * side, plan.layers * side), F32)],
            [pltpu.VMEM((side * inner, plan.per_dev), F32)],
        )
        return correction

    packed = []
    for g, group in enumerate(plan.groups):
        *near, aside = pack(plan, group, me, place_row, states, g == 0)
        packed.append((near, across(aside, 1)))

    marks = gate = waiting = None
    flags, held, late = [], [], []
    last = len(plan.groups) - 1
    for g, (group, (near, aside)) in enumerate(zip(plan.groups, packed)):
        first, flagged = g == 0, g == 1
        if not first:
            near[0] = after(near[0], gate)
        cost = pl.CostEstimate(flops=0 if first else MERGE_FLOPS, bytes_accessed=0, transcendentals=0)
        sent = merge(plan, group, near, aside, first, flags if flagged else [], cost)
        messages = [sent[0]] + [across(sent[b], 2 * b) for b in range(1, plan.pairs)]
        if not first:
            before_it = held[-1][1]
            messages[0] = after(messages[0], before_it[1:])
            if flagged:
                before_it[0] = across(after(waiting, messages[1]), plan.plane)
        if g == last:
            buffer, row_marks, cells = settle(plan, plan.groups[0], *held[0], None, None, own, order, None)
            messages[0] = after(messages[0], cells)
            halo = faces(cells)
        relays, rows_left, more = relay(plan, group, messages, marks, flagged)
        late.append(rows_left)
        if first:
            marks, own, over = more
            flags = [over]
        if flagged:
            (flag,) = more
        gate = waiting = relays[0]
        ready = list(relays)
        if g == last:
            ready[1:] = [after(r, halo[:2]) for r in ready[1:]]
            waiting = after(waiting, halo[:2])
        if not first:
            ready[1:] = [after(r, held[-1][1][1:]) for r in ready[1:]]
        arrived = [None]
        for m in range(2, plan.lines):
            value = ready[m - 1]
            if m > 2 and g != last:
                value = after(value, arrived[-1])
            if m > 2 and first:
                value = after(value, packed[-1][1])
            arrived.append(across(value, m * plan.plane))
        if not first:
            arrived[0] = across(after(waiting, [messages[1], held[-1][1][0]]), plan.plane)
        held.append((messages, arrived))

    buffer, flag = settle(plan, plan.groups[1], *held[1], row_marks, buffer, None, None, flag)
    flag = jnp.maximum(flag[:1, :1], across(flag, 1)[:1, :1])
    correction = solve(cells, halo)
    (buffer,) = settle(plan, plan.groups[last], *held[last], row_marks, buffer, None, None, None)

    def send_rest(buffer, correction, late):
        for group, parts in zip(plan.groups, late):
            parts = [across(part, m * plan.plane) for m, part in zip(plan.spill, parts)]
            buffer = add_late(plan, group, parts, row_marks, buffer)
        cells = cells_of(plan, buffer, order)
        return buffer, solve(cells, faces(cells))

    def keep(buffer, correction, late):
        return buffer, correction

    if plan.spill:
        buffer, correction = lax.cond(flag[0, 0] > 0.0, send_rest, keep, buffer, correction, late)
    new_states = buffer.reshape(BX, BS, fields, plan.layers, points).transpose(0, 1, 3, 2, 4)
    return new_states, correction


def solution(mesh):
    placed = (P(("gx", "gy"), None, None), P(("gx", "gy")), P(), P(), P(), P(), P(), P())
    return jax.shard_map(
        shards,
        mesh=mesh,
        in_specs=placed,
        out_specs=(P("gx", "gy", None, None, None), P("gx", "gy", None)),
        check_vma=False,
    )
```

```python
import functools

import jax
import jax.numpy as jnp
import numpy as np
from jax import lax
from jax.experimental import pallas as pl
from jax.experimental.pallas import tpu as pltpu
from jax.sharding import PartitionSpec as P

BX = 4
BS = 2
FACE = 8
MERGE_FLOPS = 40_000_000_000
VMEM_LIMIT = 12 * 1024 * 1024
PARAMS = pltpu.CompilerParams(vmem_limit_bytes=VMEM_LIMIT)
HIGHEST = lax.Precision.HIGHEST
F32 = jnp.float32
BF16 = jnp.bfloat16


class Plan:
    def __init__(self, n_x, n_y, slots, fields, points, layers, extent):
        self.n_x, self.n_y = n_x, n_y
        self.devices = n_x * n_y
        self.lines = n_x // 2
        self.plane = self.devices // self.lines
        self.slots, self.fields, self.points = slots, fields, points
        self.layers, self.extent, self.side = layers, extent, extent - 2
        self.per_dev = BX * BS * layers
        self.cap = 2 * self.per_dev // self.devices
        self.msg_rows = self.lines * self.cap
        self.pairs = self.plane // 2
        self.pair_rows = 2 * self.msg_rows
        self.rows = self.plane * self.msg_rows
        self.full = self.plane * self.cap
        self.kept = [self.full] * 2 + [self.full * 3 // 4] * (self.lines - 2)
        self.spill = [m for m in range(self.lines) if self.kept[m] < self.full]
        second = (fields - 3) * 4 // 9
        self.groups = [(0, 3), (3, second), (3 + second, fields - 3 - second)]


def halves(value, count):
    if count & (count - 1) == 0:
        return lax.shift_right_logical(value, int(count).bit_length() - 1)
    return value // count


def rest(value, count):
    if count & (count - 1) == 0:
        return value & (count - 1)
    return value % count


def three_terms(value):
    high = value.astype(BF16)
    left = value - high.astype(F32)
    middle = left.astype(BF16)
    low = (left - middle.astype(F32)).astype(BF16)
    return high, middle, low


def pick(chooser, value, contract=((1,), (0,))):
    high, middle, low = three_terms(value)
    dims = (contract, ((), ()))
    product = functools.partial(lax.dot_general, dimension_numbers=dims, preferred_element_type=F32)
    return (product(chooser, high) + product(chooser, middle)) + product(chooser, low)


def iota(shape, dim):
    return lax.broadcasted_iota(jnp.int32, shape, dim)


def before(count):
    return (iota((count, count), 0) < iota((count, count), 1)).astype(BF16)


def pack_kernel(plan, fields, marked, me_ref, place_ref, states_ref, *refs):
    outs, chooser_ref = refs[:-1], refs[-1]
    field = pl.program_id(0)
    rows = plan.msg_rows

    @pl.when(field == 0)
    def _():
        me = me_ref[0]
        new_place = place_ref[...]
        live = new_place >= 0
        placed = jnp.maximum(new_place, 0)
        column = halves(placed, plan.layers)
        layer_pos = rest(placed, plan.layers)
        span = BS * plan.n_y
        elem_x = halves(column, span)
        elem_s = rest(column, span)
        target = halves(elem_x, BX) * plan.n_y + halves(elem_s, BS)
        local_row = (rest(elem_x, BX) * BS + rest(elem_s, BS)) * plan.layers + layer_pos
        target = jnp.where(live, target, -1)
        hot = iota((plan.devices, plan.slots), 0) == target
        earlier = jnp.dot(hot.astype(BF16), before(plan.slots), preferred_element_type=F32)
        rank = jnp.sum(jnp.where(hot, earlier, 0.0), axis=0, keepdims=True).astype(jnp.int32)
        across = target ^ me
        row = rest(across, plan.plane) * rows + halves(across, plan.plane) * plan.cap + rank
        row = jnp.where(live, row, -1)
        chooser = (iota((plan.rows, plan.slots), 0) == row).astype(F32)
        chooser_ref[...] = chooser.astype(BF16)
        if marked:
            marks = lax.dot_general(
                jnp.broadcast_to((local_row + 1).astype(F32), (8, plan.slots)),
                chooser,
                (((1,), (1,)), ((), ())),
                precision=HIGHEST,
                preferred_element_type=F32,
            )
            for out, held in zip(outs, [rows] * (len(outs) - 1) + [rows * plan.pairs]):
                out[fields * held : fields * held + 8, :] = jnp.zeros((8, plan.points), F32)
                out[fields * held : fields * held + 8, : plan.rows] = marks

    moved = pick(chooser_ref[...], states_ref[0])
    start = pl.multiple_of(field * rows, rows)
    aside = pl.multiple_of(field * rows * plan.pairs, rows)
    for b in range(plan.pairs):
        outs[b][pl.ds(start, rows), :] = moved[2 * b * rows : (2 * b + 1) * rows]
        outs[-1][pl.ds(aside + b * rows, rows), :] = moved[(2 * b + 1) * rows : (2 * b + 2) * rows]


def whole(shape):
    return pl.BlockSpec(shape, lambda *_: (0,) * len(shape))


def pack(plan, group, me, place_row, states, marked):
    first, fields = group
    extra = 8 if marked else 0
    shapes = [(fields * plan.msg_rows + extra, plan.points)] * plan.pairs
    shapes.append((fields * plan.msg_rows * plan.pairs + extra, plan.points))
    return pl.pallas_call(
        functools.partial(pack_kernel, plan, fields, marked),
        grid=(fields,),
        in_specs=[
            pl.BlockSpec(memory_space=pltpu.SMEM),
            whole((1, plan.slots)),
            pl.BlockSpec((1, plan.slots, plan.points), lambda f: (first + f, 0, 0)),
        ],
        out_specs=[pl.BlockSpec(memory_space=pltpu.VMEM)] * len(shapes),
        out_shape=[jax.ShapeDtypeStruct(shape, F32) for shape in shapes],
        scratch_shapes=[pltpu.VMEM((plan.rows, plan.slots), BF16)],
        compiler_params=PARAMS,
    )(me, place_row, states)


def merge_kernel(plan, fields, marked, flagged, *refs):
    near, refs = refs[: plan.pairs], refs[plan.pairs :]
    aside, outs = refs[0], refs[-plan.pairs :]
    rows = plan.msg_rows
    for b, out in enumerate(outs):
        for field in range(fields):
            start = field * plan.pair_rows
            other = (field * plan.pairs + b) * rows
            out[start : start + rows, :] = near[b][field * rows : (field + 1) * rows, :]
            out[start + rows : start + 2 * rows, :] = aside[other : other + rows, :]
        if marked:
            lane = iota((8, plan.rows), 1)
            mine = near[0][fields * rows : fields * rows + 8, : plan.rows]
            base = fields * rows * plan.pairs
            other = aside[base : base + 8, : plan.rows]
            marks = jnp.where(rest(halves(lane, rows), 2) == 0, mine, other)
            base = fields * plan.pair_rows
            out[base : base + 8, :] = jnp.zeros((8, plan.points), F32)
            out[base : base + 8, : plan.rows] = marks
        if flagged:
            base = fields * plan.pair_rows
            out[base : base + 8, :] = jnp.zeros((8, plan.points), F32)
            out[base : base + 8, : plan.rows] = refs[1][...]


def merge(plan, group, near, aside, marked, flags, cost):
    _, fields = group
    shape = (fields * plan.pair_rows + (8 if marked or flags else 0), plan.points)
    return simple_call(
        functools.partial(merge_kernel, plan, fields, marked, bool(flags)),
        [*near, aside, *flags],
        [jax.ShapeDtypeStruct(shape, F32)] * plan.pairs,
        [],
        cost,
    )


def route_rows(plan, marks):
    lane = iota((1, plan.rows), 1)
    step = rest(halves(lane, plan.cap), plan.lines)
    filled = marks[:1] > 0.0
    valid = (iota((plan.lines, plan.rows), 0) == step) & filled
    earlier = jnp.dot(valid.astype(BF16), before(plan.rows), preferred_element_type=F32)
    earlier = earlier.astype(jnp.int32)
    row = halves(lane, plan.msg_rows) * plan.cap + rest(lane, plan.cap)
    over = jnp.zeros((1, plan.rows), F32)
    for m in range(1, plan.lines):
        number = earlier[m : m + 1]
        row = jnp.where(step == m, number + m * plan.full, row)
        over = jnp.maximum(over, jnp.where((step == m) & filled & (number >= plan.kept[m]), 1.0, 0.0))
    return jnp.where(filled, row, -1), jnp.max(over, axis=1, keepdims=True)


def gather_marks(plan, fields, messages):
    lane = iota((8, plan.rows), 1)
    marks = jnp.zeros((8, plan.rows), F32)
    base = fields * plan.pair_rows
    for b, message in enumerate(messages):
        part = message[base : base + 8, : plan.rows]
        marks = jnp.where(halves(lane, plan.pair_rows) == b, part, marks)
    return marks


def put_tail(plan, out, value):
    base = out.shape[0] - 8
    out[base:, :] = jnp.zeros((8, plan.points), F32)
    out[base:, : plan.rows] = value


def relay_kernel(plan, fields, marked, flagged, *refs):
    messages, refs = refs[: plan.pairs], refs[plan.pairs :]
    if not marked:
        marks_ref, refs = refs[0], refs[1:]
    outs, refs = refs[: plan.lines - 1], refs[plan.lines - 1 :]
    late, refs = refs[: len(plan.spill)], refs[len(plan.spill) :]
    held = refs[-1]
    marks = gather_marks(plan, fields, messages) if marked else marks_ref[...]
    row, over = route_rows(plan, marks)
    spread = (iota((plan.rows, plan.rows), 0) == row).astype(F32)
    if marked:
        marks_out, own_out, flag_out = refs[:3]
        landed = lax.dot_general(
            marks, spread, (((1,), (1,)), ((), ())), precision=HIGHEST, preferred_element_type=F32
        )
        marks_out[...] = marks
        own_out[...] = landed
        flag_out[...] = jnp.broadcast_to(over, (8, plan.rows))
        for out in outs:
            put_tail(plan, out, landed)
    if flagged:
        flag = messages[0][fields * plan.pair_rows :, : plan.rows]
        for message in messages[1:]:
            flag = jnp.maximum(flag, message[fields * plan.pair_rows :, : plan.rows])
        refs[0][...] = flag
        for out in outs:
            put_tail(plan, out, flag)
    chooser = spread[plan.full :].astype(BF16)
    for field in range(fields):
        for b, message in enumerate(messages):
            held[b * plan.pair_rows : (b + 1) * plan.pair_rows, :] = message[
                field * plan.pair_rows : (field + 1) * plan.pair_rows, :
            ]
        moved = pick(chooser, held[...])
        for m, out in enumerate(outs, 1):
            at, kept = (m - 1) * plan.full, plan.kept[m]
            out[field * kept : (field + 1) * kept, :] = moved[at : at + kept]
        for m, out in zip(plan.spill, late):
            at, kept = (m - 1) * plan.full, plan.kept[m]
            left = plan.full - kept
            out[field * left : (field + 1) * left, :] = moved[at + kept : at + plan.full]


def relay(plan, group, messages, marks, flagged):
    _, fields = group
    marked = marks is None
    extra = 8 if marked or flagged else 0
    shapes = [(fields * kept + extra, plan.points) for kept in plan.kept[1:]]
    shapes += [(fields * (plan.full - plan.kept[m]), plan.points) for m in plan.spill]
    shapes += [(8, plan.rows)] * (3 if marked else 1 if flagged else 0)
    result = simple_call(
        functools.partial(relay_kernel, plan, fields, marked, flagged),
        list(messages) + ([] if marked else [marks]),
        [jax.ShapeDtypeStruct(shape, F32) for shape in shapes],
        [pltpu.VMEM((plan.rows, plan.points), F32)],
    )
    split = plan.lines - 1
    return result[:split], result[split : split + len(plan.spill)], result[split + len(plan.spill) :]


def element_chooser(plan, marks):
    element = iota((plan.per_dev, plan.rows), 0).astype(F32) + 1.0
    return (element == marks[:1]).astype(F32).astype(BF16)


def settle_kernel(plan, fields, marked, flagged, *refs):
    messages, refs = refs[: plan.pairs], refs[plan.pairs :]
    relays, refs = refs[: plan.lines - 1], refs[plan.lines - 1 :]
    if marked or flagged:
        tails, refs = refs[: plan.lines - 1], refs[plan.lines - 1 :]
    if marked:
        own_ref, order_ref, out, marks_out, cells_out, chooser_ref, held, pressure_ref = refs
    elif flagged:
        marks_ref, flag_ref, _, out, flag_out, chooser_ref, held = refs
    else:
        marks_ref, _, out, chooser_ref, held = refs
    field = pl.program_id(0)

    @pl.when(field == 0)
    def _():
        if marked:
            lane = iota((8, plan.rows), 1)
            marks = own_ref[...]
            for m in range(1, plan.lines):
                marks = jnp.where(halves(lane, plan.full) == m, tails[m - 1][:, : plan.rows], marks)
            marks_out[...] = marks
        else:
            marks = marks_ref[...]
        if flagged:
            flag = flag_ref[...]
            for tail in tails:
                flag = jnp.maximum(flag, tail[:, : plan.rows])
            flag_out[...] = flag
        chooser_ref[...] = element_chooser(plan, marks)
        for m in plan.spill:
            start = m * plan.full + plan.kept[m]
            held[start : (m + 1) * plan.full, :] = jnp.zeros((plan.full - plan.kept[m], plan.points), F32)

    for j in range(plan.plane):
        start = j % 2 * plan.msg_rows
        held[j * plan.cap : (j + 1) * plan.cap, :] = messages[j // 2][start : start + plan.cap, :]
    for m, part in enumerate(relays, 1):
        held[m * plan.full : m * plan.full + plan.kept[m], :] = part[...]
    placed = pick(chooser_ref[...], held[...])
    out[...] = placed.reshape(out.shape)

    if marked:

        @pl.when(field == 0)
        def _():
            pressure_ref[...] = 3.0 * placed

        @pl.when(field == 1)
        def _():
            pressure_ref[...] = pressure_ref[...] - 3.0 * placed

        @pl.when(field == 2)
        def _():
            cells_out[...] = pick(order_ref[...], pressure_ref[...] + placed, ((1,), (1,)))


def cell_order(side):
    rows = []
    for k in range(side):
        rows += [(i * side + j) * side + k for i in range(side) for j in range(side)]
        rows += [(i * side + side - 1) * side + k for i in range(side)]
        rows += [(i * side) * side + k for i in range(side)]
    order = np.zeros((len(rows), side**3), np.float32)
    order[np.arange(len(rows)), rows] = 1.0
    return order


def states_block(plan, first):
    columns = BX * BS
    block = pl.BlockSpec((columns, 1, plan.layers, plan.points), lambda f: (0, first + f, 0, 0))
    return block, jax.ShapeDtypeStruct((columns, plan.fields, plan.layers, plan.points), F32)


def settle(plan, group, messages, relays, marks, buffer, own, order, flag):
    first, fields = group
    marked, flagged = marks is None, flag is not None
    in_vmem = pl.BlockSpec(memory_space=pltpu.VMEM)
    block, states = states_block(plan, first)
    out_specs, out_shape = [block], [states]
    scratch = [pltpu.VMEM((plan.per_dev, plan.rows), BF16), pltpu.VMEM((plan.rows, plan.points), F32)]
    operands = list(messages) + list(relays)
    in_specs = [pl.BlockSpec((plan.pair_rows, plan.points), lambda f: (f, 0))] * plan.pairs
    in_specs += [pl.BlockSpec((kept, plan.points), lambda f: (f, 0)) for kept in plan.kept[1:]]
    if marked or flagged:
        operands += list(relays)
        in_specs += [
            pl.BlockSpec((8, plan.points), lambda f, at=fields * kept // 8: (at, 0)) for kept in plan.kept[1:]
        ]
    known = [own, order] if marked else [marks, flag] if flagged else [marks]
    operands += known
    in_specs += [in_vmem] * len(known)
    aliases = {}
    row = jax.ShapeDtypeStruct((8, plan.rows), F32)
    if marked:
        out_shape += [row, jax.ShapeDtypeStruct((order.shape[0], plan.per_dev), F32)]
        out_specs += [in_vmem] * 2
        scratch += [pltpu.VMEM((plan.per_dev, plan.points), F32)]
    else:
        aliases = {len(operands): 0}
        operands += [buffer]
        in_specs += [pl.BlockSpec(memory_space=pl.ANY)]
        if flagged:
            out_shape += [row]
            out_specs += [in_vmem]
    return pl.pallas_call(
        functools.partial(settle_kernel, plan, fields, marked, flagged),
        grid=(fields,),
        in_specs=in_specs,
        out_specs=out_specs,
        out_shape=out_shape,
        scratch_shapes=scratch,
        input_output_aliases=aliases,
        compiler_params=PARAMS,
    )(*operands)


def add_late_kernel(plan, *refs):
    parts, (marks_ref, states_ref, out, held) = refs[: len(plan.spill)], refs[len(plan.spill) :]
    held[...] = jnp.zeros(held.shape, F32)
    for m, part in zip(plan.spill, parts):
        held[m * plan.full + plan.kept[m] : (m + 1) * plan.full, :] = part[...]
    placed = pick(element_chooser(plan, marks_ref[...]), held[...])
    out[...] = states_ref[...] + placed.reshape(out.shape)


def add_late(plan, group, parts, marks, buffer):
    first, fields = group
    block, states = states_block(plan, first)
    return pl.pallas_call(
        functools.partial(add_late_kernel, plan),
        grid=(fields,),
        in_specs=[pl.BlockSpec((plan.full - plan.kept[m], plan.points), lambda f: (f, 0)) for m in plan.spill]
        + [pl.BlockSpec(memory_space=pltpu.VMEM), block],
        out_specs=block,
        out_shape=states,
        scratch_shapes=[pltpu.VMEM((plan.rows, plan.points), F32)],
        input_output_aliases={len(parts) + 1: 0},
        compiler_params=PARAMS,
    )(*parts, marks, buffer)


def cells_kernel(plan, states_ref, order_ref, out):
    held = states_ref[...]
    pressure = 3.0 * held[:, 0] - 3.0 * held[:, 1] + held[:, 2]
    out[...] = pick(order_ref[...], pressure.reshape(plan.per_dev, plan.points), ((1,), (1,)))


def cells_of(plan, buffer, order):
    return pl.pallas_call(
        functools.partial(cells_kernel, plan),
        grid=(1,),
        in_specs=[
            pl.BlockSpec((BX * BS, 3, plan.layers, plan.points), lambda f: (0, 0, 0, 0)),
            whole(order.shape),
        ],
        out_specs=whole((order.shape[0], plan.per_dev)),
        out_shape=jax.ShapeDtypeStruct((order.shape[0], plan.per_dev), F32),
        compiler_params=PARAMS,
    )(buffer, order)


def lane_steps(plan):
    lane = iota((FACE, plan.per_dev), 1)
    layer = rest(lane, plan.layers)
    row_s = rest(halves(lane, plan.layers), BS)
    row_x = halves(lane, plan.layers * BS)
    return layer, row_s, row_x


def roll(value, steps):
    return pltpu.roll(value, steps % value.shape[1], 1)


def solve_kernel(plan, cells, from_xlow, from_xup, from_slow, from_sup, *refs):
    tables, refs = refs[:10], refs[10:]
    total, out_xlow, out_xup, out_slow, out_sup, box, section, modal, weights, values_w, sums = refs
    vectors_x, vectors_s, vectors_w, own_x, own_s, own_w, pick_x, pick_s, spread_x, spread_s = tables
    side, extent = plan.side, plan.extent
    layer, row_s, row_x = lane_steps(plan)
    points = side * side
    stride = points + 2 * FACE
    width = plan.layers
    wide = width * BS
    box_rows = points + 4 * FACE

    def cell(k, start):
        return cells[k * stride + start : k * stride + start + FACE, :]

    def piece(ref, k):
        return ref[k * FACE : (k + 1) * FACE, :]

    for k in range(side):
        w = k + 1
        for i in range(side):
            box[w * box_rows + i * FACE : w * box_rows + (i + 1) * FACE, :] = cell(k, i * FACE)
        at = w * box_rows + points
        low = jnp.where(row_x == 0, roll(piece(from_xlow, k), wide), roll(cell(k, points - FACE), wide))
        up = jnp.where(row_x == BX - 1, roll(piece(from_xup, k), -wide), roll(cell(k, 0), -wide))
        box[at : at + FACE, :] = low
        box[at + FACE : at + 2 * FACE, :] = up
        top, bottom = cell(k, points), cell(k, points + FACE)
        back = (BS - 1) * width
        low = jnp.where(row_s == 0, roll(piece(from_slow, k), -back), roll(top, width))
        up = jnp.where(row_s == BS - 1, roll(piece(from_sup, k), back), roll(bottom, -width))
        box[at + 2 * FACE : at + 3 * FACE, :] = low
        box[at + 3 * FACE : at + 4 * FACE, :] = up
    last = (extent - 1) * box_rows
    for i in range(side):
        below = jnp.where(layer == 0, 0.0, roll(cell(side - 1, i * FACE), 1))
        above = jnp.where(layer == width - 1, 0.0, roll(cell(0, i * FACE), -1))
        box[i * FACE : (i + 1) * FACE, :] = below
        box[last + i * FACE : last + (i + 1) * FACE, :] = above

    def exact(left, right, contract=((1,), (0,))):
        dims = (contract, ((), ()))
        return lax.dot_general(left, right, dims, precision=HIGHEST, preferred_element_type=F32)

    mix_t = exact(exact(pick_x[...], vectors_x[...]), spread_x[...], ((1,), (1,)))
    mix_t = mix_t * exact(exact(pick_s[...], vectors_s[...]), spread_s[...], ((1,), (1,)))
    modal_rows = spread_x.shape[0]
    lanes = plan.per_dev
    held_by = (iota((width, lanes), 0) == rest(iota((width, lanes), 1), width)).astype(F32)
    for w in range(extent):
        weights[w] = exact(vectors_w[w], held_by, ((0,), (0,)))
    values_w[...] = exact(own_w[...], held_by, ((0,), (0,)))
    sum_xs = jnp.sum(spread_x[...] * own_x[...] + spread_s[...] * own_s[...], axis=1, keepdims=True)
    sum_xs = jnp.where(iota(sum_xs.shape, 0) < extent * extent, sum_xs, 1.0)
    for w in range(extent):
        rows = points if w in (0, extent - 1) else box_rows
        section[w] = exact(mix_t[:rows], box[w * box_rows : w * box_rows + rows, :], ((0,), (0,)))
    sums[...] = jnp.broadcast_to(sum_xs, sums.shape)

    @pl.loop(0, modal_rows // FACE)
    def _(block):
        part = pl.ds(pl.multiple_of(block * FACE, FACE), FACE)
        held = [section[w, part, :] for w in range(extent)]
        out = [None] * extent
        base = sums[part, :]
        for k in range(extent):
            value = None
            for w in range(extent):
                term = weights[w, k : k + 1, :] * held[w]
                value = term if value is None else value + term
            value = value / (base + values_w[k : k + 1, :])
            for w in range(extent):
                term = weights[w, k : k + 1, :] * value
                out[w] = term if out[w] is None else out[w] + term
        for w in range(extent):
            modal[w, part, :] = out[w]

    for w in range(extent):
        rows = points if w in (0, extent - 1) else box_rows
        box[w * box_rows : w * box_rows + rows, :] = exact(mix_t[:rows], modal[w])

    for k in range(side):
        at = (k + 1) * box_rows
        total[k * points : (k + 1) * points, :] = box[at : at + points, :]
        for out, shift in ((out_xlow, 0), (out_xup, 1), (out_slow, 2), (out_sup, 3)):
            start = at + points + shift * FACE
            out[k * FACE : (k + 1) * FACE, :] = box[start : start + FACE, :]
    for i in range(side):
        below = jnp.where(layer == width - 1, 0.0, roll(box[i * FACE : (i + 1) * FACE, :], -1))
        above = jnp.where(layer == 0, 0.0, roll(box[last + i * FACE : last + (i + 1) * FACE, :], 1))
        top = (side - 1) * points + i * FACE
        total[top : top + FACE, :] += below
        total[i * FACE : (i + 1) * FACE, :] += above


def finish_kernel(plan, total, xlow, xup, slow, sup, from_x_up, from_x_low, from_s_up, from_s_low, out, held):
    side = plan.side
    points = side * side
    layer, row_s, row_x = lane_steps(plan)
    width = plan.layers
    wide = width * BS
    back = (BS - 1) * width
    sub = iota((FACE, plan.per_dev), 0)
    for k in range(side):
        part = slice(k * FACE, (k + 1) * FACE)
        rows = [total[k * points + i * FACE : k * points + (i + 1) * FACE, :] for i in range(side)]
        rows[side - 1] = rows[side - 1] + jnp.where(
            row_x == BX - 1, roll(from_x_up[part, :], -wide), roll(xlow[part, :], -wide)
        )
        rows[0] = rows[0] + jnp.where(row_x == 0, roll(from_x_low[part, :], wide), roll(xup[part, :], wide))
        to_last = jnp.where(row_s == BS - 1, roll(from_s_up[part, :], back), roll(slow[part, :], -width))
        to_first = jnp.where(row_s == 0, roll(from_s_low[part, :], -back), roll(sup[part, :], width))
        for i in range(side):
            last = jnp.broadcast_to(to_last[i : i + 1, :], sub.shape)
            first = jnp.broadcast_to(to_first[i : i + 1, :], sub.shape)
            value = rows[i] + jnp.where(sub == side - 1, last, 0.0) + jnp.where(sub == 0, first, 0.0)
            held[k * points + i * FACE : k * points + (i + 1) * FACE, :] = value
    lanes = plan.layers * side
    source = iota((plan.per_dev, lanes), 0)
    lane = iota((plan.per_dev, lanes), 1)
    terms = three_terms(held[...])
    kept = rest(iota((points, lanes), 1), side)
    for column in range(BX * BS):
        chooser = (source == halves(lane, side) + column * plan.layers).astype(F32).astype(BF16)
        high, middle, low = [jnp.dot(t, chooser, preferred_element_type=F32) for t in terms]
        spread = (high + middle) + low
        value = jnp.zeros((points, lanes), F32)
        for k in range(side):
            value = jnp.where(kept == k, spread[k * points : (k + 1) * points], value)
        b, s = column // BS, column % BS
        for i in range(side):
            out[b * side + i, s * side : (s + 1) * side, :] = value[i * side : (i + 1) * side]


def simple_call(kernel, operands, out_shape, scratch, cost=None):
    return pl.pallas_call(
        kernel,
        in_specs=[pl.BlockSpec(memory_space=pltpu.VMEM)] * len(operands),
        out_specs=[pl.BlockSpec(memory_space=pltpu.VMEM)] * len(out_shape),
        out_shape=out_shape,
        scratch_shapes=scratch,
        compiler_params=PARAMS,
        cost_estimate=cost,
    )(*operands)


def box_rows_of(extent):
    inside = range(1, extent - 1)
    points = [(u, v) for u in inside for v in inside]
    points += [(u, v) for u in (0, extent - 1) for v in inside]
    points += [(u, v) for v in (0, extent - 1) for u in inside]
    modes = [(i, j) for i in range(extent) for j in range(extent)]
    modal_rows = -(-len(modes) // FACE) * FACE

    def hot(rows, values):
        table = np.zeros((rows, extent), np.float32)
        table[np.arange(len(values)), values] = 1.0
        return jnp.asarray(table)

    us, vs = zip(*points)
    i_s, j_s = zip(*modes)
    return hot(len(us), us), hot(len(vs), vs), hot(modal_rows, i_s), hot(modal_rows, j_s)


def after(value, earlier):
    return lax.optimization_barrier((value, earlier))[0]


def shards(old_states, new_place, vectors_x, vectors_s, vectors_w, values_x, values_s, values_w):
    n_x, n_y = lax.axis_size("gx"), lax.axis_size("gy")
    slots, fields, points = old_states.shape
    plan = Plan(n_x, n_y, slots, fields, points, vectors_w.shape[0], vectors_x.shape[0])
    place = lax.axis_index("gx") * n_y + lax.axis_index("gy")
    me = place.astype(jnp.int32).reshape(1)
    states = jnp.transpose(old_states, (1, 0, 2))
    place_row = new_place.reshape(1, slots)
    both = ("gx", "gy")

    def across(value, flip):
        return lax.ppermute(value, both, [(d, d ^ flip) for d in range(plan.devices)])

    def shifted(value, axis, steps):
        count = lax.axis_size(axis)
        return lax.ppermute(value, axis, [(s, (s + steps) % count) for s in range(count)])

    order = jnp.asarray(cell_order(plan.side), BF16)
    tables = [vectors_x, vectors_s, jnp.transpose(vectors_w, (1, 0, 2))]
    tables += [values_x.reshape(1, -1), values_s.reshape(1, -1), values_w, *box_rows_of(plan.extent)]

    side = plan.side
    inner = side * side

    def faces(cells):
        layered = cells.reshape(side, inner + 2 * FACE, plan.per_dev)

        def rows(start):
            return layered[:, start : start + FACE].reshape(side * FACE, plan.per_dev)

        ends = [rows(inner - FACE), rows(0)]
        side_faces = [shifted(rows(inner), "gy", 1), shifted(rows(inner + FACE), "gy", -1)]
        return [shifted(ends[0], "gx", 1), shifted(ends[1], "gx", -1)] + side_faces

    def solve(cells, halo):
        face = jax.ShapeDtypeStruct((side * FACE, plan.per_dev), F32)
        sections = (plan.extent, tables[-1].shape[0], plan.per_dev)
        total, xlow, xup, slow, sup = simple_call(
            functools.partial(solve_kernel, plan),
            [cells, *halo, *tables],
            [jax.ShapeDtypeStruct((side * inner, plan.per_dev), F32)] + [face] * 4,
            [pltpu.VMEM((plan.extent * (inner + 4 * FACE), plan.per_dev), F32)]
            + [pltpu.VMEM(sections, F32)] * 2
            + [pltpu.VMEM((plan.extent, plan.extent, plan.per_dev), F32)]
            + [pltpu.VMEM((plan.extent, plan.per_dev), F32), pltpu.VMEM(sections[1:], F32)],
        )
        returned = [shifted(xlow, "gx", -1), shifted(xup, "gx", 1), shifted(slow, "gy", -1), shifted(sup, "gy", 1)]
        (correction,) = simple_call(
            functools.partial(finish_kernel, plan),
            [total, xlow, xup, slow, sup, *returned],
            [jax.ShapeDtypeStruct((BX * side, BS * side, plan.layers * side), F32)],
            [pltpu.VMEM((side * inner, plan.per_dev), F32)],
        )
        return correction

    packed = []
    for g, group in enumerate(plan.groups):
        *near, aside = pack(plan, group, me, place_row, states, g == 0)
        packed.append((near, across(aside, 1)))

    marks = gate = waiting = None
    flags, held, late = [], [], []
    last = len(plan.groups) - 1
    for g, (group, (near, aside)) in enumerate(zip(plan.groups, packed)):
        first, flagged = g == 0, g == 1
        if not first:
            near[0] = after(near[0], gate)
        cost = pl.CostEstimate(flops=0 if first else MERGE_FLOPS, bytes_accessed=0, transcendentals=0)
        sent = merge(plan, group, near, aside, first, flags if flagged else [], cost)
        messages = [sent[0]] + [across(sent[b], 2 * b) for b in range(1, plan.pairs)]
        if not first:
            before_it = held[-1][1]
            messages[0] = after(messages[0], before_it[1:])
            if flagged:
                before_it[0] = across(after(waiting, messages[1]), plan.plane)
        if g == last:
            buffer, row_marks, cells = settle(plan, plan.groups[0], *held[0], None, None, own, order, None)
            messages[0] = after(messages[0], cells)
            halo = faces(cells)
        relays, rows_left, more = relay(plan, group, messages, marks, flagged)
        late.append(rows_left)
        if first:
            marks, own, over = more
            flags = [over]
        if flagged:
            (flag,) = more
        gate = waiting = relays[0]
        ready = list(relays)
        if g == last:
            ready[1:] = [after(r, halo[:2]) for r in ready[1:]]
            waiting = after(waiting, halo[:2])
        if not first:
            ready[1:] = [after(r, held[-1][1][1:]) for r in ready[1:]]
        arrived = [None]
        for m in range(2, plan.lines):
            value = ready[m - 1]
            if m > 2 and g != last:
                value = after(value, arrived[-1])
            if m > 2 and first:
                value = after(value, packed[-1][1])
            arrived.append(across(value, m * plan.plane))
        if not first:
            arrived[0] = across(after(waiting, [messages[1], held[-1][1][0]]), plan.plane)
        held.append((messages, arrived))

    buffer, flag = settle(plan, plan.groups[1], *held[1], row_marks, buffer, None, None, flag)
    flag = jnp.maximum(flag[:1, :1], across(flag, 1)[:1, :1])
    correction = solve(after(cells, [buffer, flag]), halo)
    (buffer,) = settle(plan, plan.groups[last], *held[last], row_marks, buffer, None, None, None)

    def send_rest(buffer, correction, late):
        for group, parts in zip(plan.groups, late):
            parts = [across(part, m * plan.plane) for m, part in zip(plan.spill, parts)]
            buffer = add_late(plan, group, parts, row_marks, buffer)
        cells = cells_of(plan, buffer, order)
        return buffer, solve(cells, faces(cells))

    def keep(buffer, correction, late):
        return buffer, correction

    if plan.spill:
        buffer, correction = lax.cond(flag[0, 0] > 0.0, send_rest, keep, buffer, correction, late)
    new_states = buffer.reshape(BX, BS, fields, plan.layers, points).transpose(0, 1, 3, 2, 4)
    return new_states, correction


def solution(mesh):
    placed = (P(("gx", "gy"), None, None), P(("gx", "gy")), P(), P(), P(), P(), P(), P())
    return jax.shard_map(
        shards,
        mesh=mesh,
        in_specs=placed,
        out_specs=(P("gx", "gy", None, None, None), P("gx", "gy", None)),
        check_vma=False,
    )
```

```python
import functools

import jax
import jax.numpy as jnp
import numpy as np
from jax import lax
from jax.experimental import pallas as pl
from jax.experimental.pallas import tpu as pltpu
from jax.sharding import PartitionSpec as P

BX = 4
BS = 2
FACE = 8
MERGE_FLOPS = 40_000_000_000
VMEM_LIMIT = 12 * 1024 * 1024
PARAMS = pltpu.CompilerParams(vmem_limit_bytes=VMEM_LIMIT)
HIGHEST = lax.Precision.HIGHEST
F32 = jnp.float32
BF16 = jnp.bfloat16


class Plan:
    def __init__(self, n_x, n_y, slots, fields, points, layers, extent):
        self.n_x, self.n_y = n_x, n_y
        self.devices = n_x * n_y
        self.lines = n_x // 2
        self.plane = self.devices // self.lines
        self.slots, self.fields, self.points = slots, fields, points
        self.layers, self.extent, self.side = layers, extent, extent - 2
        self.per_dev = BX * BS * layers
        self.cap = 2 * self.per_dev // self.devices
        self.msg_rows = self.lines * self.cap
        self.pairs = self.plane // 2
        self.pair_rows = 2 * self.msg_rows
        self.rows = self.plane * self.msg_rows
        self.full = self.plane * self.cap
        self.kept = [self.full] * 2 + [self.full * 3 // 4] * (self.lines - 2)
        self.spill = [m for m in range(self.lines) if self.kept[m] < self.full]
        second = (fields - 3) * 4 // 9
        self.groups = [(0, 3), (3, second), (3 + second, fields - 3 - second)]


def halves(value, count):
    if count & (count - 1) == 0:
        return lax.shift_right_logical(value, int(count).bit_length() - 1)
    return value // count


def rest(value, count):
    if count & (count - 1) == 0:
        return value & (count - 1)
    return value % count


def three_terms(value):
    high = value.astype(BF16)
    left = value - high.astype(F32)
    middle = left.astype(BF16)
    low = (left - middle.astype(F32)).astype(BF16)
    return high, middle, low


def pick(chooser, value, contract=((1,), (0,))):
    high, middle, low = three_terms(value)
    dims = (contract, ((), ()))
    product = functools.partial(lax.dot_general, dimension_numbers=dims, preferred_element_type=F32)
    return (product(chooser, high) + product(chooser, middle)) + product(chooser, low)


def iota(shape, dim):
    return lax.broadcasted_iota(jnp.int32, shape, dim)


def before(count):
    return (iota((count, count), 0) < iota((count, count), 1)).astype(BF16)


def pack_kernel(plan, fields, marked, me_ref, place_ref, states_ref, *refs):
    outs, chooser_ref = refs[:-1], refs[-1]
    field = pl.program_id(0)
    rows = plan.msg_rows

    @pl.when(field == 0)
    def _():
        me = me_ref[0]
        new_place = place_ref[...]
        live = new_place >= 0
        placed = jnp.maximum(new_place, 0)
        column = halves(placed, plan.layers)
        layer_pos = rest(placed, plan.layers)
        span = BS * plan.n_y
        elem_x = halves(column, span)
        elem_s = rest(column, span)
        target = halves(elem_x, BX) * plan.n_y + halves(elem_s, BS)
        local_row = (rest(elem_x, BX) * BS + rest(elem_s, BS)) * plan.layers + layer_pos
        target = jnp.where(live, target, -1)
        hot = iota((plan.devices, plan.slots), 0) == target
        earlier = jnp.dot(hot.astype(BF16), before(plan.slots), preferred_element_type=F32)
        rank = jnp.sum(jnp.where(hot, earlier, 0.0), axis=0, keepdims=True).astype(jnp.int32)
        across = target ^ me
        row = rest(across, plan.plane) * rows + halves(across, plan.plane) * plan.cap + rank
        row = jnp.where(live, row, -1)
        chooser = (iota((plan.rows, plan.slots), 0) == row).astype(F32)
        chooser_ref[...] = chooser.astype(BF16)
        if marked:
            marks = lax.dot_general(
                jnp.broadcast_to((local_row + 1).astype(F32), (8, plan.slots)),
                chooser,
                (((1,), (1,)), ((), ())),
                precision=HIGHEST,
                preferred_element_type=F32,
            )
            for out, held in zip(outs, [rows] * (len(outs) - 1) + [rows * plan.pairs]):
                out[fields * held : fields * held + 8, :] = jnp.zeros((8, plan.points), F32)
                out[fields * held : fields * held + 8, : plan.rows] = marks

    moved = pick(chooser_ref[...], states_ref[0])
    start = pl.multiple_of(field * rows, rows)
    aside = pl.multiple_of(field * rows * plan.pairs, rows)
    for b in range(plan.pairs):
        outs[b][pl.ds(start, rows), :] = moved[2 * b * rows : (2 * b + 1) * rows]
        outs[-1][pl.ds(aside + b * rows, rows), :] = moved[(2 * b + 1) * rows : (2 * b + 2) * rows]


def whole(shape):
    return pl.BlockSpec(shape, lambda *_: (0,) * len(shape))


def pack(plan, group, me, place_row, states, marked):
    first, fields = group
    extra = 8 if marked else 0
    shapes = [(fields * plan.msg_rows + extra, plan.points)] * plan.pairs
    shapes.append((fields * plan.msg_rows * plan.pairs + extra, plan.points))
    return pl.pallas_call(
        functools.partial(pack_kernel, plan, fields, marked),
        grid=(fields,),
        in_specs=[
            pl.BlockSpec(memory_space=pltpu.SMEM),
            whole((1, plan.slots)),
            pl.BlockSpec((1, plan.slots, plan.points), lambda f: (first + f, 0, 0)),
        ],
        out_specs=[pl.BlockSpec(memory_space=pltpu.VMEM)] * len(shapes),
        out_shape=[jax.ShapeDtypeStruct(shape, F32) for shape in shapes],
        scratch_shapes=[pltpu.VMEM((plan.rows, plan.slots), BF16)],
        compiler_params=PARAMS,
    )(me, place_row, states)


def merge_kernel(plan, fields, marked, flagged, *refs):
    near, refs = refs[: plan.pairs], refs[plan.pairs :]
    aside, outs = refs[0], refs[-plan.pairs :]
    rows = plan.msg_rows
    for b, out in enumerate(outs):
        for field in range(fields):
            start = field * plan.pair_rows
            other = (field * plan.pairs + b) * rows
            out[start : start + rows, :] = near[b][field * rows : (field + 1) * rows, :]
            out[start + rows : start + 2 * rows, :] = aside[other : other + rows, :]
        if marked:
            lane = iota((8, plan.rows), 1)
            mine = near[0][fields * rows : fields * rows + 8, : plan.rows]
            base = fields * rows * plan.pairs
            other = aside[base : base + 8, : plan.rows]
            marks = jnp.where(rest(halves(lane, rows), 2) == 0, mine, other)
            base = fields * plan.pair_rows
            out[base : base + 8, :] = jnp.zeros((8, plan.points), F32)
            out[base : base + 8, : plan.rows] = marks
        if flagged:
            base = fields * plan.pair_rows
            out[base : base + 8, :] = jnp.zeros((8, plan.points), F32)
            out[base : base + 8, : plan.rows] = refs[1][...]


def merge(plan, group, near, aside, marked, flags, cost):
    _, fields = group
    shape = (fields * plan.pair_rows + (8 if marked or flags else 0), plan.points)
    return simple_call(
        functools.partial(merge_kernel, plan, fields, marked, bool(flags)),
        [*near, aside, *flags],
        [jax.ShapeDtypeStruct(shape, F32)] * plan.pairs,
        [],
        cost,
    )


def route_rows(plan, marks):
    lane = iota((1, plan.rows), 1)
    step = rest(halves(lane, plan.cap), plan.lines)
    filled = marks[:1] > 0.0
    valid = (iota((plan.lines, plan.rows), 0) == step) & filled
    earlier = jnp.dot(valid.astype(BF16), before(plan.rows), preferred_element_type=F32)
    earlier = earlier.astype(jnp.int32)
    row = halves(lane, plan.msg_rows) * plan.cap + rest(lane, plan.cap)
    over = jnp.zeros((1, plan.rows), F32)
    for m in range(1, plan.lines):
        number = earlier[m : m + 1]
        row = jnp.where(step == m, number + m * plan.full, row)
        over = jnp.maximum(over, jnp.where((step == m) & filled & (number >= plan.kept[m]), 1.0, 0.0))
    return jnp.where(filled, row, -1), jnp.max(over, axis=1, keepdims=True)


def gather_marks(plan, fields, messages):
    lane = iota((8, plan.rows), 1)
    marks = jnp.zeros((8, plan.rows), F32)
    base = fields * plan.pair_rows
    for b, message in enumerate(messages):
        part = message[base : base + 8, : plan.rows]
        marks = jnp.where(halves(lane, plan.pair_rows) == b, part, marks)
    return marks


def put_tail(plan, out, value):
    base = out.shape[0] - 8
    out[base:, :] = jnp.zeros((8, plan.points), F32)
    out[base:, : plan.rows] = value


def relay_kernel(plan, fields, marked, flagged, *refs):
    messages, refs = refs[: plan.pairs], refs[plan.pairs :]
    if not marked:
        marks_ref, refs = refs[0], refs[1:]
    outs, refs = refs[: plan.lines - 1], refs[plan.lines - 1 :]
    late, refs = refs[: len(plan.spill)], refs[len(plan.spill) :]
    held = refs[-1]
    marks = gather_marks(plan, fields, messages) if marked else marks_ref[...]
    row, over = route_rows(plan, marks)
    spread = (iota((plan.rows, plan.rows), 0) == row).astype(F32)
    if marked:
        marks_out, own_out, flag_out = refs[:3]
        landed = lax.dot_general(
            marks, spread, (((1,), (1,)), ((), ())), precision=HIGHEST, preferred_element_type=F32
        )
        marks_out[...] = marks
        own_out[...] = landed
        flag_out[...] = jnp.broadcast_to(over, (8, plan.rows))
        for out in outs:
            put_tail(plan, out, landed)
    if flagged:
        flag = messages[0][fields * plan.pair_rows :, : plan.rows]
        for message in messages[1:]:
            flag = jnp.maximum(flag, message[fields * plan.pair_rows :, : plan.rows])
        refs[0][...] = flag
        for out in outs:
            put_tail(plan, out, flag)
    chooser = spread[plan.full :].astype(BF16)
    for field in range(fields):
        for b, message in enumerate(messages):
            held[b * plan.pair_rows : (b + 1) * plan.pair_rows, :] = message[
                field * plan.pair_rows : (field + 1) * plan.pair_rows, :
            ]
        moved = pick(chooser, held[...])
        for m, out in enumerate(outs, 1):
            at, kept = (m - 1) * plan.full, plan.kept[m]
            out[field * kept : (field + 1) * kept, :] = moved[at : at + kept]
        for m, out in zip(plan.spill, late):
            at, kept = (m - 1) * plan.full, plan.kept[m]
            left = plan.full - kept
            out[field * left : (field + 1) * left, :] = moved[at + kept : at + plan.full]


def relay(plan, group, messages, marks, flagged):
    _, fields = group
    marked = marks is None
    extra = 8 if marked or flagged else 0
    shapes = [(fields * kept + extra, plan.points) for kept in plan.kept[1:]]
    shapes += [(fields * (plan.full - plan.kept[m]), plan.points) for m in plan.spill]
    shapes += [(8, plan.rows)] * (3 if marked else 1 if flagged else 0)
    result = simple_call(
        functools.partial(relay_kernel, plan, fields, marked, flagged),
        list(messages) + ([] if marked else [marks]),
        [jax.ShapeDtypeStruct(shape, F32) for shape in shapes],
        [pltpu.VMEM((plan.rows, plan.points), F32)],
    )
    split = plan.lines - 1
    return result[:split], result[split : split + len(plan.spill)], result[split + len(plan.spill) :]


def element_chooser(plan, marks):
    element = iota((plan.per_dev, plan.rows), 0).astype(F32) + 1.0
    return (element == marks[:1]).astype(F32).astype(BF16)


def settle_kernel(plan, fields, marked, flagged, *refs):
    messages, refs = refs[: plan.pairs], refs[plan.pairs :]
    relays, refs = refs[: plan.lines - 1], refs[plan.lines - 1 :]
    if marked or flagged:
        tails, refs = refs[: plan.lines - 1], refs[plan.lines - 1 :]
    if marked:
        own_ref, order_ref, out, marks_out, cells_out, chooser_ref, held, pressure_ref = refs
    elif flagged:
        marks_ref, flag_ref, _, out, flag_out, chooser_ref, held = refs
    else:
        marks_ref, _, out, chooser_ref, held = refs
    field = pl.program_id(0)

    @pl.when(field == 0)
    def _():
        if marked:
            lane = iota((8, plan.rows), 1)
            marks = own_ref[...]
            for m in range(1, plan.lines):
                marks = jnp.where(halves(lane, plan.full) == m, tails[m - 1][:, : plan.rows], marks)
            marks_out[...] = marks
        else:
            marks = marks_ref[...]
        if flagged:
            flag = flag_ref[...]
            for tail in tails:
                flag = jnp.maximum(flag, tail[:, : plan.rows])
            flag_out[...] = flag
        chooser_ref[...] = element_chooser(plan, marks)
        for m in plan.spill:
            start = m * plan.full + plan.kept[m]
            held[start : (m + 1) * plan.full, :] = jnp.zeros((plan.full - plan.kept[m], plan.points), F32)

    for j in range(plan.plane):
        start = j % 2 * plan.msg_rows
        held[j * plan.cap : (j + 1) * plan.cap, :] = messages[j // 2][start : start + plan.cap, :]
    for m, part in enumerate(relays, 1):
        held[m * plan.full : m * plan.full + plan.kept[m], :] = part[...]
    placed = pick(chooser_ref[...], held[...])
    out[...] = placed.reshape(out.shape)

    if marked:

        @pl.when(field == 0)
        def _():
            pressure_ref[...] = 3.0 * placed

        @pl.when(field == 1)
        def _():
            pressure_ref[...] = pressure_ref[...] - 3.0 * placed

        @pl.when(field == 2)
        def _():
            cells_out[...] = pick(order_ref[...], pressure_ref[...] + placed, ((1,), (1,)))


def cell_order(side):
    rows = []
    for k in range(side):
        rows += [(i * side + j) * side + k for i in range(side) for j in range(side)]
        rows += [(i * side + side - 1) * side + k for i in range(side)]
        rows += [(i * side) * side + k for i in range(side)]
    order = np.zeros((len(rows), side**3), np.float32)
    order[np.arange(len(rows)), rows] = 1.0
    return order


def states_block(plan, first):
    columns = BX * BS
    block = pl.BlockSpec((columns, 1, plan.layers, plan.points), lambda f: (0, first + f, 0, 0))
    return block, jax.ShapeDtypeStruct((columns, plan.fields, plan.layers, plan.points), F32)


def settle(plan, group, messages, relays, marks, buffer, own, order, flag):
    first, fields = group
    marked, flagged = marks is None, flag is not None
    in_vmem = pl.BlockSpec(memory_space=pltpu.VMEM)
    block, states = states_block(plan, first)
    out_specs, out_shape = [block], [states]
    scratch = [pltpu.VMEM((plan.per_dev, plan.rows), BF16), pltpu.VMEM((plan.rows, plan.points), F32)]
    operands = list(messages) + list(relays)
    in_specs = [pl.BlockSpec((plan.pair_rows, plan.points), lambda f: (f, 0))] * plan.pairs
    in_specs += [pl.BlockSpec((kept, plan.points), lambda f: (f, 0)) for kept in plan.kept[1:]]
    if marked or flagged:
        operands += list(relays)
        in_specs += [
            pl.BlockSpec((8, plan.points), lambda f, at=fields * kept // 8: (at, 0)) for kept in plan.kept[1:]
        ]
    known = [own, order] if marked else [marks, flag] if flagged else [marks]
    operands += known
    in_specs += [in_vmem] * len(known)
    aliases = {}
    row = jax.ShapeDtypeStruct((8, plan.rows), F32)
    if marked:
        out_shape += [row, jax.ShapeDtypeStruct((order.shape[0], plan.per_dev), F32)]
        out_specs += [in_vmem] * 2
        scratch += [pltpu.VMEM((plan.per_dev, plan.points), F32)]
    else:
        aliases = {len(operands): 0}
        operands += [buffer]
        in_specs += [pl.BlockSpec(memory_space=pl.ANY)]
        if flagged:
            out_shape += [row]
            out_specs += [in_vmem]
    return pl.pallas_call(
        functools.partial(settle_kernel, plan, fields, marked, flagged),
        grid=(fields,),
        in_specs=in_specs,
        out_specs=out_specs,
        out_shape=out_shape,
        scratch_shapes=scratch,
        input_output_aliases=aliases,
        compiler_params=PARAMS,
    )(*operands)


def add_late_kernel(plan, *refs):
    parts, (marks_ref, states_ref, out, held) = refs[: len(plan.spill)], refs[len(plan.spill) :]
    held[...] = jnp.zeros(held.shape, F32)
    for m, part in zip(plan.spill, parts):
        held[m * plan.full + plan.kept[m] : (m + 1) * plan.full, :] = part[...]
    placed = pick(element_chooser(plan, marks_ref[...]), held[...])
    out[...] = states_ref[...] + placed.reshape(out.shape)


def add_late(plan, group, parts, marks, buffer):
    first, fields = group
    block, states = states_block(plan, first)
    return pl.pallas_call(
        functools.partial(add_late_kernel, plan),
        grid=(fields,),
        in_specs=[pl.BlockSpec((plan.full - plan.kept[m], plan.points), lambda f: (f, 0)) for m in plan.spill]
        + [pl.BlockSpec(memory_space=pltpu.VMEM), block],
        out_specs=block,
        out_shape=states,
        scratch_shapes=[pltpu.VMEM((plan.rows, plan.points), F32)],
        input_output_aliases={len(parts) + 1: 0},
        compiler_params=PARAMS,
    )(*parts, marks, buffer)


def cells_kernel(plan, states_ref, order_ref, out):
    held = states_ref[...]
    pressure = 3.0 * held[:, 0] - 3.0 * held[:, 1] + held[:, 2]
    out[...] = pick(order_ref[...], pressure.reshape(plan.per_dev, plan.points), ((1,), (1,)))


def cells_of(plan, buffer, order):
    return pl.pallas_call(
        functools.partial(cells_kernel, plan),
        grid=(1,),
        in_specs=[
            pl.BlockSpec((BX * BS, 3, plan.layers, plan.points), lambda f: (0, 0, 0, 0)),
            whole(order.shape),
        ],
        out_specs=whole((order.shape[0], plan.per_dev)),
        out_shape=jax.ShapeDtypeStruct((order.shape[0], plan.per_dev), F32),
        compiler_params=PARAMS,
    )(buffer, order)


def lane_steps(plan):
    lane = iota((FACE, plan.per_dev), 1)
    layer = rest(lane, plan.layers)
    row_s = rest(halves(lane, plan.layers), BS)
    row_x = halves(lane, plan.layers * BS)
    return layer, row_s, row_x


def roll(value, steps):
    return pltpu.roll(value, steps % value.shape[1], 1)


def solve_kernel(plan, cells, from_xlow, from_xup, from_slow, from_sup, *refs):
    tables, refs = refs[:10], refs[10:]
    total, out_xlow, out_xup, out_slow, out_sup, box, section, modal, weights, values_w, sums = refs
    vectors_x, vectors_s, vectors_w, own_x, own_s, own_w, pick_x, pick_s, spread_x, spread_s = tables
    side, extent = plan.side, plan.extent
    layer, row_s, row_x = lane_steps(plan)
    points = side * side
    stride = points + 2 * FACE
    width = plan.layers
    wide = width * BS
    box_rows = points + 4 * FACE

    def cell(k, start):
        return cells[k * stride + start : k * stride + start + FACE, :]

    def piece(ref, k):
        return ref[k * FACE : (k + 1) * FACE, :]

    for k in range(side):
        w = k + 1
        for i in range(side):
            box[w * box_rows + i * FACE : w * box_rows + (i + 1) * FACE, :] = cell(k, i * FACE)
        at = w * box_rows + points
        low = jnp.where(row_x == 0, roll(piece(from_xlow, k), wide), roll(cell(k, points - FACE), wide))
        up = jnp.where(row_x == BX - 1, roll(piece(from_xup, k), -wide), roll(cell(k, 0), -wide))
        box[at : at + FACE, :] = low
        box[at + FACE : at + 2 * FACE, :] = up
        top, bottom = cell(k, points), cell(k, points + FACE)
        back = (BS - 1) * width
        low = jnp.where(row_s == 0, roll(piece(from_slow, k), -back), roll(top, width))
        up = jnp.where(row_s == BS - 1, roll(piece(from_sup, k), back), roll(bottom, -width))
        box[at + 2 * FACE : at + 3 * FACE, :] = low
        box[at + 3 * FACE : at + 4 * FACE, :] = up
    last = (extent - 1) * box_rows
    for i in range(side):
        below = jnp.where(layer == 0, 0.0, roll(cell(side - 1, i * FACE), 1))
        above = jnp.where(layer == width - 1, 0.0, roll(cell(0, i * FACE), -1))
        box[i * FACE : (i + 1) * FACE, :] = below
        box[last + i * FACE : last + (i + 1) * FACE, :] = above

    def exact(left, right, contract=((1,), (0,))):
        dims = (contract, ((), ()))
        return lax.dot_general(left, right, dims, precision=HIGHEST, preferred_element_type=F32)

    mix_t = exact(exact(pick_x[...], vectors_x[...]), spread_x[...], ((1,), (1,)))
    mix_t = mix_t * exact(exact(pick_s[...], vectors_s[...]), spread_s[...], ((1,), (1,)))
    modal_rows = spread_x.shape[0]
    lanes = plan.per_dev
    held_by = (iota((width, lanes), 0) == rest(iota((width, lanes), 1), width)).astype(F32)
    for w in range(extent):
        weights[w] = exact(vectors_w[w], held_by, ((0,), (0,)))
    values_w[...] = exact(own_w[...], held_by, ((0,), (0,)))
    sum_xs = jnp.sum(spread_x[...] * own_x[...] + spread_s[...] * own_s[...], axis=1, keepdims=True)
    sum_xs = jnp.where(iota(sum_xs.shape, 0) < extent * extent, sum_xs, 1.0)
    for w in range(extent):
        rows = points if w in (0, extent - 1) else box_rows
        section[w] = exact(mix_t[:rows], box[w * box_rows : w * box_rows + rows, :], ((0,), (0,)))
    sums[...] = jnp.broadcast_to(sum_xs, sums.shape)

    @pl.loop(0, modal_rows // FACE)
    def _(block):
        part = pl.ds(pl.multiple_of(block * FACE, FACE), FACE)
        held = [section[w, part, :] for w in range(extent)]
        out = [None] * extent
        base = sums[part, :]
        for k in range(extent):
            value = None
            for w in range(extent):
                term = weights[w, k : k + 1, :] * held[w]
                value = term if value is None else value + term
            value = value / (base + values_w[k : k + 1, :])
            for w in range(extent):
                term = weights[w, k : k + 1, :] * value
                out[w] = term if out[w] is None else out[w] + term
        for w in range(extent):
            modal[w, part, :] = out[w]

    for w in range(extent):
        rows = points if w in (0, extent - 1) else box_rows
        box[w * box_rows : w * box_rows + rows, :] = exact(mix_t[:rows], modal[w])

    for k in range(side):
        at = (k + 1) * box_rows
        total[k * points : (k + 1) * points, :] = box[at : at + points, :]
        for out, shift in ((out_xlow, 0), (out_xup, 1), (out_slow, 2), (out_sup, 3)):
            start = at + points + shift * FACE
            out[k * FACE : (k + 1) * FACE, :] = box[start : start + FACE, :]
    for i in range(side):
        below = jnp.where(layer == width - 1, 0.0, roll(box[i * FACE : (i + 1) * FACE, :], -1))
        above = jnp.where(layer == 0, 0.0, roll(box[last + i * FACE : last + (i + 1) * FACE, :], 1))
        top = (side - 1) * points + i * FACE
        total[top : top + FACE, :] += below
        total[i * FACE : (i + 1) * FACE, :] += above


def finish_kernel(plan, total, xlow, xup, slow, sup, from_x_up, from_x_low, from_s_up, from_s_low, out, held):
    side = plan.side
    points = side * side
    layer, row_s, row_x = lane_steps(plan)
    width = plan.layers
    wide = width * BS
    back = (BS - 1) * width
    sub = iota((FACE, plan.per_dev), 0)
    for k in range(side):
        part = slice(k * FACE, (k + 1) * FACE)
        rows = [total[k * points + i * FACE : k * points + (i + 1) * FACE, :] for i in range(side)]
        rows[side - 1] = rows[side - 1] + jnp.where(
            row_x == BX - 1, roll(from_x_up[part, :], -wide), roll(xlow[part, :], -wide)
        )
        rows[0] = rows[0] + jnp.where(row_x == 0, roll(from_x_low[part, :], wide), roll(xup[part, :], wide))
        to_last = jnp.where(row_s == BS - 1, roll(from_s_up[part, :], back), roll(slow[part, :], -width))
        to_first = jnp.where(row_s == 0, roll(from_s_low[part, :], -back), roll(sup[part, :], width))
        for i in range(side):
            last = jnp.broadcast_to(to_last[i : i + 1, :], sub.shape)
            first = jnp.broadcast_to(to_first[i : i + 1, :], sub.shape)
            value = rows[i] + jnp.where(sub == side - 1, last, 0.0) + jnp.where(sub == 0, first, 0.0)
            held[k * points + i * FACE : k * points + (i + 1) * FACE, :] = value
    lanes = plan.layers * side
    source = iota((plan.per_dev, lanes), 0)
    lane = iota((plan.per_dev, lanes), 1)
    terms = three_terms(held[...])
    kept = rest(iota((points, lanes), 1), side)
    for column in range(BX * BS):
        chooser = (source == halves(lane, side) + column * plan.layers).astype(F32).astype(BF16)
        high, middle, low = [jnp.dot(t, chooser, preferred_element_type=F32) for t in terms]
        spread = (high + middle) + low
        value = jnp.zeros((points, lanes), F32)
        for k in range(side):
            value = jnp.where(kept == k, spread[k * points : (k + 1) * points], value)
        b, s = column // BS, column % BS
        for i in range(side):
            out[b * side + i, s * side : (s + 1) * side, :] = value[i * side : (i + 1) * side]


def simple_call(kernel, operands, out_shape, scratch, cost=None):
    return pl.pallas_call(
        kernel,
        in_specs=[pl.BlockSpec(memory_space=pltpu.VMEM)] * len(operands),
        out_specs=[pl.BlockSpec(memory_space=pltpu.VMEM)] * len(out_shape),
        out_shape=out_shape,
        scratch_shapes=scratch,
        compiler_params=PARAMS,
        cost_estimate=cost,
    )(*operands)


def box_rows_of(extent):
    inside = range(1, extent - 1)
    points = [(u, v) for u in inside for v in inside]
    points += [(u, v) for u in (0, extent - 1) for v in inside]
    points += [(u, v) for v in (0, extent - 1) for u in inside]
    modes = [(i, j) for i in range(extent) for j in range(extent)]
    modal_rows = -(-len(modes) // FACE) * FACE

    def hot(rows, values):
        table = np.zeros((rows, extent), np.float32)
        table[np.arange(len(values)), values] = 1.0
        return jnp.asarray(table)

    us, vs = zip(*points)
    i_s, j_s = zip(*modes)
    return hot(len(us), us), hot(len(vs), vs), hot(modal_rows, i_s), hot(modal_rows, j_s)


def after(value, earlier):
    return lax.optimization_barrier((value, earlier))[0]


def shards(old_states, new_place, vectors_x, vectors_s, vectors_w, values_x, values_s, values_w):
    n_x, n_y = lax.axis_size("gx"), lax.axis_size("gy")
    slots, fields, points = old_states.shape
    plan = Plan(n_x, n_y, slots, fields, points, vectors_w.shape[0], vectors_x.shape[0])
    place = lax.axis_index("gx") * n_y + lax.axis_index("gy")
    me = place.astype(jnp.int32).reshape(1)
    states = jnp.transpose(old_states, (1, 0, 2))
    place_row = new_place.reshape(1, slots)
    both = ("gx", "gy")

    def across(value, flip):
        return lax.ppermute(value, both, [(d, d ^ flip) for d in range(plan.devices)])

    def shifted(value, axis, steps):
        count = lax.axis_size(axis)
        return lax.ppermute(value, axis, [(s, (s + steps) % count) for s in range(count)])

    order = jnp.asarray(cell_order(plan.side), BF16)
    tables = [vectors_x, vectors_s, jnp.transpose(vectors_w, (1, 0, 2))]
    tables += [values_x.reshape(1, -1), values_s.reshape(1, -1), values_w, *box_rows_of(plan.extent)]

    side = plan.side
    inner = side * side

    def faces(cells):
        layered = cells.reshape(side, inner + 2 * FACE, plan.per_dev)

        def rows(start):
            return layered[:, start : start + FACE].reshape(side * FACE, plan.per_dev)

        ends = [rows(inner - FACE), rows(0)]
        side_faces = [shifted(rows(inner), "gy", 1), shifted(rows(inner + FACE), "gy", -1)]
        return [shifted(ends[0], "gx", 1), shifted(ends[1], "gx", -1)] + side_faces

    def solve(cells, halo):
        face = jax.ShapeDtypeStruct((side * FACE, plan.per_dev), F32)
        sections = (plan.extent, tables[-1].shape[0], plan.per_dev)
        total, xlow, xup, slow, sup = simple_call(
            functools.partial(solve_kernel, plan),
            [cells, *halo, *tables],
            [jax.ShapeDtypeStruct((side * inner, plan.per_dev), F32)] + [face] * 4,
            [pltpu.VMEM((plan.extent * (inner + 4 * FACE), plan.per_dev), F32)]
            + [pltpu.VMEM(sections, F32)] * 2
            + [pltpu.VMEM((plan.extent, plan.extent, plan.per_dev), F32)]
            + [pltpu.VMEM((plan.extent, plan.per_dev), F32), pltpu.VMEM(sections[1:], F32)],
        )
        returned = [shifted(xlow, "gx", -1), shifted(xup, "gx", 1), shifted(slow, "gy", -1), shifted(sup, "gy", 1)]
        (correction,) = simple_call(
            functools.partial(finish_kernel, plan),
            [total, xlow, xup, slow, sup, *returned],
            [jax.ShapeDtypeStruct((BX * side, BS * side, plan.layers * side), F32)],
            [pltpu.VMEM((side * inner, plan.per_dev), F32)],
        )
        return correction

    packed = []
    for g, group in enumerate(plan.groups):
        *near, aside = pack(plan, group, me, place_row, states, g == 0)
        packed.append((near, across(aside, 1)))

    marks = gate = waiting = None
    flags, held, late = [], [], []
    last = len(plan.groups) - 1
    for g, (group, (near, aside)) in enumerate(zip(plan.groups, packed)):
        first, flagged = g == 0, g == 1
        if not first:
            near[0] = after(near[0], gate)
        cost = pl.CostEstimate(flops=0 if first else MERGE_FLOPS, bytes_accessed=0, transcendentals=0)
        sent = merge(plan, group, near, aside, first, flags if flagged else [], cost)
        messages = [sent[0]] + [across(sent[b], 2 * b) for b in range(1, plan.pairs)]
        if not first:
            before_it = held[-1][1]
            messages[0] = after(messages[0], before_it[1:])
            if flagged:
                before_it[0] = across(after(waiting, messages[2]), plan.plane)
        if g == last:
            buffer, row_marks, cells = settle(plan, plan.groups[0], *held[0], None, None, own, order, None)
            messages[0] = after(messages[0], cells)
            halo = faces(cells)
        relays, rows_left, more = relay(plan, group, messages, marks, flagged)
        late.append(rows_left)
        if first:
            marks, own, over = more
            flags = [over]
        if flagged:
            (flag,) = more
        gate = waiting = relays[0]
        ready = list(relays)
        if g == last:
            ready[1:] = [after(r, halo[:2]) for r in ready[1:]]
            waiting = after(waiting, halo[:2])
        if not first:
            ready[1:] = [after(r, held[-1][1][1:]) for r in ready[1:]]
        arrived = [None]
        for m in range(2, plan.lines):
            value = ready[m - 1]
            if m > 2 and g != last:
                value = after(value, arrived[-1])
            if m > 2 and first:
                value = after(value, packed[-1][1])
            arrived.append(across(value, m * plan.plane))
        if not first:
            arrived[0] = across(after(waiting, [messages[2], held[-1][1][0]]), plan.plane)
        held.append((messages, arrived))

    buffer, flag = settle(plan, plan.groups[1], *held[1], row_marks, buffer, None, None, flag)
    flag = jnp.maximum(flag[:1, :1], across(flag, 1)[:1, :1])
    correction = solve(after(cells, [buffer, flag]), halo)
    (buffer,) = settle(plan, plan.groups[last], *held[last], row_marks, buffer, None, None, None)

    def send_rest(buffer, correction, late):
        for group, parts in zip(plan.groups, late):
            parts = [across(part, m * plan.plane) for m, part in zip(plan.spill, parts)]
            buffer = add_late(plan, group, parts, row_marks, buffer)
        cells = cells_of(plan, buffer, order)
        return buffer, solve(cells, faces(cells))

    def keep(buffer, correction, late):
        return buffer, correction

    if plan.spill:
        buffer, correction = lax.cond(flag[0, 0] > 0.0, send_rest, keep, buffer, correction, late)
    new_states = buffer.reshape(BX, BS, fields, plan.layers, points).transpose(0, 1, 3, 2, 4)
    return new_states, correction


def solution(mesh):
    placed = (P(("gx", "gy"), None, None), P(("gx", "gy")), P(), P(), P(), P(), P(), P())
    return jax.shard_map(
        shards,
        mesh=mesh,
        in_specs=placed,
        out_specs=(P("gx", "gy", None, None, None), P("gx", "gy", None)),
        check_vma=False,
    )
```
